32 devices in a mesh: dp: 4 (over y, x), shard: 8 (over z, core).
Axes of the slice: x: 2, y: 2, z: 4, core: 2. Of those that a mesh axis runs over, the one named last changes fastest.
Arguments:
- clip_maps: bfloat16 [128, 32, 2, 1024], P(('dp', 'shard')), may hold values from -6 to 6
- lengths: int32 [128], P(('dp', 'shard')), may hold values from 7 to 31, as said below
- labels: int32 [128, 527], P(('dp', 'shard')), may hold values 0 or 1
- conv1_weight: bfloat16 [9216, 2048], P('shard'), may hold values from -0.0625 to 0.0625
- norm1_gain: float32 [2048], replicated, may hold values from 0.5 to 1.5
- norm1_shift: float32 [2048], replicated, may hold values from -0.5 to 0.5
- conv2_weight: bfloat16 [18432, 2048], P('shard'), may hold values from -0.046875 to 0.046875
- norm2_gain: float32 [2048], replicated, may hold values from 0.5 to 1.5
- norm2_shift: float32 [2048], replicated, may hold values from -0.5 to 0.5
- fc1_weight: bfloat16 [2048, 2048], P('shard'), may hold values from -0.125 to 0.125
- fc1_bias: float32 [2048], replicated, may hold values from -0.5 to 0.5
- fc2_weight: bfloat16 [2048, 527], P('shard'), may hold values from -0.125 to 0.125
- fc2_bias: float32 [527], replicated, may hold values from -1.5 to 0.5
Outputs:
- logits: float32 [128, 527], P(('dp', 'shard'))
- input_grad: float32 [128, 32, 2, 1024], P(('dp', 'shard'))
- conv1_grad: float32 [9216, 2048], P('shard')
- norm1_gain_grad: float32 [2048], replicated
- norm1_shift_grad: float32 [2048], replicated
- conv2_grad: float32 [18432, 2048], P('shard')
- norm2_gain_grad: float32 [2048], replicated
- norm2_shift_grad: float32 [2048], replicated
- fc1_grad: float32 [2048, 2048], P('shard')
- fc1_bias_grad: float32 [2048], replicated
- fc2_grad: float32 [2048, 527], P('shard')
- fc2_bias_grad: float32 [527], replicated
The draws below stay inside these ranges and needn't reach their ends.
Inputs may be any that keep to these rules, and one draw needn't show every extreme that they name: `lengths`: every clip has 7, 15 or 31 valid frames; both 7 and 31 occur in every draw.
All inputs are finite; a program needn't handle non-finite values. No bound on the sum of `labels` on one device may be relied on, other than what follows from the above.
Results may differ from the reference program's by a relative error of at most 0.018.
Values may be sent and summed in bfloat16 or wider, within the bound.
No kernel may reach another device: no remote copies, remote signals or barrier semaphores. Data moves between devices by JAX's collectives and lax.ppermute only.
A program may use at most 576 MiB of HBM per device.

```python
import math
import jax
import jax.numpy as jnp
from jax import lax

C_IN = 1024
C_MID = 2048
FC_WIDTH = 2048
CLASSES = 527
FRAMES = 32
MEL = 2
CLIPS = 128


def draw_lengths(key, part):
    key = jax.random.fold_in(key, 5)
    group_ids = jax.random.randint(key, (CLIPS,), 0, 3)
    group_ids = group_ids.at[0].set(2).at[1].set(0)
    return jnp.where(group_ids == 0, 7, jnp.where(group_ids == 1, 15, 31)).astype(jnp.int32)


def place_ends(drawn, own_key, smallest, high):
    dims = drawn.shape
    spot = [jax.random.randint(jax.random.fold_in(own_key, axis), (), 0, dims[axis]) for axis in range(len(dims))]
    drawn = drawn.at[tuple(spot)].set(smallest)
    longest = dims.index(max(dims))
    spot[longest] = (spot[longest] + 1) % dims[longest]
    return drawn.at[tuple(spot)].set(high)


def levels(stream_key, dims, shards, low, high):
    def one(position, parts):
        steps = jax.random.uniform(jax.random.fold_in(jax.random.fold_in(stream_key, 6), position), (parts,), jnp.float32, low / len(shards), high / len(shards))
        return jnp.repeat(jnp.exp(steps), dims[position] // parts).reshape((-1,) + (1,) * (len(dims) - position - 1))

    factor_of = one(*shards[0])
    for cut in shards[1:]:
        factor_of = factor_of * one(*cut)
    return factor_of


def noise(key, dims, deviation, limit, cuts=(), kind=jnp.bfloat16):
    loudness = levels(key, dims, cuts, -0.22, 0.18) if cuts else 1.0
    drawn = jax.random.normal(key, dims, jnp.float32) * deviation * loudness
    return jnp.minimum(jnp.maximum(drawn, -limit), limit).astype(kind)


def setup_inputs(seed: int = 0) -> dict:
    key_list = jax.random.split(jax.random.key(seed), 14)
    clip_maps = noise(key_list[0], (CLIPS, FRAMES, MEL, C_IN), 1.0, 6.0, ((0, 32),))
    lengths = draw_lengths(jax.random.fold_in(key_list[13], 71), 0)
    labels = place_ends((jax.random.randint(key_list[2], (CLIPS, CLASSES), 0, 20) < 1).astype(jnp.int32), jax.random.fold_in(key_list[2], 1), 0, 1)
    conv1_weight = noise(key_list[3], (9 * C_IN, C_MID), (9 * C_IN) ** -0.5, 0.0625, ((0, 8),))
    norm1_gain = jnp.clip(1.0 + 0.1 * jax.random.normal(key_list[4], (C_MID,), jnp.float32), 0.5, 1.5)
    norm1_shift = jnp.clip(jax.random.uniform(key_list[5], (C_MID,), jnp.float32, -0.5, 0.5), -0.5, 0.5)
    conv2_weight = noise(key_list[6], (9 * C_MID, C_MID), (9 * C_MID) ** -0.5, 0.046875, ((0, 8),))
    norm2_gain = jnp.clip(1.0 + 0.1 * jax.random.normal(key_list[7], (C_MID,), jnp.float32), 0.5, 1.5)
    norm2_shift = jnp.clip(jax.random.uniform(key_list[8], (C_MID,), jnp.float32, -0.5, 0.5), -0.5, 0.5)
    fc1_weight = noise(key_list[9], (C_MID, FC_WIDTH), C_MID ** -0.5, 0.125, ((0, 8),))
    fc1_bias = jnp.clip(jax.random.uniform(key_list[10], (FC_WIDTH,), jnp.float32, -0.5, 0.5), -0.5, 0.5)
    fc2_weight = noise(key_list[11], (FC_WIDTH, CLASSES), FC_WIDTH ** -0.5, 0.125, ((0, 8),))
    fc2_bias = jnp.clip(jax.random.uniform(key_list[12], (CLASSES,), jnp.float32, -1.5, 0.5), -1.5, 0.5)
    return dict(clip_maps=clip_maps, lengths=lengths, labels=labels, conv1_weight=conv1_weight, norm1_gain=norm1_gain, norm1_shift=norm1_shift, conv2_weight=conv2_weight, norm2_gain=norm2_gain, norm2_shift=norm2_shift, fc1_weight=fc1_weight, fc1_bias=fc1_bias, fc2_weight=fc2_weight, fc2_bias=fc2_bias)


@jax.custom_vjp
def low(v):
    return lax.optimization_barrier(v.astype(jnp.bfloat16)).astype(jnp.float32)

@jax.custom_vjp
def low_back(v):
    return v

def low_keep(v):
    return (low(v), None)

def low_pass(kept, grad):
    return (grad,)

def back_keep(v):
    return (v, None)

def back_low(kept, grad):
    return (low(grad),)
low.defvjp(low_keep, low_pass)
low_back.defvjp(back_keep, back_low)
epsilon = 1e-05

def matmul(left, right):
    return jnp.dot(left, right, precision=lax.Precision.HIGHEST, preferred_element_type=jnp.float32)

def patch_rows(grid_in):
    clip_count, frame_count, mel_count, chan_count = grid_in.shape
    padded = jnp.pad(grid_in, ((0, 0), (1, 1), (1, 1), (0, 0)))
    tap_list = [padded[:, shift_t:shift_t + frame_count, shift_m:shift_m + mel_count, :] for shift_t in range(3) for shift_m in range(3)]
    stacked = jnp.stack(tap_list, axis=3)
    return stacked.reshape(clip_count * frame_count * mel_count, 9 * chan_count)

def convolve(grid_in, weight):
    clip_count = grid_in.shape[0]
    block = math.gcd(clip_count, 64)

    def one_block(grid_block):
        result = matmul(patch_rows(grid_block), weight)
        return result.reshape(grid_block.shape[0], grid_block.shape[1], grid_block.shape[2], weight.shape[1])
    blocked = grid_in.reshape((clip_count // block, block) + grid_in.shape[1:])
    result = lax.map(jax.checkpoint(one_block), blocked)
    return result.reshape((clip_count,) + result.shape[2:])

def batch_norm(values_in, valid_four, pixel_count, gain, shift):
    sum_first = lax.optimization_barrier(jnp.sum(values_in * valid_four, axis=(0, 1, 2)))
    sum_square = lax.optimization_barrier(jnp.sum(values_in * values_in * valid_four, axis=(0, 1, 2)))
    mean_value = sum_first / pixel_count
    variance = sum_square / pixel_count - mean_value * mean_value
    normed = (values_in - mean_value) * lax.rsqrt(variance + epsilon)
    return normed * gain + shift

def reference(clip_maps, lengths, labels, conv1_weight, norm1_gain, norm1_shift, conv2_weight, norm2_gain, norm2_shift, fc1_weight, fc1_bias, fc2_weight, fc2_bias):
    clip_count, frame_count, mel_count, chan_in = clip_maps.shape
    frame_ids = lax.broadcasted_iota(jnp.int32, (clip_count, frame_count), 1)
    valid_two = (frame_ids < lengths[:, None]).astype(jnp.float32)
    valid_four = valid_two[:, :, None, None]
    pixel_count = jnp.sum(valid_two) * mel_count
    half_ids = lax.broadcasted_iota(jnp.int32, (clip_count, frame_count // 2), 1)
    half_len = lengths // 2
    pooled_valid = (half_ids < half_len[:, None]).astype(jnp.float32)[:, :, None]
    half_float = half_len.astype(jnp.float32)[:, None]
    targets = labels.astype(jnp.float32)

    def forward(maps_in, weight_one, gain_one, shift_one, weight_two, gain_two, shift_two, weight_fc1, bias_fc1, weight_fc2, bias_fc2):
        masked = maps_in * valid_four
        first_out = low_back(convolve(masked, weight_one))
        act_one = low(jax.nn.silu(batch_norm(first_out, valid_four, pixel_count, gain_one, shift_one)) * valid_four)
        second_out = low_back(convolve(act_one, weight_two))
        act_two = jax.nn.silu(batch_norm(second_out, valid_four, pixel_count, gain_two, shift_two)) * valid_four
        chan_mid = act_two.shape[3]
        pooled = lax.optimization_barrier(jnp.mean(act_two.reshape(clip_count, frame_count // 2, 2, mel_count // 2, 2, chan_mid), axis=(2, 4)))
        pooled = lax.optimization_barrier(jnp.mean(pooled, axis=2))
        largest = lax.optimization_barrier(jnp.max(jnp.where(pooled_valid > 0, pooled, -1e+30), axis=1, keepdims=True))
        exp_sum = lax.optimization_barrier(jnp.sum(jnp.exp(pooled - largest) * pooled_valid, axis=1))
        log_sum = largest[:, 0, :] + jnp.log(exp_sum)
        mean_time = lax.optimization_barrier(jnp.sum(pooled * pooled_valid, axis=1)) / half_float
        embedding = low(log_sum + mean_time)
        hidden = low_back(matmul(embedding, weight_fc1) + bias_fc1)
        gated = low(jax.nn.silu(hidden))
        class_logits = low_back(matmul(gated, weight_fc2) + bias_fc2)
        loss = jnp.sum(jax.nn.softplus(class_logits) - targets * class_logits)
        return (loss, class_logits)
    inputs = (clip_maps.astype(jnp.float32), conv1_weight.astype(jnp.float32), norm1_gain, norm1_shift, conv2_weight.astype(jnp.float32), norm2_gain, norm2_shift, fc1_weight.astype(jnp.float32), fc1_bias, fc2_weight.astype(jnp.float32), fc2_bias)
    loss, pullback, class_logits = jax.vjp(forward, *inputs, has_aux=True)
    grads = pullback(jnp.ones((), loss.dtype))
    return (class_logits, grads[0], grads[1], grads[2], grads[3], grads[4], grads[5], grads[6], grads[7], grads[8], grads[9], grads[10])
```

```python
import jax
import jax.numpy as jnp
from jax import lax
from jax.sharding import PartitionSpec as P

epsilon = 1e-05
row_chunks = 4
bf16 = jnp.bfloat16
f32 = jnp.float32


def roll_to(stacked, start, axis):
    size = stacked.shape[axis]
    doubled = jnp.concatenate([stacked, stacked], axis=axis)
    return lax.dynamic_slice_in_dim(doubled, start, size, axis=axis)


def receive_from(value, axis, size, step):
    if step % size == 0:
        return value
    return lax.ppermute(value, axis, [(i, (i - step) % size) for i in range(size)])


def send_to(value, axis, size, step):
    return lax.ppermute(value, axis, [(i, (i + step) % size) for i in range(size)])


def gather_relative(value, axis, size):
    return [receive_from(value, axis, size, step) for step in range(size)]


def scatter_sum(terms, axis, size):
    total = terms[0].astype(f32)
    for step in range(1, size):
        total = total + send_to(terms[step].astype(bf16), axis, size, step).astype(f32)
    return total


def exchange(chunks, axis, size, me):
    parts = []
    for step in range(size):
        chunk = lax.dynamic_index_in_dim(chunks, (me - step + size) % size, 0, keepdims=False)
        parts.append(receive_from(chunk, axis, size, step))
    return roll_to(jnp.stack(parts), (size - me) % size, 0)


def shifted(rows):
    zero = jnp.zeros((1, rows.shape[1]), rows.dtype)
    return jnp.concatenate(
        [
            jnp.concatenate([zero, rows[:-1]], axis=0),
            rows,
            jnp.concatenate([rows[1:], zero], axis=0),
        ],
        axis=1,
    )


def mel_taps(taps):
    grid = taps.reshape((3, 3) + taps.shape[1:])
    first = jnp.stack([grid[:, 1], grid[:, 0]], axis=2)
    second = jnp.stack([grid[:, 2], grid[:, 1]], axis=2)
    return jnp.stack([first, second], axis=1)


def fold_mel_taps(wide):
    grid = jnp.stack(
        [
            wide[:, 0, :, 1],
            wide[:, 0, :, 0] + wide[:, 1, :, 1],
            wide[:, 1, :, 0],
        ],
        axis=1,
    )
    return grid.reshape((9,) + grid.shape[2:])


def dot(left, right):
    return jnp.dot(left, right, preferred_element_type=f32)


def transpose_dot(left, right):
    return lax.dot_general(left, right, (((0,), (0,)), ((), ())), preferred_element_type=f32)


def dot_transpose(left, right):
    return lax.dot_general(left, right, (((1,), (1,)), ((), ())), preferred_element_type=f32)


def silu_slope(values_in):
    sigma = jax.nn.sigmoid(values_in)
    return sigma + values_in * sigma * (1.0 - sigma)


def both_mels(sums):
    half = sums.shape[0] // 2
    total = sums[:half] + sums[half:]
    return total, jnp.concatenate([total, total])


def norm_of(values_in, valid, pixel_count):
    _, sum_first = both_mels(jnp.sum(values_in * valid, axis=0))
    _, sum_square = both_mels(jnp.sum(values_in * values_in * valid, axis=0))
    mean_value = sum_first / pixel_count
    inv_std = lax.rsqrt(sum_square / pixel_count - mean_value * mean_value + epsilon)
    return (values_in - mean_value) * inv_std, inv_std


def make_device(dp, shard):
    everyone = ("dp", "shard")

    def in_order(gathered):
        split = gathered.reshape((dp, shard) + gathered.shape[1:])
        return jnp.swapaxes(split, 0, 1)

    def weight_in(weight, d, s):
        rows, columns = weight.shape
        part = rows // (9 * dp)
        own = lax.dynamic_index_in_dim(weight.reshape(9, dp, part, columns), d, 1, keepdims=False)
        chunks = own.reshape(9, part, shard, columns // shard)
        chunks = jnp.moveaxis(chunks, 2, 0)
        return exchange(chunks, "shard", shard, s).reshape(9, shard, part, columns // shard)

    def weight_out(grad, d, s):
        _, _, part, columns = grad.shape
        chunks = grad.astype(bf16).reshape(shard, 9, part, columns)
        parts = exchange(chunks, "shard", shard, s)
        own = jnp.moveaxis(parts, 0, 2).reshape(9, part, shard * columns)
        groups = roll_to(jnp.stack(gather_relative(own, "dp", dp)), (dp - d) % dp, 0)
        return jnp.moveaxis(groups, 0, 1).reshape(9 * dp * part, shard * columns).astype(f32)

    def on_device(
        clip_maps,
        lengths,
        labels,
        conv1_weight,
        norm1_gain,
        norm1_shift,
        conv2_weight,
        norm2_gain,
        norm2_shift,
        fc1_weight,
        fc1_bias,
        fc2_weight,
        fc2_bias,
    ):
        d, s = lax.axis_index("dp"), lax.axis_index("shard")
        clip_count, frames, mels, chan_in = clip_maps.shape
        chan_mid = norm1_gain.shape[0]
        clips = clip_count * dp * shard
        rows = clips * frames
        lane = chan_mid // (dp * shard)
        lane_in = chan_in // (dp * shard)
        wide = mels * lane

        all_lengths = in_order(lax.all_gather(lengths, everyone)).reshape(clips)
        all_labels = in_order(lax.all_gather(labels, everyone)).reshape(clips, labels.shape[1])
        frame_ids = lax.broadcasted_iota(jnp.int32, (clips, frames), 1)
        valid = (frame_ids < all_lengths[:, None]).astype(f32).reshape(rows, 1)
        pixel_count = (jnp.sum(all_lengths) * mels).astype(f32)

        own_frames = lax.broadcasted_iota(jnp.int32, (clip_count, frames), 1)
        own_valid = (own_frames < lengths[:, None])[:, :, None, None]

        masked = clip_maps * own_valid.astype(bf16)
        split = masked.reshape(clip_count, frames, mels, shard, dp, lane_in)
        chunks = jnp.moveaxis(split, 4, 0).reshape(dp, clip_count * frames, mels * shard * lane_in)
        group = exchange(chunks, "dp", dp, d).reshape(dp * clip_count * frames, mels * shard * lane_in)
        maps_in = roll_to(
            jnp.stack(gather_relative(group, "shard", shard)), (shard - s) % shard, 0
        ).reshape(rows, mels * shard * lane_in)

        taps_one = weight_in(conv1_weight, d, s).reshape(9, shard * lane_in, dp, lane)
        taps_one = roll_to(taps_one, d, 2)
        wide_one = mel_taps(taps_one)
        wide_one = jnp.moveaxis(wide_one, 3, 4).reshape(3 * mels * shard * lane_in, dp * wide)

        taps_two = weight_in(conv2_weight, d, s)
        taps_two = roll_to(roll_to(taps_two, s, 1).reshape(9, shard * lane, dp, lane), d, 2)
        wide_two = mel_taps(taps_two).reshape(3, mels, shard, lane, mels, dp, lane)
        wide_two = wide_two.transpose(0, 2, 1, 3, 5, 4, 6).reshape(3 * shard * wide, dp * wide)

        full_fc1 = lax.all_gather(fc1_weight, "shard", axis=0, tiled=True)
        full_fc2 = lax.all_gather(fc2_weight, "shard", axis=0, tiled=True)

        own_start = (s * dp + d) * lane

        def own_channels(vector):
            own = lax.dynamic_slice_in_dim(vector, own_start, lane)
            return jnp.concatenate([own] * mels)

        gain_one, shift_one = own_channels(norm1_gain), own_channels(norm1_shift)
        gain_two, shift_two = own_channels(norm2_gain), own_channels(norm2_shift)

        step = rows // row_chunks
        cuts = [slice(i * step, (i + 1) * step) for i in range(row_chunks)]

        def scatter_dp(out):
            return scatter_sum(
                [out[:, k * wide : (k + 1) * wide] for k in range(dp)], "dp", dp
            )

        first_out = jnp.concatenate(
            [scatter_dp(dot(shifted(maps_in[cut]), wide_one)) for cut in cuts], axis=0
        )
        normed_one, inv_one = norm_of(first_out, valid, pixel_count)
        pre_one = normed_one * gain_one + shift_one
        act_one = (jax.nn.silu(pre_one) * valid).astype(bf16)

        second_parts, act_parts = [], []
        for cut in cuts:
            act_part = jnp.concatenate(gather_relative(act_one[cut], "shard", shard), axis=1)
            act_parts.append(act_part)
            second_parts.append(scatter_dp(dot(shifted(act_part), wide_two)))
        second_out = jnp.concatenate(second_parts, axis=0)
        normed_two, inv_two = norm_of(second_out, valid, pixel_count)
        pre_two = normed_two * gain_two + shift_two
        act_two = jax.nn.silu(pre_two) * valid

        halves = frames // 2
        pooled = jnp.sum(act_two.reshape(clips, halves, 2, wide), axis=2)
        pooled = (pooled[:, :, :lane] + pooled[:, :, lane:]) / (2.0 * mels)
        half_len = all_lengths // 2
        half_ids = lax.broadcasted_iota(jnp.int32, (clips, halves), 1)
        pooled_valid = (half_ids < half_len[:, None]).astype(f32)[:, :, None]
        half_float = half_len.astype(f32)[:, None]
        largest = jnp.max(jnp.where(pooled_valid > 0, pooled, -1e30), axis=1, keepdims=True)
        exp_terms = jnp.exp(pooled - largest) * pooled_valid
        exp_sum = jnp.sum(exp_terms, axis=1)
        log_sum = largest[:, 0, :] + jnp.log(exp_sum)
        mean_time = jnp.sum(pooled * pooled_valid, axis=1) / half_float
        own_embedding = (log_sum + mean_time).astype(bf16)
        embedding = in_order(lax.all_gather(own_embedding, everyone))
        embedding = jnp.moveaxis(embedding, 2, 0).reshape(clips, chan_mid)
        hidden = dot(embedding, full_fc1) + fc1_bias
        gated = jax.nn.silu(hidden).astype(bf16)
        logits = dot(gated, full_fc2) + fc2_bias
        d_logits = (jax.nn.sigmoid(logits) - all_labels.astype(f32)).astype(bf16)
        d_gated = dot_transpose(d_logits, full_fc2)
        d_hidden = (d_gated * silu_slope(hidden)).astype(bf16)
        own_fc1 = lax.dynamic_slice_in_dim(fc1_weight, d * lane, lane, axis=0)
        d_embed = dot_transpose(d_hidden, own_fc1)
        soft = exp_terms / exp_sum[:, None, :]
        d_pooled = d_embed[:, None, :] * (soft + pooled_valid / half_float[:, :, None])

        fc_rows = shard_rows = fc1_weight.shape[0]
        fc1_grad = transpose_dot(
            lax.dynamic_slice_in_dim(embedding, s * fc_rows, fc_rows, axis=1), d_hidden
        )
        fc2_rows = fc2_weight.shape[0]
        fc2_grad = transpose_dot(
            lax.dynamic_slice_in_dim(gated, s * fc2_rows, fc2_rows, axis=1), d_logits
        )
        fc1_bias_grad = jnp.sum(d_hidden.astype(f32), axis=0)
        fc2_bias_grad = jnp.sum(d_logits.astype(f32), axis=0)
        own_logits = lax.dynamic_slice_in_dim(logits, (s * dp + d) * clip_count, clip_count, axis=0)

        d_frames = jnp.concatenate([d_pooled, d_pooled], axis=2) / (2.0 * mels)
        d_frames = jnp.broadcast_to(d_frames[:, :, None, :], (clips, halves, 2, wide))
        dz_two = d_frames.reshape(rows, wide) * valid * silu_slope(pre_two)
        shift_two_grad, shift_two_lanes = both_mels(jnp.sum(dz_two, axis=0))
        gain_two_grad, gain_two_lanes = both_mels(jnp.sum(dz_two * normed_two, axis=0))
        d_second = (
            gain_two
            * inv_two
            * (dz_two - (shift_two_lanes + normed_two * gain_two_lanes) / pixel_count)
            * valid
        ).astype(bf16)

        back_two = wide_two.reshape(3, shard * wide, dp * wide)[::-1]
        back_two = jnp.swapaxes(back_two, 1, 2).reshape(3 * dp * wide, shard * wide)
        d_act_parts, d_second_parts = [], []
        for cut in cuts:
            part = jnp.concatenate(gather_relative(d_second[cut], "dp", dp), axis=1)
            d_second_parts.append(part)
            out = dot(shifted(part), back_two)
            d_act_parts.append(
                scatter_sum(
                    [out[:, k * wide : (k + 1) * wide] for k in range(shard)], "shard", shard
                )
            )
        d_act_one = jnp.concatenate(d_act_parts, axis=0)
        act_all = jnp.concatenate(act_parts, axis=0)
        grad_two = transpose_dot(shifted(act_all), jnp.concatenate(d_second_parts, axis=0))
        grad_two = grad_two.reshape(3, shard, mels, lane, dp, mels, lane)
        grad_two = grad_two.transpose(0, 2, 1, 3, 5, 4, 6).reshape(
            3, mels, shard * lane, mels, dp * lane
        )
        grad_two = fold_mel_taps(grad_two).reshape(9, shard, lane, dp, lane)
        grad_two = roll_to(roll_to(grad_two, (shard - s) % shard, 1), (dp - d) % dp, 3)
        conv2_grad = weight_out(grad_two.reshape(9, shard, lane, dp * lane), d, s)

        dz_one = d_act_one * valid * silu_slope(pre_one)
        shift_one_grad, shift_one_lanes = both_mels(jnp.sum(dz_one, axis=0))
        gain_one_grad, gain_one_lanes = both_mels(jnp.sum(dz_one * normed_one, axis=0))
        d_first = (
            gain_one
            * inv_one
            * (dz_one - (shift_one_lanes + normed_one * gain_one_lanes) / pixel_count)
            * valid
        ).astype(bf16)

        back_one = wide_one.reshape(3, mels * shard * lane_in, dp * wide)[::-1]
        back_one = jnp.swapaxes(back_one, 1, 2).reshape(3 * dp * wide, mels * shard * lane_in)
        d_first_all = jnp.concatenate(
            [jnp.concatenate(gather_relative(d_first[cut], "dp", dp), axis=1) for cut in cuts], axis=0
        )
        d_in = dot(shifted(d_first_all), back_one).astype(bf16)
        d_in = d_in.reshape(shard, rows // shard, mels * shard * lane_in)
        d_in = scatter_sum(
            [
                lax.dynamic_index_in_dim(d_in, (s + k) % shard, 0, keepdims=False)
                for k in range(shard)
            ],
            "shard",
            shard,
        ).astype(bf16)
        d_in = exchange(d_in.reshape(dp, rows // (shard * dp), mels * shard * lane_in), "dp", dp, d)
        d_in = d_in.reshape(dp, clip_count, frames, mels, shard, lane_in)
        input_grad = jnp.moveaxis(d_in, 0, 4).reshape(clip_maps.shape).astype(f32)
        input_grad = input_grad * own_valid.astype(f32)

        grad_one = transpose_dot(shifted(maps_in), d_first_all)
        grad_one = grad_one.reshape(3, mels, shard * lane_in, dp, mels, lane)
        grad_one = jnp.moveaxis(grad_one, 4, 3).reshape(3, mels, shard * lane_in, mels, dp * lane)
        grad_one = fold_mel_taps(grad_one).reshape(9, shard, lane_in, dp, lane)
        grad_one = roll_to(grad_one, (dp - d) % dp, 3)
        conv1_grad = weight_out(grad_one.reshape(9, shard, lane_in, dp * lane), d, s)

        norm_grads = jnp.stack([gain_one_grad, shift_one_grad, gain_two_grad, shift_two_grad])
        norm_grads = in_order(lax.all_gather(norm_grads, everyone))
        norm_grads = jnp.moveaxis(norm_grads, 2, 0).reshape(4, chan_mid)
        return (
            own_logits,
            input_grad,
            conv1_grad,
            norm_grads[0],
            norm_grads[1],
            conv2_grad,
            norm_grads[2],
            norm_grads[3],
            fc1_grad,
            fc1_bias_grad,
            fc2_grad,
            fc2_bias_grad,
        )

    return on_device


def patch_rows(grid_in):
    clip_count, frame_count, mel_count, chan_count = grid_in.shape
    padded = jnp.pad(grid_in, ((0, 0), (1, 1), (1, 1), (0, 0)))
    tap_list = [
        padded[:, shift_t : shift_t + frame_count, shift_m : shift_m + mel_count, :]
        for shift_t in range(3)
        for shift_m in range(3)
    ]
    stacked = jnp.stack(tap_list, axis=3)
    return stacked.reshape(clip_count * frame_count * mel_count, 9 * chan_count)


def fold_rows(grad_rows, clip_count, frame_count, mel_count):
    chan_count = grad_rows.shape[1] // 9
    tap_terms = grad_rows.reshape(clip_count, frame_count, mel_count, 9, chan_count)
    summed = jnp.zeros((clip_count, frame_count + 2, mel_count + 2, chan_count), jnp.float32)
    for tap_index in range(9):
        shift_t = tap_index // 3
        shift_m = tap_index % 3
        summed = summed + jnp.pad(
            tap_terms[:, :, :, tap_index, :],
            ((0, 0), (shift_t, 2 - shift_t), (shift_m, 2 - shift_m), (0, 0)),
        )
    return summed[:, 1 : frame_count + 1, 1 : mel_count + 1, :]


def normalize(values_in, sum_first, sum_square, pixel_count, gain, shift):
    mean_value = sum_first / pixel_count
    inv_std = lax.rsqrt(sum_square / pixel_count - mean_value * mean_value + epsilon)
    normed = (values_in - mean_value) * inv_std
    return (normed, inv_std, normed * gain + shift)


def make_valid(clip_lengths, frame_count, mel_count):
    clip_count = clip_lengths.shape[0]
    frame_ids = lax.broadcasted_iota(jnp.int32, (clip_count, frame_count), 1)
    valid_two = (frame_ids < clip_lengths[:, None]).astype(jnp.float32)
    pixel_valid = jnp.broadcast_to(
        valid_two[:, :, None], (clip_count, frame_count, mel_count)
    ).reshape(-1, 1)
    return (valid_two[:, :, None, None], pixel_valid)


def pool_map(act_grid):
    clip_count, frame_count, mel_count, chans = act_grid.shape
    pooled = jnp.mean(
        act_grid.reshape(clip_count, frame_count // 2, 2, mel_count // 2, 2, chans), axis=(2, 4)
    )
    return jnp.mean(pooled, axis=2)


def pooled_slope(d_pooled, pre_two, pixel_valid, mel_count):
    clip_count, half_frames, chans = d_pooled.shape
    d_frames = jnp.repeat(d_pooled, 2, axis=1)[:, :, None, :] / (2.0 * mel_count)
    d_act_two = jnp.broadcast_to(d_frames, (clip_count, 2 * half_frames, mel_count, chans)).reshape(
        -1, chans
    )
    return d_act_two * pixel_valid * silu_slope(pre_two)


def tag_head(
    pooled, clip_lengths, labels, full_fc1, full_fc2, back_fc1, back_fc2, fc1_bias, fc2_bias
):
    clip_count, half_frames, chans = pooled.shape
    half_ids = lax.broadcasted_iota(jnp.int32, (clip_count, half_frames), 1)
    half_len = clip_lengths // 2
    pooled_valid = (half_ids < half_len[:, None]).astype(jnp.float32)[:, :, None]
    half_float = half_len.astype(jnp.float32)[:, None]
    largest = jnp.max(jnp.where(pooled_valid > 0, pooled, -1e30), axis=1, keepdims=True)
    exp_terms = jnp.exp(pooled - largest) * pooled_valid
    exp_sum = jnp.sum(exp_terms, axis=1)
    log_sum = largest[:, 0, :] + jnp.log(exp_sum)
    mean_time = jnp.sum(pooled * pooled_valid, axis=1) / half_float
    embedding = (log_sum + mean_time).astype(jnp.bfloat16)
    hidden = jnp.dot(embedding, full_fc1, preferred_element_type=jnp.float32) + fc1_bias
    gated_low = jax.nn.silu(hidden).astype(jnp.bfloat16)
    class_logits = jnp.dot(gated_low, full_fc2, preferred_element_type=jnp.float32) + fc2_bias
    d_logits = (jax.nn.sigmoid(class_logits) - labels.astype(jnp.float32)).astype(jnp.bfloat16)
    fc2_term = transpose_dot(gated_low, d_logits)
    fc2_bias_term = jnp.sum(d_logits.astype(jnp.float32), axis=0)
    d_gated = jnp.dot(d_logits, back_fc2.T, preferred_element_type=jnp.float32)
    d_hidden = (d_gated * silu_slope(hidden)).astype(jnp.bfloat16)
    fc1_term = transpose_dot(embedding, d_hidden)
    fc1_bias_term = jnp.sum(d_hidden.astype(jnp.float32), axis=0)
    d_embed = jnp.dot(d_hidden, back_fc1.T, preferred_element_type=jnp.float32)
    soft_weights = exp_terms / exp_sum[:, None, :]
    d_pooled = d_embed[:, None, :] * (soft_weights + pooled_valid / half_float[:, :, None])
    return (class_logits, d_pooled, fc1_term, fc2_term, fc1_bias_term, fc2_bias_term)


def on_device(
    clip_maps,
    lengths,
    labels,
    conv1_weight,
    norm1_gain,
    norm1_shift,
    conv2_weight,
    norm2_gain,
    norm2_shift,
    fc1_weight,
    fc1_bias,
    fc2_weight,
    fc2_bias,
):
    clip_count, frame_count, mel_count, chan_in = clip_maps.shape
    chan_mid = norm1_gain.shape[0]
    valid_four, pixel_valid = make_valid(lengths, frame_count, mel_count)
    masked = clip_maps * valid_four.astype(jnp.bfloat16)
    sent = (conv1_weight, conv2_weight, fc1_weight, fc2_weight)
    gathered = (
        lax.all_gather(sent[0], "shard", axis=0, tiled=True),
        lax.all_gather(sent[1], "shard", axis=0, tiled=True),
        lax.all_gather(sent[2], "shard", axis=0, tiled=True),
        lax.all_gather(sent[3], "shard", axis=0, tiled=True),
    )
    full_one, full_two, full_fc1, full_fc2 = gathered
    patch_one = patch_rows(masked)
    first_out = jnp.dot(patch_one, full_one, preferred_element_type=jnp.float32)
    sum_one, square_one, pixel_count = lax.psum(
        (
            jnp.sum(first_out * pixel_valid, axis=0),
            jnp.sum(first_out * first_out * pixel_valid, axis=0),
            jnp.sum(pixel_valid),
        ),
        ("dp", "shard"),
    )
    normed_one, inv_one, pre_one = normalize(
        first_out, sum_one, square_one, pixel_count, norm1_gain, norm1_shift
    )
    act_one = (jax.nn.silu(pre_one) * pixel_valid).astype(jnp.bfloat16)
    patch_two = patch_rows(act_one.reshape(clip_count, frame_count, mel_count, chan_mid))
    second_out = jnp.dot(patch_two, full_two, preferred_element_type=jnp.float32)
    sum_two, square_two = lax.psum(
        (
            jnp.sum(second_out * pixel_valid, axis=0),
            jnp.sum(second_out * second_out * pixel_valid, axis=0),
        ),
        ("dp", "shard"),
    )
    normed_two, inv_two, pre_two = normalize(
        second_out, sum_two, square_two, pixel_count, norm2_gain, norm2_shift
    )
    act_two = (jax.nn.silu(pre_two) * pixel_valid).reshape(
        clip_count, frame_count, mel_count, chan_mid
    )
    pooled_own = pool_map(act_two)
    back_weights = (
        lax.all_gather(sent[0], "shard", axis=0, tiled=True),
        lax.all_gather(sent[1], "shard", axis=0, tiled=True),
        lax.all_gather(sent[2], "shard", axis=0, tiled=True),
        lax.all_gather(sent[3], "shard", axis=0, tiled=True),
    )
    back_one, back_two, back_fc1, back_fc2 = back_weights
    class_logits, d_pooled, fc1_term, fc2_term, fc1_bias_term, fc2_bias_term = tag_head(
        pooled_own, lengths, labels, full_fc1, full_fc2, back_fc1, back_fc2, fc1_bias, fc2_bias
    )
    dz_two = pooled_slope(d_pooled, pre_two, pixel_valid, mel_count)
    shift_two_grad, gain_two_grad, fc1_bias_grad, fc2_bias_grad = lax.psum(
        (
            jnp.sum(dz_two, axis=0),
            jnp.sum(dz_two * normed_two, axis=0),
            fc1_bias_term,
            fc2_bias_term,
        ),
        ("dp", "shard"),
    )
    d_second = (
        norm2_gain
        * inv_two
        * (dz_two - (shift_two_grad + normed_two * gain_two_grad) / pixel_count)
        * pixel_valid
    ).astype(jnp.bfloat16)
    conv2_part = lax.psum_scatter(
        transpose_dot(patch_two, d_second), "shard", scatter_dimension=0, tiled=True
    )
    d_patch_two = jnp.dot(d_second, back_two.T, preferred_element_type=jnp.float32)
    d_act_one = fold_rows(d_patch_two, clip_count, frame_count, mel_count).reshape(-1, chan_mid)
    dz_one = d_act_one * pixel_valid * silu_slope(pre_one)
    shift_one_grad, gain_one_grad = lax.psum(
        (jnp.sum(dz_one, axis=0), jnp.sum(dz_one * normed_one, axis=0)), ("dp", "shard")
    )
    d_first = (
        norm1_gain
        * inv_one
        * (dz_one - (shift_one_grad + normed_one * gain_one_grad) / pixel_count)
        * pixel_valid
    ).astype(jnp.bfloat16)
    conv1_term = transpose_dot(patch_one, d_first)
    d_patch_one = jnp.dot(d_first, back_one.T, preferred_element_type=jnp.float32)
    input_grad = fold_rows(d_patch_one, clip_count, frame_count, mel_count) * valid_four
    conv1_part, fc1_part, fc2_part = (
        lax.psum_scatter(conv1_term, "shard", scatter_dimension=0, tiled=True),
        lax.psum_scatter(fc1_term, "shard", scatter_dimension=0, tiled=True),
        lax.psum_scatter(fc2_term, "shard", scatter_dimension=0, tiled=True),
    )
    conv1_grad, conv2_grad, fc1_grad, fc2_grad = (
        lax.psum(conv1_part.astype(jnp.bfloat16), "dp").astype(jnp.float32),
        lax.psum(conv2_part.astype(jnp.bfloat16), "dp").astype(jnp.float32),
        lax.psum(fc1_part.astype(jnp.bfloat16), "dp").astype(jnp.float32),
        lax.psum(fc2_part.astype(jnp.bfloat16), "dp").astype(jnp.float32),
    )
    return (
        class_logits,
        input_grad,
        conv1_grad,
        gain_one_grad,
        shift_one_grad,
        conv2_grad,
        gain_two_grad,
        shift_two_grad,
        fc1_grad,
        fc1_bias_grad,
        fc2_grad,
        fc2_bias_grad,
    )


def solution(mesh):
    both = ("dp", "shard")
    in_specs = (
        P(both, None, None, None),
        P(both),
        P(both, None),
        P("shard", None),
        P(),
        P(),
        P("shard", None),
        P(),
        P(),
        P("shard", None),
        P(),
        P("shard", None),
        P(),
    )
    out_specs = (
        P(both, None),
        P(both, None, None, None),
        P("shard", None),
        P(),
        P(),
        P("shard", None),
        P(),
        P(),
        P("shard", None),
        P(),
        P("shard", None),
        P(),
    )
    dp, shard = mesh.shape["dp"], mesh.shape["shard"]
    step = make_device(dp, shard) if shard <= 8 else on_device
    return jax.shard_map(
        step, mesh=mesh, in_specs=in_specs, out_specs=out_specs, check_vma=False
    )
```

```python
import functools
import math
import jax
import jax.numpy as jnp
from jax import lax
from jax.experimental import pallas as pl
from jax.experimental.pallas import tpu as pltpu
from jax.sharding import PartitionSpec as P
bf16 = jnp.bfloat16
f32 = jnp.float32
epsilon = 1e-05
big_vmem = 56 * 1024 * 1024
VM = pl.BlockSpec(memory_space=pltpu.VMEM)
SM = pl.BlockSpec(memory_space=pltpu.SMEM)
HB = pl.BlockSpec(memory_space=pl.ANY)

def params():
    return pltpu.CompilerParams(vmem_limit_bytes=big_vmem)

def cost(flops, moved):
    return pl.CostEstimate(flops=int(flops), bytes_accessed=int(moved), transcendentals=0)


def split_kernel(shard, place, weight, *refs):
    outs, (own, sem) = refs[:shard], refs[shard:]
    copy = pltpu.make_async_copy(weight.at[:, place[0]], own, sem)
    copy.start()
    copy.wait()
    for step in range(shard):
        column = lax.rem(place[1] - step + shard, shard)
        width = outs[step].shape[2]
        outs[step][...] = own[:, :, pl.ds(pl.multiple_of(column * width, width), width)]


def split_weight(weight, place, dp, shard):
    rows, columns = weight.shape
    part = rows // (9 * dp)
    chunk = jax.ShapeDtypeStruct((9, part, columns // shard), bf16)
    return pl.pallas_call(
        functools.partial(split_kernel, shard),
        out_shape=[chunk] * shard,
        in_specs=[SM, HB],
        out_specs=[VM] * shard,
        scratch_shapes=[pltpu.VMEM((9, part, columns), bf16), pltpu.SemaphoreType.DMA(())],
        compiler_params=params(),
        cost_estimate=cost(0, 4 * rows * columns // dp),
        name="split_weight",
    )(place, weight.reshape(9, dp, part, columns))


def expand_kernel(shard, by_mel, table, *refs):
    pieces, (spread, out, held) = refs[:shard], refs[shard:]
    for step in range(shard):
        held[pl.ds(9 * step, 9)] = pieces[step][...]
    part = held.shape[1]

    def one(position, carry):
        for a in range(3):
            taps = [held[table[(3 * a + b) * shard + position]] for b in range(3)]
            for m in range(2):
                pair = jnp.concatenate([taps[m + 1], taps[m]], axis=1)
                wide = jnp.dot(pair, spread[...], preferred_element_type=f32).astype(bf16)
                if by_mel:
                    out[a, m, position] = wide
                else:
                    out[a, position, pl.ds(m * part, part)] = wide
        return carry

    lax.fori_loop(0, shard, one, 0)


def expand_weight(pieces, table, spread, by_mel):
    shard = len(pieces)
    _, part, columns = pieces[0].shape
    shape = (3, 2, shard, part, 2 * columns) if by_mel else (3, shard, 2 * part, 2 * columns)
    wide = pl.pallas_call(
        functools.partial(expand_kernel, shard, by_mel),
        out_shape=jax.ShapeDtypeStruct(shape, bf16),
        in_specs=[SM] + [VM] * (shard + 1),
        out_specs=VM,
        scratch_shapes=[pltpu.VMEM((9 * shard, part, columns), bf16)],
        compiler_params=params(),
        cost_estimate=cost(2 * 6 * shard * part * 4 * columns * columns, 30 * shard * part * columns),
        name="expand_weight",
    )(table, *pieces, spread)
    return wide.reshape(3, 2 * shard * part, 2 * columns)


def conv_kernel(count, back, split, tile, *refs):
    rows_in, taps, outs, (first, last) = refs[:count], refs[count], refs[count + 1 : -2], refs[-2:]
    height = first.shape[0] - 8
    width = first.shape[1]
    first[0:8] = jnp.zeros((8, width), f32)
    last[height:] = jnp.zeros((8, width), f32)
    late, early = (2, 0) if back else (0, 2)
    contract = (((1,), (1,)), ((), ())) if back else (((1,), (0,)), ((), ()))

    def block(ref, at):
        value = ref[at] if len(ref.shape) == 2 else jnp.concatenate(
            [ref[i, at] for i in range(ref.shape[0])], axis=1)
        return value

    def one(i, carry):
        at = pl.ds(pl.multiple_of(i * tile, tile), tile)
        rows = jnp.concatenate([block(ref, at) for ref in rows_in], axis=1)
        first[pl.ds(pl.multiple_of(i * tile + 8, 8), tile)] = lax.dot_general(
            rows, taps[late], contract, preferred_element_type=f32)
        last[at] = lax.dot_general(rows, taps[early], contract, preferred_element_type=f32)
        return carry

    lax.fori_loop(0, height // tile, one, 0)

    def two(i, carry):
        start = pl.multiple_of(i * tile, tile)
        at = pl.ds(start, tile)
        rows = jnp.concatenate([block(ref, at) for ref in rows_in], axis=1)
        total = lax.dot_general(rows, taps[1], contract, preferred_element_type=f32)
        before = first[pl.ds(start, tile + 8)]
        after = last[pl.ds(start, tile + 8)]
        total = total + before[7 : tile + 7] + after[1 : tile + 1]
        total = total.astype(bf16)
        column = 0
        for out in outs:
            if len(out.shape) == 2:
                step = out.shape[1]
                out[at] = total[:, column : column + step]
                column += step
            else:
                step = out.shape[2]
                for k in range(out.shape[0]):
                    out[k, at] = total[:, column : column + step]
                    column += step
        return carry

    lax.fori_loop(0, height // tile, two, 0)


def convolve(rows_in, taps, out_shapes, back=False, tile=256, name="convolve"):
    height = rows_in[0].shape[-2]
    width = taps.shape[1] if back else taps.shape[2]
    moved = 2 * (sum(r.size for r in rows_in) + taps.size + sum(math.prod(s) for s in out_shapes))
    return pl.pallas_call(
        functools.partial(conv_kernel, len(rows_in), back, None, tile),
        out_shape=[jax.ShapeDtypeStruct(s, bf16) for s in out_shapes],
        in_specs=[VM] * (len(rows_in) + 1),
        out_specs=[VM] * len(out_shapes),
        scratch_shapes=[pltpu.VMEM((height + 8, width), f32)] * 2,
        compiler_params=params(),
        cost_estimate=cost(2 * height * taps.size, moved),
        name=name,
    )(*rows_in, taps)


def grad_kernel(chunks, x_count, g_count, part, by_mel, shard, tile, table, *refs):
    n = chunks * x_count
    x_refs, g_refs = refs[:n], refs[n : n + chunks * g_count]
    spread, outs = refs[n + chunks * g_count], refs[n + chunks * g_count + 1 : -2]
    total, moved = refs[-2:]
    height = g_refs[0].shape[0]
    half = spread.shape[0] // 2
    total[...] = jnp.zeros_like(total)

    def block(ref, at):
        return ref[at] if len(ref.shape) == 2 else jnp.concatenate(
            [ref[i, at] for i in range(ref.shape[0])], axis=1)

    width = 2 * half
    moved[0:8] = jnp.zeros((8, width), f32)
    moved[height + 8 :] = jnp.zeros((8, width), f32)
    for chunk in range(chunks):
        xs = x_refs[chunk * x_count : (chunk + 1) * x_count]
        gs = g_refs[chunk * g_count : (chunk + 1) * g_count]
        column = 0
        for g in gs:
            moved[8 : height + 8, column : column + g.shape[1]] = g[...].astype(f32)
            column += g.shape[1]

        def one(i, carry, xs=xs):
            start = pl.multiple_of(i * tile, tile)
            at = pl.ds(start, tile)
            rows = jnp.concatenate([block(ref, at) for ref in xs], axis=1)
            around = moved[pl.ds(start, tile + 16)]
            three = jnp.concatenate(
                [around[9 - a : 9 - a + tile].astype(bf16) for a in range(3)], axis=1)
            total[...] += lax.dot_general(
                rows, three, (((0,), (0,)), ((), ())), preferred_element_type=f32)
            return carry

        lax.fori_loop(0, height // tile, one, 0)

    def fold(position, carry):
        for a in range(3):
            if by_mel:
                at = [pl.multiple_of((m * shard + position) * part, part) for m in range(2)]
            else:
                at = [pl.multiple_of((2 * position + m) * part, part) for m in range(2)]
            rows = [total[pl.ds(start, part), a * width : (a + 1) * width].astype(bf16) for start in at]
            top, bottom = [
                lax.dot_general(r, spread[...], (((1,), (1,)), ((), ())), preferred_element_type=f32)
                for r in rows
            ]
            taps = [top[:, half:], top[:, :half] + bottom[:, half:], bottom[:, :half]]
            for b in range(3):
                outs[0][table[(3 * a + b) * shard + position]] = taps[b].astype(bf16)
        return carry

    lax.fori_loop(0, shard, fold, 0)


def weight_grad(x_chunks, g_chunks, table, spread, part, by_mel, shard, tile=256, name="weight_grad"):
    chunks = len(x_chunks)
    xs = [x for chunk in x_chunks for x in chunk]
    gs = [g for chunk in g_chunks for g in chunk]
    height = gs[0].shape[0]
    wide = spread.shape[0]
    deep = 2 * shard * part
    flops = 2 * chunks * height * deep * wide * 3
    return pl.pallas_call(
        functools.partial(grad_kernel, chunks, len(x_chunks[0]), len(g_chunks[0]), part, by_mel, shard, tile),
        out_shape=jax.ShapeDtypeStruct((9 * shard, part, wide // 2), bf16),
        in_specs=[SM] + [VM] * (len(xs) + len(gs) + 1),
        out_specs=VM,
        scratch_shapes=[pltpu.VMEM((deep, 3 * wide), f32), pltpu.VMEM((height + 16, wide), f32)],
        compiler_params=params(),
        cost_estimate=cost(flops, sum(2 * v.size for v in xs + gs) + 9 * shard * part * wide),
        name=name,
    )(table, *xs, *gs, spread)


def join_kernel(dp, shard, place, *refs):
    parts, out = refs[:-1], refs[-1]
    half = shard // 2
    width = parts[0].shape[3]
    for source in range(dp):
        group = lax.bitwise_xor(place[0], source)
        for step in range(shard):
            column = lax.rem(place[1] + step, shard)
            value = parts[2 * source + step // half][step % half, 0]
            out[0, group, :, pl.ds(pl.multiple_of(column * width, width), width)] = value.astype(f32)


def join_grad(parts, place, dp, shard):
    half, _, part, width = parts[0].shape
    block = pl.BlockSpec((half, 1, part, width), lambda i: (0, i, 0, 0))
    out = pl.pallas_call(
        functools.partial(join_kernel, dp, shard),
        grid=(9,),
        out_shape=jax.ShapeDtypeStruct((9, dp, part, shard * width), f32),
        in_specs=[SM] + [block] * len(parts),
        out_specs=pl.BlockSpec((1, dp, part, shard * width), lambda i: (i, 0, 0, 0)),
        compiler_params=params(),
        cost_estimate=cost(0, 6 * 9 * dp * part * shard * width),
        name="join_grad",
    )(place, *parts)
    return out.reshape(9 * dp * part, shard * width)


def roll_to(stacked, start, axis):
    size = stacked.shape[axis]
    doubled = jnp.concatenate([stacked, stacked], axis=axis)
    return lax.dynamic_slice_in_dim(doubled, start, size, axis=axis)


def pick(stacked, index):
    return lax.dynamic_index_in_dim(stacked, index, 0, keepdims=False)


def dot(left, right):
    return jnp.dot(left, right, preferred_element_type=f32)


def dot_transpose(left, right):
    return lax.dot_general(left, right, (((1,), (1,)), ((), ())), preferred_element_type=f32)


def both_mels(sums):
    half = sums.shape[0] // 2
    total = sums[:half] + sums[half:]
    return total, jnp.concatenate([total, total])


def norm_of(values_in, valid, pixel_count):
    _, sum_first = both_mels(jnp.sum(values_in * valid, axis=0))
    _, sum_square = both_mels(jnp.sum(values_in * values_in * valid, axis=0))
    mean_value = sum_first / pixel_count
    inv_std = lax.rsqrt(sum_square / pixel_count - mean_value * mean_value + epsilon)
    return (values_in - mean_value) * inv_std, inv_std


def make_device(dp, shard):
    depth = shard // 2

    def permute(value, axis, size, move):
        return lax.ppermute(value, axis, [(i, move(i) % size) for i in range(size)])

    def from_z(value, k):
        return permute(value, "shard", shard, lambda i: i - 2 * k)

    def to_z(value, k):
        return permute(value, "shard", shard, lambda i: i + 2 * k)

    def from_shard(value, k):
        return permute(value, "shard", shard, lambda i: i - k)

    def other_core(value):
        return permute(value, "shard", shard, lambda i: i ^ 1)

    def other_dp(value, r):
        return permute(value, "dp", dp, lambda i: i ^ r)

    def gather_dp(value, order):
        one, two = other_dp(value, 1), other_dp(value, 2)
        three = other_dp(one, 2) if order == 0 else other_dp(two, 1)
        return [value, one, two, three]

    def unswap(parts, d):
        low = [jnp.where(d % 2 == 1, parts[r ^ 1], parts[r]) for r in range(dp)]
        return [jnp.where(d // 2 == 1, low[r ^ 2], low[r]) for r in range(dp)]

    def core_order(mine, theirs, c):
        return [jnp.where(c == 0, mine, theirs), jnp.where(c == 0, theirs, mine)]

    def gather_small(value, d, z, c):
        line = jnp.stack([value] + [from_z(value, k) for k in range(1, depth)])
        line = roll_to(line, (depth - z) % depth, 0)
        pair = jnp.stack(core_order(line, other_core(line), c), axis=1)
        return jnp.stack(unswap([pair] + [other_dp(pair, r) for r in range(1, dp)], d), axis=2)

    def weight_in(weight, place):
        pieces = split_weight(weight, place, dp, shard)
        return [pieces[0]] + [from_shard(pieces[k], k) for k in range(1, shard)]

    def weight_out(grad, place):
        part, width = grad.shape[1:]
        pieces = grad.reshape(shard, 9, part, width)
        parts = [pieces[0]] + [from_shard(pieces[shard - k], k) for k in range(1, shard)]
        half = shard // 2
        low = gather_dp(jnp.stack(parts[:half]), 0)
        high = gather_dp(jnp.stack(parts[half:]), 1)
        return join_grad([h for pair in zip(low, high) for h in pair], place, dp, shard)

    def on_device(
        clip_maps,
        lengths,
        labels,
        conv1_weight,
        norm1_gain,
        norm1_shift,
        conv2_weight,
        norm2_gain,
        norm2_shift,
        fc1_weight,
        fc1_bias,
        fc2_weight,
        fc2_bias,
    ):
        d, s = lax.axis_index("dp"), lax.axis_index("shard")
        z, c = s // 2, s % 2
        place = jnp.stack([d, s]).astype(jnp.int32)
        clip_count, frames, mels, chan_in = clip_maps.shape
        chan_mid = norm1_gain.shape[0]
        classes = labels.shape[1]
        clips = clip_count * dp * shard
        rows = clips * frames
        step = rows // depth
        own_rows = clip_count * frames
        lane = chan_mid // (dp * shard)
        lane_in = chan_in // (dp * shard)
        wide = mels * lane
        quarter = shard * lane_in
        wide_in = mels * quarter

        position = lax.broadcasted_iota(jnp.int32, (9, shard), 1)
        tap = lax.broadcasted_iota(jnp.int32, (9, shard), 0)

        def table_of(block):
            group = tap * shard + block
            return (((group // 9 - s + shard) % shard) * 9 + group % 9).reshape(9 * shard).astype(jnp.int32)

        table_one = table_of(position)
        table_two = table_of(2 * ((z + position % depth) % depth) + (c ^ (position // depth)))

        from_row = lax.broadcasted_iota(jnp.int32, (dp * wide, dp * wide), 0)
        to_lane = lax.broadcasted_iota(jnp.int32, (dp * wide, dp * wide), 1)
        spread = (
            (from_row // (dp * lane) == to_lane // lane % mels)
            & (from_row // lane % dp == (d ^ (to_lane // wide)))
            & (from_row % lane == to_lane % lane)
        ).astype(bf16)
        from_row = lax.broadcasted_iota(jnp.int32, (chan_in, chan_in), 0)
        to_lane = lax.broadcasted_iota(jnp.int32, (chan_in, chan_in), 1)
        sort_in = (
            (from_row // (dp * lane_in) == to_lane // lane_in % shard)
            & (from_row // lane_in % dp == (d ^ (to_lane // quarter)))
            & (from_row % lane_in == to_lane % lane_in)
        ).astype(bf16)

        pieces_one = weight_in(conv1_weight, place)
        own_frames = lax.broadcasted_iota(jnp.int32, (clip_count, frames), 1)
        own_valid = (own_frames < lengths[:, None])[:, :, None, None]
        masked = clip_maps * own_valid.astype(bf16)
        sorted_in = [dot(masked[:, :, m].reshape(own_rows, chan_in), sort_in).astype(bf16) for m in range(mels)]
        from_dp = []
        for r in range(dp):
            at = slice(r * quarter, (r + 1) * quarter)
            part = jnp.concatenate([v[:, at] for v in sorted_in], axis=1)
            from_dp.append(other_dp(part, r) if r else part)
        group = jnp.concatenate(unswap(from_dp, d), axis=0)
        maps_in = []
        for k in range(depth):
            mine = from_z(group, k) if k else group
            maps_in.append(jnp.concatenate(core_order(mine, other_core(mine), c), axis=0))
        wide_one = expand_weight(pieces_one, table_one, spread, True)

        notes = jnp.concatenate([labels, lengths[:, None]], axis=1).astype(bf16)
        notes = jnp.pad(notes, ((0, 0), (0, -(classes + 1) % 128)))
        notes = gather_small(notes, d, z, c).reshape(clips, notes.shape[1])
        all_labels = notes[:, :classes].astype(f32)
        all_lengths = notes[:, classes].astype(jnp.int32)
        frame_ids = lax.broadcasted_iota(jnp.int32, (clips, frames), 1)
        valid = (frame_ids < all_lengths[:, None]).astype(f32).reshape(rows, 1)
        valid_here = roll_to(valid.reshape(depth, step, 1), z, 0).reshape(rows, 1)
        pixel_count = (jnp.sum(all_lengths) * mels).astype(f32)

        pieces_two = weight_in(conv2_weight, place)
        wide_two = expand_weight(pieces_two, table_two, spread, False)

        fc_rows = fc1_weight.shape[0]
        pad = -classes % 128
        both_fc = jnp.concatenate([fc1_weight, jnp.pad(fc2_weight, ((0, 0), (0, pad)))], axis=1)
        own_fc = lax.dynamic_slice_in_dim(both_fc, d * lane, lane, axis=0)
        line = jnp.stack([own_fc] + [from_z(own_fc, k) for k in range(1, depth)])
        line = roll_to(line, (depth - z) % depth, 0)
        square = jnp.stack(unswap(gather_dp(line, 0), d), axis=1)
        full_fc = jnp.stack(core_order(square, other_core(square), c), axis=1)
        full_fc = full_fc.reshape(chan_mid, both_fc.shape[1])
        full_fc1, full_fc2 = full_fc[:, : fc1_weight.shape[1]], full_fc[:, fc1_weight.shape[1] :][:, :classes]

        own_start = (s * dp + d) * lane

        def own_channels(vector):
            own = lax.dynamic_slice_in_dim(vector, own_start, lane)
            return jnp.concatenate([own] * mels)

        gain_one, shift_one = own_channels(norm1_gain), own_channels(norm1_shift)
        gain_two, shift_two = own_channels(norm2_gain), own_channels(norm2_shift)

        def scatter_dp(outs):
            total = outs[0].astype(f32)
            for r in range(1, dp):
                total = total + other_dp(outs[r], r).astype(f32)
            return total

        parts = [scatter_dp(convolve([v], wide_one, [(step, wide)] * dp, name="conv1")) for v in maps_in]
        first_out = jnp.concatenate(parts, axis=0)
        normed_one, inv_one = norm_of(first_out, valid_here, pixel_count)
        pre_one = normed_one * gain_one + shift_one
        act_one = (jax.nn.silu(pre_one) * valid_here).astype(bf16).reshape(depth, step, wide)

        acts, parts = [], []
        for p in range(depth):
            own = pick(act_one, (p - z + depth) % depth)
            line = [own] + [from_z(own, k) for k in range(1, depth)]
            acts.append(line + [other_core(v) for v in line])
            parts.append(scatter_dp(convolve(acts[p], wide_two, [(step, wide)] * dp, name="conv2")))
        second_out = jnp.concatenate(parts, axis=0)
        normed_two, inv_two = norm_of(second_out, valid, pixel_count)
        pre_two = normed_two * gain_two + shift_two
        sigma_two = jax.nn.sigmoid(pre_two)
        act_two = pre_two * sigma_two * valid
        slope_two = (sigma_two + act_two * (1.0 - sigma_two)) * valid

        halves = frames // 2
        pooled = jnp.sum(act_two.reshape(clips, halves, 2, wide), axis=2)
        pooled = (pooled[:, :, :lane] + pooled[:, :, lane:]) / (2.0 * mels)
        half_len = all_lengths // 2
        half_ids = lax.broadcasted_iota(jnp.int32, (clips, halves), 1)
        pooled_valid = (half_ids < half_len[:, None]).astype(f32)[:, :, None]
        half_float = half_len.astype(f32)[:, None]
        largest = jnp.max(jnp.where(pooled_valid > 0, pooled, -1e30), axis=1, keepdims=True)
        exp_terms = jnp.exp(pooled - largest) * pooled_valid
        exp_sum = jnp.sum(exp_terms, axis=1)
        log_sum = largest[:, 0, :] + jnp.log(exp_sum)
        mean_time = jnp.sum(pooled * pooled_valid, axis=1) / half_float
        own_embedding = (log_sum + mean_time).astype(bf16)
        embedding = gather_small(own_embedding, d, z, c).reshape(dp * shard, clips, lane)
        embedding = jnp.moveaxis(embedding, 0, 1).reshape(clips, chan_mid)
        hidden = dot(embedding, full_fc1) + fc1_bias
        sigma = jax.nn.sigmoid(hidden)
        gated = (hidden * sigma).astype(bf16)
        logits = dot(gated, full_fc2) + fc2_bias
        d_logits = (jax.nn.sigmoid(logits) - all_labels).astype(bf16)
        d_gated = dot_transpose(d_logits, full_fc2)
        d_hidden = (d_gated * (sigma + hidden * sigma * (1.0 - sigma))).astype(bf16)
        own_fc1 = lax.dynamic_slice_in_dim(fc1_weight, d * lane, lane, axis=0)
        d_embed = dot_transpose(d_hidden, own_fc1)
        soft = exp_terms / exp_sum[:, None, :]
        d_pooled = d_embed[:, None, :] * (soft + pooled_valid / half_float[:, :, None])

        own_columns = lax.dynamic_slice_in_dim(embedding, s * fc_rows, fc_rows, axis=1)
        fc1_grad = dot(own_columns.T, d_hidden)
        own_columns = lax.dynamic_slice_in_dim(gated, s * fc_rows, fc_rows, axis=1)
        fc2_grad = dot(own_columns.T, d_logits)
        fc1_bias_grad = jnp.sum(d_hidden.astype(f32), axis=0)
        fc2_bias_grad = jnp.sum(d_logits.astype(f32), axis=0)
        own_logits = lax.dynamic_slice_in_dim(logits, (s * dp + d) * clip_count, clip_count, axis=0)

        d_frames = jnp.concatenate([d_pooled, d_pooled], axis=2) / (2.0 * mels)
        d_frames = jnp.broadcast_to(d_frames[:, :, None, :], (clips, halves, 2, wide))
        dz_two = d_frames.reshape(rows, wide) * slope_two
        shift_two_grad, shift_two_lanes = both_mels(jnp.sum(dz_two, axis=0))
        gain_two_grad, gain_two_lanes = both_mels(jnp.sum(dz_two * normed_two, axis=0))
        d_second = (
            gain_two
            * inv_two
            * (dz_two - (shift_two_lanes + normed_two * gain_two_lanes) / pixel_count)
            * valid
        ).astype(bf16)

        parts, grads = [], []
        for p in range(depth):
            grads.append(gather_dp(d_second[p * step : (p + 1) * step], p % 2))
            mine, theirs = convolve(grads[p], wide_two, [(depth, step, wide)] * 2, back=True, name="back2")
            line = mine.astype(f32) + other_core(theirs).astype(f32)
            total = line[0]
            for k in range(1, depth):
                total = total + to_z(line[k].astype(bf16), k).astype(f32)
            parts.append(total)
        grad_two = weight_grad(acts, grads, table_two, spread, lane, False, shard, name="grad2")
        conv2_grad = weight_out(grad_two, place)

        d_act_one = roll_to(jnp.stack(parts), z, 0).reshape(rows, wide)
        sigma_one = jax.nn.sigmoid(pre_one)
        dz_one = d_act_one * valid_here * (sigma_one + pre_one * sigma_one * (1.0 - sigma_one))
        shift_one_grad, shift_one_lanes = both_mels(jnp.sum(dz_one, axis=0))
        gain_one_grad, gain_one_lanes = both_mels(jnp.sum(dz_one * normed_one, axis=0))
        d_first = (
            gain_one
            * inv_one
            * (dz_one - (shift_one_lanes + normed_one * gain_one_lanes) / pixel_count)
            * valid_here
        ).astype(bf16)

        grads = []
        total = 0.0
        for k in range(depth):
            grads.append(gather_dp(d_first[k * step : (k + 1) * step], k % 2))
            (out,) = convolve(grads[k], wide_one, [(step, wide_in)], back=True, name="back1")
            out = out.reshape(2, step // 2, wide_in)
            line = pick(out, c).astype(f32) + other_core(pick(out, 1 - c)).astype(f32)
            total = total + (to_z(line.astype(bf16), k).astype(f32) if k else line)
        grad_one = weight_grad([[v] for v in maps_in], grads, table_one, spread, lane_in, True, shard, name="grad1")
        conv1_grad = weight_out(grad_one, place)

        total = total.astype(bf16).reshape(dp, own_rows, wide_in)
        from_dp = [other_dp(pick(total, d ^ r), r) if r else pick(total, d) for r in range(dp)]
        input_grad = []
        for m in range(mels):
            at = slice(m * quarter, (m + 1) * quarter)
            mixed = jnp.concatenate([v[:, at] for v in from_dp], axis=1)
            input_grad.append(dot_transpose(mixed, sort_in).reshape(clip_count, frames, chan_in))
        input_grad = jnp.stack(input_grad, axis=2) * own_valid.astype(f32)

        norm_grads = jnp.stack([gain_one_grad, shift_one_grad, gain_two_grad, shift_two_grad])
        norm_grads = gather_small(norm_grads, d, z, c).reshape(dp * shard, 4, lane)
        norm_grads = jnp.moveaxis(norm_grads, 0, 1).reshape(4, chan_mid)
        return (
            own_logits,
            input_grad,
            conv1_grad,
            norm_grads[0],
            norm_grads[1],
            conv2_grad,
            norm_grads[2],
            norm_grads[3],
            fc1_grad,
            fc1_bias_grad,
            fc2_grad,
            fc2_bias_grad,
        )

    return on_device


def patch_rows(grid_in):
    clip_count, frame_count, mel_count, chan_count = grid_in.shape
    padded = jnp.pad(grid_in, ((0, 0), (1, 1), (1, 1), (0, 0)))
    tap_list = [
        padded[:, shift_t : shift_t + frame_count, shift_m : shift_m + mel_count, :]
        for shift_t in range(3)
        for shift_m in range(3)
    ]
    stacked = jnp.stack(tap_list, axis=3)
    return stacked.reshape(clip_count * frame_count * mel_count, 9 * chan_count)


def fold_rows(grad_rows, clip_count, frame_count, mel_count):
    chan_count = grad_rows.shape[1] // 9
    tap_terms = grad_rows.reshape(clip_count, frame_count, mel_count, 9, chan_count)
    summed = jnp.zeros((clip_count, frame_count + 2, mel_count + 2, chan_count), jnp.float32)
    for tap_index in range(9):
        shift_t = tap_index // 3
        shift_m = tap_index % 3
        summed = summed + jnp.pad(
            tap_terms[:, :, :, tap_index, :],
            ((0, 0), (shift_t, 2 - shift_t), (shift_m, 2 - shift_m), (0, 0)),
        )
    return summed[:, 1 : frame_count + 1, 1 : mel_count + 1, :]


def normalize(values_in, sum_first, sum_square, pixel_count, gain, shift):
    mean_value = sum_first / pixel_count
    inv_std = lax.rsqrt(sum_square / pixel_count - mean_value * mean_value + epsilon)
    normed = (values_in - mean_value) * inv_std
    return (normed, inv_std, normed * gain + shift)


def silu_slope(values_in):
    sigma = jax.nn.sigmoid(values_in)
    return sigma + values_in * sigma * (1.0 - sigma)


def transpose_dot(left, right):
    return lax.dot_general(
        left, right, (((0,), (0,)), ((), ())), preferred_element_type=jnp.float32
    )


def make_valid(clip_lengths, frame_count, mel_count):
    clip_count = clip_lengths.shape[0]
    frame_ids = lax.broadcasted_iota(jnp.int32, (clip_count, frame_count), 1)
    valid_two = (frame_ids < clip_lengths[:, None]).astype(jnp.float32)
    pixel_valid = jnp.broadcast_to(
        valid_two[:, :, None], (clip_count, frame_count, mel_count)
    ).reshape(-1, 1)
    return (valid_two[:, :, None, None], pixel_valid)


def pool_map(act_grid):
    clip_count, frame_count, mel_count, chans = act_grid.shape
    pooled = jnp.mean(
        act_grid.reshape(clip_count, frame_count // 2, 2, mel_count // 2, 2, chans), axis=(2, 4)
    )
    return jnp.mean(pooled, axis=2)


def pooled_slope(d_pooled, pre_two, pixel_valid, mel_count):
    clip_count, half_frames, chans = d_pooled.shape
    d_frames = jnp.repeat(d_pooled, 2, axis=1)[:, :, None, :] / (2.0 * mel_count)
    d_act_two = jnp.broadcast_to(d_frames, (clip_count, 2 * half_frames, mel_count, chans)).reshape(
        -1, chans
    )
    return d_act_two * pixel_valid * silu_slope(pre_two)


def tag_head(
    pooled, clip_lengths, labels, full_fc1, full_fc2, back_fc1, back_fc2, fc1_bias, fc2_bias
):
    clip_count, half_frames, chans = pooled.shape
    half_ids = lax.broadcasted_iota(jnp.int32, (clip_count, half_frames), 1)
    half_len = clip_lengths // 2
    pooled_valid = (half_ids < half_len[:, None]).astype(jnp.float32)[:, :, None]
    half_float = half_len.astype(jnp.float32)[:, None]
    largest = jnp.max(jnp.where(pooled_valid > 0, pooled, -1e30), axis=1, keepdims=True)
    exp_terms = jnp.exp(pooled - largest) * pooled_valid
    exp_sum = jnp.sum(exp_terms, axis=1)
    log_sum = largest[:, 0, :] + jnp.log(exp_sum)
    mean_time = jnp.sum(pooled * pooled_valid, axis=1) / half_float
    embedding = (log_sum + mean_time).astype(jnp.bfloat16)
    hidden = jnp.dot(embedding, full_fc1, preferred_element_type=jnp.float32) + fc1_bias
    gated_low = jax.nn.silu(hidden).astype(jnp.bfloat16)
    class_logits = jnp.dot(gated_low, full_fc2, preferred_element_type=jnp.float32) + fc2_bias
    d_logits = (jax.nn.sigmoid(class_logits) - labels.astype(jnp.float32)).astype(jnp.bfloat16)
    fc2_term = transpose_dot(gated_low, d_logits)
    fc2_bias_term = jnp.sum(d_logits.astype(jnp.float32), axis=0)
    d_gated = jnp.dot(d_logits, back_fc2.T, preferred_element_type=jnp.float32)
    d_hidden = (d_gated * silu_slope(hidden)).astype(jnp.bfloat16)
    fc1_term = transpose_dot(embedding, d_hidden)
    fc1_bias_term = jnp.sum(d_hidden.astype(jnp.float32), axis=0)
    d_embed = jnp.dot(d_hidden, back_fc1.T, preferred_element_type=jnp.float32)
    soft_weights = exp_terms / exp_sum[:, None, :]
    d_pooled = d_embed[:, None, :] * (soft_weights + pooled_valid / half_float[:, :, None])
    return (class_logits, d_pooled, fc1_term, fc2_term, fc1_bias_term, fc2_bias_term)


def on_device(
    clip_maps,
    lengths,
    labels,
    conv1_weight,
    norm1_gain,
    norm1_shift,
    conv2_weight,
    norm2_gain,
    norm2_shift,
    fc1_weight,
    fc1_bias,
    fc2_weight,
    fc2_bias,
):
    clip_count, frame_count, mel_count, chan_in = clip_maps.shape
    chan_mid = norm1_gain.shape[0]
    valid_four, pixel_valid = make_valid(lengths, frame_count, mel_count)
    masked = clip_maps * valid_four.astype(jnp.bfloat16)
    sent = (conv1_weight, conv2_weight, fc1_weight, fc2_weight)
    gathered = (
        lax.all_gather(sent[0], "shard", axis=0, tiled=True),
        lax.all_gather(sent[1], "shard", axis=0, tiled=True),
        lax.all_gather(sent[2], "shard", axis=0, tiled=True),
        lax.all_gather(sent[3], "shard", axis=0, tiled=True),
    )
    full_one, full_two, full_fc1, full_fc2 = gathered
    patch_one = patch_rows(masked)
    first_out = jnp.dot(patch_one, full_one, preferred_element_type=jnp.float32)
    sum_one, square_one, pixel_count = lax.psum(
        (
            jnp.sum(first_out * pixel_valid, axis=0),
            jnp.sum(first_out * first_out * pixel_valid, axis=0),
            jnp.sum(pixel_valid),
        ),
        ("dp", "shard"),
    )
    normed_one, inv_one, pre_one = normalize(
        first_out, sum_one, square_one, pixel_count, norm1_gain, norm1_shift
    )
    act_one = (jax.nn.silu(pre_one) * pixel_valid).astype(jnp.bfloat16)
    patch_two = patch_rows(act_one.reshape(clip_count, frame_count, mel_count, chan_mid))
    second_out = jnp.dot(patch_two, full_two, preferred_element_type=jnp.float32)
    sum_two, square_two = lax.psum(
        (
            jnp.sum(second_out * pixel_valid, axis=0),
            jnp.sum(second_out * second_out * pixel_valid, axis=0),
        ),
        ("dp", "shard"),
    )
    normed_two, inv_two, pre_two = normalize(
        second_out, sum_two, square_two, pixel_count, norm2_gain, norm2_shift
    )
    act_two = (jax.nn.silu(pre_two) * pixel_valid).reshape(
        clip_count, frame_count, mel_count, chan_mid
    )
    pooled_own = pool_map(act_two)
    back_weights = (
        lax.all_gather(sent[0], "shard", axis=0, tiled=True),
        lax.all_gather(sent[1], "shard", axis=0, tiled=True),
        lax.all_gather(sent[2], "shard", axis=0, tiled=True),
        lax.all_gather(sent[3], "shard", axis=0, tiled=True),
    )
    back_one, back_two, back_fc1, back_fc2 = back_weights
    class_logits, d_pooled, fc1_term, fc2_term, fc1_bias_term, fc2_bias_term = tag_head(
        pooled_own, lengths, labels, full_fc1, full_fc2, back_fc1, back_fc2, fc1_bias, fc2_bias
    )
    dz_two = pooled_slope(d_pooled, pre_two, pixel_valid, mel_count)
    shift_two_grad, gain_two_grad, fc1_bias_grad, fc2_bias_grad = lax.psum(
        (
            jnp.sum(dz_two, axis=0),
            jnp.sum(dz_two * normed_two, axis=0),
            fc1_bias_term,
            fc2_bias_term,
        ),
        ("dp", "shard"),
    )
    d_second = (
        norm2_gain
        * inv_two
        * (dz_two - (shift_two_grad + normed_two * gain_two_grad) / pixel_count)
        * pixel_valid
    ).astype(jnp.bfloat16)
    conv2_part = lax.psum_scatter(
        transpose_dot(patch_two, d_second), "shard", scatter_dimension=0, tiled=True
    )
    d_patch_two = jnp.dot(d_second, back_two.T, preferred_element_type=jnp.float32)
    d_act_one = fold_rows(d_patch_two, clip_count, frame_count, mel_count).reshape(-1, chan_mid)
    dz_one = d_act_one * pixel_valid * silu_slope(pre_one)
    shift_one_grad, gain_one_grad = lax.psum(
        (jnp.sum(dz_one, axis=0), jnp.sum(dz_one * normed_one, axis=0)), ("dp", "shard")
    )
    d_first = (
        norm1_gain
        * inv_one
        * (dz_one - (shift_one_grad + normed_one * gain_one_grad) / pixel_count)
        * pixel_valid
    ).astype(jnp.bfloat16)
    conv1_term = transpose_dot(patch_one, d_first)
    d_patch_one = jnp.dot(d_first, back_one.T, preferred_element_type=jnp.float32)
    input_grad = fold_rows(d_patch_one, clip_count, frame_count, mel_count) * valid_four
    conv1_part, fc1_part, fc2_part = (
        lax.psum_scatter(conv1_term, "shard", scatter_dimension=0, tiled=True),
        lax.psum_scatter(fc1_term, "shard", scatter_dimension=0, tiled=True),
        lax.psum_scatter(fc2_term, "shard", scatter_dimension=0, tiled=True),
    )
    conv1_grad, conv2_grad, fc1_grad, fc2_grad = (
        lax.psum(conv1_part.astype(jnp.bfloat16), "dp").astype(jnp.float32),
        lax.psum(conv2_part.astype(jnp.bfloat16), "dp").astype(jnp.float32),
        lax.psum(fc1_part.astype(jnp.bfloat16), "dp").astype(jnp.float32),
        lax.psum(fc2_part.astype(jnp.bfloat16), "dp").astype(jnp.float32),
    )
    return (
        class_logits,
        input_grad,
        conv1_grad,
        gain_one_grad,
        shift_one_grad,
        conv2_grad,
        gain_two_grad,
        shift_two_grad,
        fc1_grad,
        fc1_bias_grad,
        fc2_grad,
        fc2_bias_grad,
    )


def solution(mesh):
    in_specs = (
        P(("dp", "shard"), None, None, None),
        P(("dp", "shard")),
        P(("dp", "shard"), None),
        P("shard", None),
        P(),
        P(),
        P("shard", None),
        P(),
        P(),
        P("shard", None),
        P(),
        P("shard", None),
        P(),
    )
    out_specs = (
        P(("dp", "shard"), None),
        P(("dp", "shard"), None, None, None),
        P("shard", None),
        P(),
        P(),
        P("shard", None),
        P(),
        P(),
        P("shard", None),
        P(),
        P("shard", None),
        P(),
    )
    dp, shard = mesh.shape["dp"], mesh.shape["shard"]
    step = make_device(dp, shard) if (dp, shard) == (4, 8) else on_device
    return jax.shard_map(
        step, mesh=mesh, in_specs=in_specs, out_specs=out_specs, check_vma=False
    )
```

```python
import functools
import math
import jax
import jax.numpy as jnp
from jax import lax
from jax.experimental import pallas as pl
from jax.experimental.pallas import tpu as pltpu
from jax.sharding import PartitionSpec as P
bf16 = jnp.bfloat16
f32 = jnp.float32
epsilon = 1e-05
big_vmem = 56 * 1024 * 1024
VM = pl.BlockSpec(memory_space=pltpu.VMEM)
SM = pl.BlockSpec(memory_space=pltpu.SMEM)
HB = pl.BlockSpec(memory_space=pl.ANY)

def params():
    return pltpu.CompilerParams(vmem_limit_bytes=big_vmem)

def cost(flops, moved):
    return pl.CostEstimate(flops=int(flops), bytes_accessed=int(moved), transcendentals=0)


def split_kernel(shard, place, weight, *refs):
    outs, (own, sem) = refs[:shard], refs[shard:]
    copy = pltpu.make_async_copy(weight.at[:, place[0]], own, sem)
    copy.start()
    copy.wait()
    for step in range(shard):
        column = lax.rem(place[1] - step + shard, shard)
        width = outs[step].shape[2]
        outs[step][...] = own[:, :, pl.ds(pl.multiple_of(column * width, width), width)]


def split_weight(weight, place, dp, shard):
    rows, columns = weight.shape
    part = rows // (9 * dp)
    chunk = jax.ShapeDtypeStruct((9, part, columns // shard), bf16)
    return pl.pallas_call(
        functools.partial(split_kernel, shard),
        out_shape=[chunk] * shard,
        in_specs=[SM, HB],
        out_specs=[VM] * shard,
        scratch_shapes=[pltpu.VMEM((9, part, columns), bf16), pltpu.SemaphoreType.DMA(())],
        compiler_params=params(),
        cost_estimate=cost(0, 4 * rows * columns // dp),
        name="split_weight",
    )(place, weight.reshape(9, dp, part, columns))


def expand_kernel(shard, by_mel, table, *refs):
    pieces, (spread, out, held) = refs[:shard], refs[shard:]
    for step in range(shard):
        held[pl.ds(9 * step, 9)] = pieces[step][...]
    part = held.shape[1]

    for a in range(3):
        taps = [
            jnp.concatenate([held[table[(3 * a + b) * shard + position]] for position in range(shard)], axis=0)
            for b in range(3)
        ]
        for m in range(2):
            pair = jnp.concatenate([taps[m + 1], taps[m]], axis=1)
            wide = jnp.dot(pair, spread[...], preferred_element_type=f32).astype(bf16)
            for position in range(shard):
                rows = wide[position * part : (position + 1) * part]
                if by_mel:
                    out[a, m, position] = rows
                else:
                    out[a, position, pl.ds(m * part, part)] = rows


def expand_weight(pieces, table, spread, by_mel):
    shard = len(pieces)
    _, part, columns = pieces[0].shape
    shape = (3, 2, shard, part, 2 * columns) if by_mel else (3, shard, 2 * part, 2 * columns)
    wide = pl.pallas_call(
        functools.partial(expand_kernel, shard, by_mel),
        out_shape=jax.ShapeDtypeStruct(shape, bf16),
        in_specs=[SM] + [VM] * (shard + 1),
        out_specs=VM,
        scratch_shapes=[pltpu.VMEM((9 * shard, part, columns), bf16)],
        compiler_params=params(),
        cost_estimate=cost(2 * 6 * shard * part * 4 * columns * columns, 30 * shard * part * columns),
        name="expand_weight",
    )(table, *pieces, spread)
    return wide.reshape(3, 2 * shard * part, 2 * columns)


def conv_kernel(count, back, tile, *refs):
    rows_in, taps, outs, (first, last) = refs[:count], refs[count], refs[count + 1 : -2], refs[-2:]
    height = first.shape[0] - 8
    width = first.shape[1]
    first[0:8] = jnp.zeros((8, width), f32)
    last[height:] = jnp.zeros((8, width), f32)
    late, early = (2, 0) if back else (0, 2)
    contract = (((1,), (1,)), ((), ())) if back else (((1,), (0,)), ((), ()))

    def block(ref, at):
        value = ref[at] if len(ref.shape) == 2 else jnp.concatenate(
            [ref[i, at] for i in range(ref.shape[0])], axis=1)
        return value

    def one(i, carry):
        at = pl.ds(pl.multiple_of(i * tile, tile), tile)
        rows = jnp.concatenate([block(ref, at) for ref in rows_in], axis=1)
        first[pl.ds(pl.multiple_of(i * tile + 8, 8), tile)] = lax.dot_general(
            rows, taps[late], contract, preferred_element_type=f32)
        last[at] = lax.dot_general(rows, taps[early], contract, preferred_element_type=f32)
        return carry

    lax.fori_loop(0, height // tile, one, 0)

    def two(i, carry):
        start = pl.multiple_of(i * tile, tile)
        at = pl.ds(start, tile)
        rows = jnp.concatenate([block(ref, at) for ref in rows_in], axis=1)
        total = lax.dot_general(rows, taps[1], contract, preferred_element_type=f32)
        before = first[pl.ds(start, tile + 8)]
        after = last[pl.ds(start, tile + 8)]
        total = total + before[7 : tile + 7] + after[1 : tile + 1]
        total = total.astype(bf16)
        column = 0
        for out in outs:
            if len(out.shape) == 2:
                step = out.shape[1]
                out[at] = total[:, column : column + step]
                column += step
            else:
                step = out.shape[2]
                for k in range(out.shape[0]):
                    out[k, at] = total[:, column : column + step]
                    column += step
        return carry

    lax.fori_loop(0, height // tile, two, 0)


def whole(shape):
    return pl.BlockSpec(shape, lambda i: (0,) * len(shape))


def convolve(rows_in, taps, out_shapes, back=False, chunk=None, name="convolve"):
    height = out_shapes[0][-2]
    width = taps.shape[1] if back else taps.shape[2]
    specs = [whole(v.shape) for v in rows_in]
    if chunk is not None:
        count, _, lanes = rows_in[0].shape
        specs = [pl.BlockSpec((count, height, lanes), lambda i: (0, chunk, 0))]
    moved = 2 * (taps.size + sum(math.prod(s) for s in out_shapes)) + 2 * height * taps.shape[2 if back else 1]
    return pl.pallas_call(
        functools.partial(conv_kernel, len(rows_in), back, height // 2),
        grid=(1,),
        out_shape=[jax.ShapeDtypeStruct(s, bf16) for s in out_shapes],
        in_specs=specs + [whole(taps.shape)],
        out_specs=[whole(s) for s in out_shapes],
        scratch_shapes=[pltpu.VMEM((height + 8, width), f32)] * 2,
        compiler_params=params(),
        cost_estimate=cost(2 * height * taps.size, moved),
        name=name,
    )(*rows_in, taps)


def grad_kernel(chunks, x_count, g_count, first, count, by_mel, shard, tile, table, *refs):
    n, m = chunks * x_count, chunks * g_count
    x_refs, g_refs = refs[:n], refs[n : n + m]
    spread = refs[n + m]
    out, total, moved, done, sem = refs[-5:]
    height = g_refs[0].shape[0]
    half = spread.shape[0] // 2
    width = 2 * half
    part = out.shape[1]
    total[...] = jnp.zeros_like(total)
    moved[0:8] = jnp.zeros((8, width), f32)
    moved[height + 8 :] = jnp.zeros((8, width), f32)
    for chunk in range(chunks):
        xs = x_refs[chunk * x_count : (chunk + 1) * x_count]
        gs = g_refs[chunk * g_count : (chunk + 1) * g_count]
        column = 0
        for g in gs:
            moved[8 : height + 8, column : column + g.shape[1]] = g[...].astype(f32)
            column += g.shape[1]

        def one(i, carry, xs=xs):
            start = pl.multiple_of(i * tile, tile)
            at = pl.ds(start, tile)
            if by_mel:
                rows = jnp.concatenate(
                    [xs[0][at, (mel * shard + first) * part : (mel * shard + first + count) * part]
                     for mel in range(2)], axis=1)
            else:
                rows = jnp.concatenate([xs[0][i, at] for i in range(count)], axis=1)
            around = moved[pl.ds(start, tile + 16)]
            three = jnp.concatenate(
                [around[9 - a : 9 - a + tile].astype(bf16) for a in range(3)], axis=1)
            total[...] += lax.dot_general(
                rows, three, (((0,), (0,)), ((), ())), preferred_element_type=f32)
            return carry

        lax.fori_loop(0, height // tile, one, 0)

    def fold(position, carry):
        for a in range(3):
            if by_mel:
                at = [pl.multiple_of((mel * count + position) * part, part) for mel in range(2)]
            else:
                at = [pl.multiple_of((2 * position + mel) * part, part) for mel in range(2)]
            top, bottom = [
                lax.dot_general(
                    total[pl.ds(start, part), a * width : (a + 1) * width].astype(bf16),
                    spread[...], (((1,), (1,)), ((), ())), preferred_element_type=f32)
                for start in at
            ]
            taps = [top[:, half:], top[:, :half] + bottom[:, half:], bottom[:, :half]]
            for b in range(3):
                done[(3 * a + b) * count + position] = taps[b].astype(bf16)
        return carry

    lax.fori_loop(0, count, fold, 0)
    copies = [
        pltpu.make_async_copy(
            done.at[tap * count + position], out.at[table[tap * shard + first + position]],
            sem.at[tap * count + position])
        for tap in range(9) for position in range(count)
    ]
    for copy in copies:
        copy.start()
    for copy in copies:
        copy.wait()


def weight_grad(x_chunks, g_chunks, table, spread, part, by_mel, shard, first, count, before=None, name="weight_grad"):
    xs = [v for v, _ in x_chunks]
    gs = [g for chunk in g_chunks for g in chunk]
    height = gs[0].shape[0]
    wide = spread.shape[0]
    deep = 2 * count * part
    flops = 2 * len(x_chunks) * height * deep * wide * 3
    inputs = [table] + xs + gs + [spread]
    specs = [pl.BlockSpec(memory_space=pltpu.SMEM)]
    for v, row in x_chunks:
        if by_mel:
            specs.append(pl.BlockSpec((height, v.shape[1]), lambda i, row=row: (row, 0)))
        else:
            specs.append(pl.BlockSpec((count, height, v.shape[2]), lambda i, row=row: (first // count, row, 0)))
    specs += [whole(v.shape) for v in gs + [spread]]
    if before is not None:
        inputs, specs = inputs + [before], specs + [HB]
    return pl.pallas_call(
        functools.partial(grad_kernel, len(x_chunks), 1, len(g_chunks[0]), first, count, by_mel, shard, height),
        grid=(1,),
        out_shape=jax.ShapeDtypeStruct((9 * shard, part, wide // 2), bf16),
        in_specs=specs,
        out_specs=HB,
        input_output_aliases={} if before is None else {len(inputs) - 1: 0},
        scratch_shapes=[
            pltpu.VMEM((deep, 3 * wide), f32),
            pltpu.VMEM((height + 16, wide), f32),
            pltpu.VMEM((9 * count, part, wide // 2), bf16),
            pltpu.SemaphoreType.DMA((9 * count,)),
        ],
        compiler_params=params(),
        cost_estimate=cost(flops, 2 * len(xs) * height * deep + sum(2 * v.size for v in gs) + 9 * count * part * wide),
        name=name,
    )(*inputs)


def join_kernel(dp, shard, place, *refs):
    parts, out = refs[:-1], refs[-1]
    half = shard // 2
    width = parts[0].shape[3]
    for source in range(dp):
        group = lax.bitwise_xor(place[0], source)
        for step in range(shard):
            column = lax.rem(place[1] + step, shard)
            value = parts[2 * source + step // half][step % half, 0]
            out[0, group, :, pl.ds(pl.multiple_of(column * width, width), width)] = value.astype(f32)


def join_grad(parts, place, dp, shard):
    half, _, part, width = parts[0].shape
    block = pl.BlockSpec((half, 1, part, width), lambda i: (0, i, 0, 0))
    out = pl.pallas_call(
        functools.partial(join_kernel, dp, shard),
        grid=(9,),
        out_shape=jax.ShapeDtypeStruct((9, dp, part, shard * width), f32),
        in_specs=[SM] + [block] * len(parts),
        out_specs=pl.BlockSpec((1, dp, part, shard * width), lambda i: (i, 0, 0, 0)),
        compiler_params=params(),
        cost_estimate=cost(0, 6 * 9 * dp * part * shard * width),
        name="join_grad",
    )(place, *parts)
    return out.reshape(9 * dp * part, shard * width)


def valid_rows(frames, lanes, length):
    return (lax.broadcasted_iota(jnp.int32, (frames, lanes), 0) < length).astype(f32)


def pack_maps_kernel(frames, order, offset, length, maps, *refs):
    outs, (mask, held, packed, flags) = refs[:-4], refs[-4:]
    step = outs[0].shape[0]
    held[...] = maps[...].astype(f32)
    packed[...] = jnp.zeros_like(packed)
    flags[...] = jnp.zeros_like(flags)

    def one(k, carry):
        source = pl.ds(pl.multiple_of(order[k] * frames, frames), frames)
        at = pl.ds(pl.multiple_of(offset[k], 8), frames)
        packed[at] = held[source]
        flags[at] = valid_rows(frames, flags.shape[1], length[k])
        return carry

    lax.fori_loop(0, order.shape[0], one, 0)
    for p, out in enumerate(outs):
        out[...] = packed[p * step : (p + 1) * step].astype(bf16)
    mask[...] = flags[: mask.shape[0]]


def pack_maps(maps, packing, frames, height, chunks):
    rows, lanes = maps.shape
    *parts, mask = pl.pallas_call(
        functools.partial(pack_maps_kernel, frames),
        out_shape=[jax.ShapeDtypeStruct((height // chunks, lanes), bf16)] * chunks
        + [jax.ShapeDtypeStruct((height, 128), f32)],
        in_specs=[SM] * 3 + [VM],
        out_specs=[VM] * (chunks + 1),
        scratch_shapes=[
            pltpu.VMEM((rows, lanes), f32),
            pltpu.VMEM((height + frames, lanes), f32),
            pltpu.VMEM((height + frames, 128), f32),
        ],
        compiler_params=params(),
        cost_estimate=cost(0, 8 * rows * lanes),
        name="pack_maps",
    )(*packing, maps)
    return parts, mask


def unpack_maps_kernel(frames, order, offset, *refs):
    parts, (out, held, spaced) = refs[:-3], refs[-3:]
    step = parts[0].shape[0]
    for p, part in enumerate(parts):
        held[p * step : (p + 1) * step] = part[...].astype(f32)
    held[len(parts) * step :] = jnp.zeros((frames, held.shape[1]), f32)

    def one(k, carry):
        target = pl.ds(pl.multiple_of(order[k] * frames, frames), frames)
        spaced[target] = held[pl.ds(pl.multiple_of(offset[k], 8), frames)]
        return carry

    lax.fori_loop(0, order.shape[0], one, 0)
    out[...] = spaced[...].astype(bf16)


def unpack_maps(parts, packing, frames, rows):
    step, lanes = parts[0].shape
    return pl.pallas_call(
        functools.partial(unpack_maps_kernel, frames),
        out_shape=jax.ShapeDtypeStruct((rows, lanes), bf16),
        in_specs=[SM] * 2 + [VM] * len(parts),
        out_specs=VM,
        scratch_shapes=[
            pltpu.VMEM((len(parts) * step + frames, lanes), f32),
            pltpu.VMEM((rows, lanes), f32),
        ],
        compiler_params=params(),
        cost_estimate=cost(0, 8 * rows * lanes),
        name="unpack_maps",
    )(*packing[:2], *parts)


def unpack_rows_kernel(frames, order, offset, length, value, out, held):
    height = value.shape[0]
    held[:height] = value[...]
    held[height:] = jnp.zeros((frames, held.shape[1]), f32)

    def one(k, carry):
        target = pl.ds(pl.multiple_of(order[k] * frames, frames), frames)
        rows = held[pl.ds(pl.multiple_of(offset[k], 8), frames)]
        out[target] = rows * valid_rows(frames, rows.shape[1], length[k])
        return carry

    lax.fori_loop(0, order.shape[0], one, 0)


def pack_rows_kernel(frames, order, offset, length, value, out, held):
    held[...] = jnp.zeros_like(held)

    def one(k, carry):
        rows = value[pl.ds(pl.multiple_of(order[k] * frames, frames), frames)]
        target = pl.ds(pl.multiple_of(offset[k], 8), frames)
        held[target] = rows * valid_rows(frames, rows.shape[1], length[k])
        return carry

    lax.fori_loop(0, order.shape[0], one, 0)
    out[...] = held[: out.shape[0]]


def move_rows(value, packing, frames, height, packed):
    lanes = value.shape[1]
    held = height if packed else value.shape[0]
    return pl.pallas_call(
        functools.partial(pack_rows_kernel if packed else unpack_rows_kernel, frames),
        out_shape=jax.ShapeDtypeStruct((height, lanes), f32),
        in_specs=[SM] * 3 + [VM],
        out_specs=VM,
        scratch_shapes=[pltpu.VMEM((held + frames, lanes), f32)],
        compiler_params=params(),
        cost_estimate=cost(0, 8 * height * lanes),
        name="pack_rows" if packed else "unpack_rows",
    )(*packing, value)


under_way_w, under_way_xy, chunks = 7, 3, 4


def roll_to(stacked, start, axis):
    size = stacked.shape[axis]
    doubled = jnp.concatenate([stacked, stacked], axis=axis)
    return lax.dynamic_slice_in_dim(doubled, start, size, axis=axis)


def pick(stacked, index):
    return lax.dynamic_index_in_dim(stacked, index, 0, keepdims=False)


def dot(left, right):
    return jnp.dot(left, right, preferred_element_type=f32)


def dot_transpose(left, right):
    return lax.dot_general(left, right, (((1,), (1,)), ((), ())), preferred_element_type=f32)


def both_mels(sums):
    half = sums.shape[0] // 2
    total = sums[:half] + sums[half:]
    return total, jnp.concatenate([total, total])


def norm_of(values_in, valid, pixel_count):
    _, sum_first = both_mels(jnp.sum(values_in * valid, axis=0))
    _, sum_square = both_mels(jnp.sum(values_in * values_in * valid, axis=0))
    mean_value = sum_first / pixel_count
    inv_std = lax.rsqrt(sum_square / pixel_count - mean_value * mean_value + epsilon)
    return (values_in - mean_value) * inv_std, inv_std


def make_device(dp, shard):
    depth = shard // 2
    lanes = {}

    def after(value, *earlier):
        return lax.optimization_barrier((value,) + earlier)[0]

    def queued(lane, value, send, most=2):
        sent = lanes.setdefault(lane, [])
        if len(sent) >= most:
            value = after(value, sent[-most])
        sent.append(send(value))
        return sent[-1]

    def permute(value, axis, size, move):
        return lax.ppermute(value, axis, [(i, move(i) % size) for i in range(size)])

    def from_z(value, k):
        return queued("z", value, lambda v: permute(v, "shard", shard, lambda i: i - 2 * k), under_way_z)

    def to_z(value, k):
        return queued("z", value, lambda v: permute(v, "shard", shard, lambda i: i + 2 * k), under_way_z)

    def from_shard(value, k, *earlier):
        value = after(value, *earlier)
        return queued("z", value, lambda v: permute(v, "shard", shard, lambda i: i - k), under_way_w)

    def other_core(value):
        return permute(value, "shard", shard, lambda i: i ^ 1)

    def other_dp(value, r):
        return queued("xy", value, lambda v: permute(v, "dp", dp, lambda i: i ^ r), under_way_xy)

    def gather_dp(value, order):
        one, two = other_dp(value, 1), other_dp(value, 2)
        three = other_dp(one, 2) if order == 0 else other_dp(two, 1)
        return [value, one, two, three]

    def gather_chunks(values):
        near = []
        for p, value in enumerate(values):
            near.append([value, other_dp(value, 1), other_dp(value, 2)])
            if p:
                near[p - 1].append(other_dp(near[p - 1][1 + (p - 1) % 2], 2 - (p - 1) % 2))
        near[-1].append(other_dp(near[-1][1 + p % 2], 2 - p % 2))
        return near

    def tied(values, *earlier):
        return [after(values[0], *earlier)] + list(values[1:])

    def unswap(parts, d):
        low = [jnp.where(d % 2 == 1, parts[r ^ 1], parts[r]) for r in range(dp)]
        return [jnp.where(d // 2 == 1, low[r ^ 2], low[r]) for r in range(dp)]

    far = [k for k in range(1, depth) if 2 * k != depth] + [depth // 2]

    def core_order(mine, theirs, c):
        return [jnp.where(c == 0, mine, theirs), jnp.where(c == 0, theirs, mine)]

    def gather_small(value, d, z, c):
        near = [permute(value, "dp", dp, lambda i, r=r: i ^ r) for r in range(1, dp)]
        square = jnp.stack(unswap([value] + near, d))
        far = [permute(square, "shard", shard, lambda i, k=k: i - 2 * k) for k in range(1, depth)]
        line = roll_to(jnp.stack([square] + far), (depth - z) % depth, 0)
        return jnp.stack(core_order(line, other_core(line), c), axis=1)

    def weight_in(pieces, done=()):
        done = dict(done)
        return [pieces[0]] + [from_shard(pieces[k], k, *done.get(k, ())) for k in range(1, shard)]

    def send_grad(grad, done=()):
        done = dict(done)
        pieces = grad.reshape((shard, 9) + grad.shape[1:])
        return [pieces[0]] + [from_shard(pieces[shard - k], k, *done.get(k, ())) for k in range(1, shard)]

    def near_grad(parts):
        half = shard // 2
        return [gather_dp(jnp.stack(parts[:half]), 0), gather_dp(jnp.stack(parts[half:]), 1)]

    def on_device(
        clip_maps,
        lengths,
        labels,
        conv1_weight,
        norm1_gain,
        norm1_shift,
        conv2_weight,
        norm2_gain,
        norm2_shift,
        fc1_weight,
        fc1_bias,
        fc2_weight,
        fc2_bias,
    ):
        lanes.clear()
        d, s = lax.axis_index("dp"), lax.axis_index("shard")
        z, c = s // 2, s % 2
        place = jnp.stack([d, s]).astype(jnp.int32)
        clip_count, frames, mels, chan_in = clip_maps.shape
        chan_mid = norm1_gain.shape[0]
        classes = labels.shape[1]
        clips = clip_count * dp * shard
        rows = clips * frames
        own_rows = clip_count * frames
        lane = chan_mid // (dp * shard)
        lane_in = chan_in // (dp * shard)
        wide = mels * lane
        quarter = shard * lane_in
        wide_in = mels * quarter

        position = lax.broadcasted_iota(jnp.int32, (9, shard), 1)
        tap = lax.broadcasted_iota(jnp.int32, (9, shard), 0)

        def table_of(block):
            group = tap * shard + block
            return (((group // 9 - s + shard) % shard) * 9 + group % 9).reshape(9 * shard).astype(jnp.int32)

        table = table_of(position)

        from_row = lax.broadcasted_iota(jnp.int32, (dp * wide, dp * wide), 0)
        to_lane = lax.broadcasted_iota(jnp.int32, (dp * wide, dp * wide), 1)
        spread = (
            (from_row // (dp * lane) == to_lane // lane % mels)
            & (from_row // lane % dp == (d ^ (to_lane // wide)))
            & (from_row % lane == to_lane % lane)
        ).astype(bf16)
        from_row = lax.broadcasted_iota(jnp.int32, (chan_in, chan_in), 0)
        to_lane = lax.broadcasted_iota(jnp.int32, (chan_in, chan_in), 1)
        sort_in = (
            (from_row // (dp * lane_in) == to_lane // lane_in % shard)
            & (from_row // lane_in % dp == (d ^ (to_lane // quarter)))
            & (from_row % lane_in == to_lane % lane_in)
        ).astype(bf16)

        pieces_one = weight_in(split_weight(conv1_weight, place, dp, shard))
        own_frames = lax.broadcasted_iota(jnp.int32, (clip_count, frames), 1)
        own_valid = (own_frames < lengths[:, None])[:, :, None, None]
        clip_maps = after(clip_maps, pieces_one[0])
        masked = clip_maps * own_valid.astype(bf16)
        sorted_in = [dot(masked[:, :, m].reshape(own_rows, chan_in), sort_in).astype(bf16) for m in range(mels)]
        from_dp = []
        for r in range(dp):
            at = slice(r * quarter, (r + 1) * quarter)
            part = jnp.concatenate([v[:, at] for v in sorted_in], axis=1)
            from_dp.append(other_dp(part, r) if r else part)
        group = jnp.concatenate(unswap(from_dp, d), axis=0)
        all_maps = lax.all_gather(group, "shard", tiled=True)
        wide_one = expand_weight(pieces_one, table, spread, True)
        split_two = split_weight(after(conv2_weight, from_dp[1]), place, dp, shard)

        all_lengths = gather_small(lengths, d, z, c).reshape(clips)
        kinds = jnp.stack([all_lengths > frames // 2, (all_lengths > frames // 4) & (all_lengths <= frames // 2), all_lengths <= frames // 4])
        kinds = kinds.astype(jnp.int32)
        taken = jnp.array([frames, frames // 2, frames // 4], jnp.int32)[:, None]
        before = lax.broadcasted_iota(jnp.int32, (clips, clips), 0) < lax.broadcasted_iota(jnp.int32, (clips, clips), 1)
        among = jnp.sum(kinds[:, :, None] * before.astype(jnp.int32)[None], axis=1)
        number = jnp.sum(kinds, axis=1, keepdims=True)
        first_rank = jnp.concatenate([jnp.zeros((1, 1), jnp.int32), number[:1], number[:1] + number[1:2]])
        used = number * taken
        first_row = jnp.concatenate([jnp.zeros((1, 1), jnp.int32), used[:1], used[:1] + used[1:2]])
        rank = jnp.sum(kinds * (first_rank + among), axis=0)
        start = jnp.sum(kinds * (first_row + among * taken), axis=0)
        ranked = (rank[None, :] == lax.broadcasted_iota(jnp.int32, (clips, clips), 0)).astype(jnp.int32)
        clip_ids = lax.broadcasted_iota(jnp.int32, (clips,), 0)
        packing = [jnp.sum(ranked * v[None, :], axis=1) for v in (clip_ids, start, all_lengths)]
        pixel_count = (jnp.sum(all_lengths) * mels).astype(f32)

        def after_maps(height):
            lanes.clear()
            step, half = height // chunks, height // 2
            def scatter_dp(outs):
                total = outs[0].astype(f32)
                for r in range(1, dp):
                    total = total + other_dp(outs[r], r).astype(f32)
                return total

            maps_in, valid = pack_maps(all_maps, packing, frames, height, chunks)
            pieces_two = weight_in(split_two)
            parts = []
            for p in range(chunks):
                value = after(maps_in[p], *[(), (), (), pieces_two[1:2]][p])
                outs = convolve([value], wide_one, [(step, wide)] * dp, name="conv1")
                parts.append(scatter_dp(outs))
            parts = tied(parts, *pieces_two[2:4])
            first_out = jnp.concatenate(parts, axis=0)

            wide_two = expand_weight(pieces_two, table, spread, False)

            own_start = (s * dp + d) * lane

            def own_channels(vector):
                own = lax.dynamic_slice_in_dim(vector, own_start, lane)
                return jnp.concatenate([own] * mels)

            gain_one, shift_one = own_channels(norm1_gain), own_channels(norm1_shift)
            gain_two, shift_two = own_channels(norm2_gain), own_channels(norm2_shift)

            normed_one, inv_one = norm_of(first_out, valid, pixel_count)
            pre_one = normed_one * gain_one + shift_one
            act_one = (jax.nn.silu(pre_one) * valid).astype(bf16)
            acts = [
                lax.all_gather(after(act_one[:half], *pieces_two[4:6]), "shard"),
                lax.all_gather(after(act_one[half:], *pieces_two[6:], wide_two), "shard"),
            ]
            pad = -classes % 128
            some_labels = jnp.pad(labels.astype(bf16), ((0, 0), (0, pad)))
            some_labels = after(some_labels, act_one)
            all_labels = gather_small(some_labels, d, z, c)
            own_fc2 = lax.dynamic_slice_in_dim(jnp.pad(fc2_weight, ((0, 0), (0, pad))), d * lane, lane, axis=0)
            far = [permute(after(own_fc2, act_one), "shard", shard, lambda i, k=k: i - 2 * k) for k in range(1, depth)]
            line = roll_to(jnp.stack([own_fc2] + far), (depth - z) % depth, 0)
            near = [permute(line, "dp", dp, lambda i, r=r: i ^ r) for r in range(1, dp)]
            square = jnp.stack(unswap([line] + near, d), axis=1)
            full_fc2 = jnp.stack(core_order(square, other_core(square), c), axis=1)
            full_fc2 = full_fc2.reshape(chan_mid, classes + pad)[:, :classes]
            all_labels = all_labels.reshape(clips, classes + pad)[:, :classes].astype(f32)
            fc_rows = fc1_weight.shape[0]
            full_fc1 = lax.all_gather(after(fc1_weight, act_one), "shard", tiled=True)
            parts, outs = [], []
            for p in range(chunks):
                value = after(acts[p // 2], *outs[:1])
                if p >= 2:
                    value = after(value, parts[p - 2], *((all_labels, full_fc2) if p == 2 else ()))
                outs = convolve([value], wide_two, [(step, wide)] * dp, chunk=p % 2, name="conv2")
                parts.append(scatter_dp(outs))
            second_out = jnp.concatenate(parts, axis=0)
            normed_two, inv_two = norm_of(second_out, valid, pixel_count)
            pre_two = normed_two * gain_two + shift_two
            sigma_two = jax.nn.sigmoid(pre_two)
            act_two = pre_two * sigma_two * valid
            slope_two = (sigma_two + act_two * (1.0 - sigma_two)) * valid

            halves = frames // 2
            act_two = move_rows(act_two, packing, frames, rows, False)
            pooled = jnp.sum(act_two.reshape(clips, halves, 2, wide), axis=2)
            pooled = (pooled[:, :, :lane] + pooled[:, :, lane:]) / (2.0 * mels)
            half_len = all_lengths // 2
            half_ids = lax.broadcasted_iota(jnp.int32, (clips, halves), 1)
            pooled_valid = (half_ids < half_len[:, None]).astype(f32)[:, :, None]
            half_float = half_len.astype(f32)[:, None]
            largest = jnp.max(jnp.where(pooled_valid > 0, pooled, -1e30), axis=1, keepdims=True)
            exp_terms = jnp.exp(pooled - largest) * pooled_valid
            exp_sum = jnp.sum(exp_terms, axis=1)
            log_sum = largest[:, 0, :] + jnp.log(exp_sum)
            mean_time = jnp.sum(pooled * pooled_valid, axis=1) / half_float
            own_embedding = (log_sum + mean_time).astype(bf16)
            embedding = gather_small(own_embedding.T, d, z, c).reshape(chan_mid, clips)
            own_columns = lax.dynamic_slice_in_dim(embedding, s * fc_rows, fc_rows, axis=0)
            embedding = embedding.T
            hidden = dot(embedding, full_fc1) + fc1_bias
            sigma = jax.nn.sigmoid(hidden)
            gated = (hidden * sigma).astype(bf16)
            logits = dot(gated, full_fc2) + fc2_bias
            d_logits = (jax.nn.sigmoid(logits) - all_labels).astype(bf16)
            d_gated = dot_transpose(d_logits, full_fc2)
            d_hidden = (d_gated * (sigma + hidden * sigma * (1.0 - sigma))).astype(bf16)
            own_fc1 = lax.dynamic_slice_in_dim(fc1_weight, d * lane, lane, axis=0)
            d_embed = dot_transpose(d_hidden, own_fc1)
            soft = exp_terms / exp_sum[:, None, :]
            d_pooled = d_embed[:, None, :] * (soft + pooled_valid / half_float[:, :, None])

            fc1_grad = dot(own_columns, d_hidden)
            own_columns = lax.dynamic_slice_in_dim(gated, s * fc_rows, fc_rows, axis=1)
            fc2_grad = dot(own_columns.T, d_logits)
            fc1_bias_grad = jnp.sum(d_hidden.astype(f32), axis=0)
            fc2_bias_grad = jnp.sum(d_logits.astype(f32), axis=0)
            own_clips = (s * dp + d) * clip_count
            own_logits = lax.dynamic_slice_in_dim(logits, own_clips, clip_count, axis=0)

            d_frames = jnp.concatenate([d_pooled, d_pooled], axis=2) / (2.0 * mels)
            d_frames = jnp.broadcast_to(d_frames[:, :, None, :], (clips, halves, 2, wide))
            dz_two = move_rows(d_frames.reshape(rows, wide), packing, frames, height, True) * slope_two
            shift_two_grad, shift_two_lanes = both_mels(jnp.sum(dz_two, axis=0))
            gain_two_grad, gain_two_lanes = both_mels(jnp.sum(dz_two * normed_two, axis=0))
            d_second = (
                gain_two
                * inv_two
                * (dz_two - (shift_two_lanes + normed_two * gain_two_lanes) / pixel_count)
                * valid
            ).astype(bf16)

            grads_two = gather_chunks(list(d_second.reshape(chunks, step, wide)))
            parts, outs = [], []
            for p in range(chunks):
                ready = tied(grads_two[p], *outs[-1:], *(grads_two[p + 1][1:3] if p + 1 < chunks else ()))
                outs += convolve(ready, wide_two, [(shard, step, wide)], back=True, name="back2")
                if p % 2:
                    out = jnp.concatenate(outs[-2:], axis=1)
                    parts.append(lax.psum_scatter(out, "shard", scatter_dimension=0))

            grad_two = None
            count = shard // 4
            act_chunks = [(acts[p // 2], p % 2) for p in range(chunks)]
            for first in range(0, shard, count):
                ready = [tied(grads_two[0], outs[-1])] + grads_two[1:]
                grad_two = weight_grad(
                    act_chunks, ready, table, spread, lane, False, shard, first, count, grad_two, name="grad2",
                )
            sent_two = send_grad(grad_two)
            parts = tied(parts, grad_two, *sent_two[1:3])

            d_act_one = jnp.concatenate(parts, axis=0).astype(f32)
            sigma_one = jax.nn.sigmoid(pre_one)
            dz_one = d_act_one * valid * (sigma_one + pre_one * sigma_one * (1.0 - sigma_one))
            shift_one_grad, shift_one_lanes = both_mels(jnp.sum(dz_one, axis=0))
            gain_one_grad, gain_one_lanes = both_mels(jnp.sum(dz_one * normed_one, axis=0))
            d_first = (
                gain_one
                * inv_one
                * (dz_one - (shift_one_lanes + normed_one * gain_one_lanes) / pixel_count)
                * valid
            ).astype(bf16)
            values = list(d_first.reshape(chunks, step, wide))
            norm_grads = jnp.stack([gain_one_grad, shift_one_grad, gain_two_grad, shift_two_grad])
            norm_grads = gather_small(norm_grads, d, z, c)
            grads_one = gather_chunks(values)
            outs = []
            for p in range(chunks):
                ready = tied(grads_one[p], *outs[-1:], *(grads_one[p + 1][1:3] if p + 1 < chunks else ()))
                ready = tied(ready, *[(), (norm_grads,), (), ()][p])
                outs += convolve(ready, wide_one, [(step, wide_in)], back=True, name="back1")
            near_two = near_grad([after(v, grads_one[-1][3]) for v in sent_two])

            grad_one = None
            count = shard // 2
            for first in range(0, shard, count):
                ready = [tied(grads_one[0], outs[-1], *(near_two[0][1:3] if first else ()))] + grads_one[1:]
                grad_one = weight_grad(
                    [(v, 0) for v in maps_in], ready, table, spread, lane_in, True, shard, first, count, grad_one, name="grad1",
                )
            d_in = unpack_maps(outs, packing, frames, rows).reshape(shard, rows // shard, wide_in)
            total = lax.psum_scatter(d_in, "shard", scatter_dimension=0)
            sent_one = send_grad(grad_one, {1: near_two[0][1:3], 4: near_two[1][1:3]})
            conv2_grad = join_grad([h for pair in zip(*near_two) for h in pair], place, dp, shard)
            total = total.reshape(dp, own_rows, wide_in)
            from_dp = [other_dp(pick(total, d ^ r), r) if r else pick(total, d) for r in range(dp)]
            near_one = near_grad(sent_one)
            conv1_grad = join_grad([h for pair in zip(*near_one) for h in pair], place, dp, shard)

            norm_grads = norm_grads.reshape(dp * shard, 4, lane)
            norm_grads = jnp.moveaxis(norm_grads, 0, 1).reshape(4, chan_mid)

            input_grad = []
            for m in range(mels):
                at = slice(m * quarter, (m + 1) * quarter)
                mixed = jnp.concatenate([v[:, at] for v in from_dp], axis=1)
                input_grad.append(dot_transpose(mixed, sort_in).reshape(clip_count, frames, chan_in))
            input_grad = jnp.stack(input_grad, axis=2) * own_valid.astype(f32)

            return (
                own_logits,
                input_grad,
                conv1_grad,
                norm_grads[0],
                norm_grads[1],
                conv2_grad,
                norm_grads[2],
                norm_grads[3],
                fc1_grad,
                fc1_bias_grad,
                fc2_grad,
                fc2_bias_grad,
            )

        def rest(height):
            def run():
                return after_maps(height)

            return run

        few = rows * 21 // 32
        assert few % (32 * chunks) == 0
        return lax.cond(jnp.sum(used) <= few, rest(few), rest(rows))

    return on_device


def patch_rows(grid_in):
    clip_count, frame_count, mel_count, chan_count = grid_in.shape
    padded = jnp.pad(grid_in, ((0, 0), (1, 1), (1, 1), (0, 0)))
    tap_list = [
        padded[:, shift_t : shift_t + frame_count, shift_m : shift_m + mel_count, :]
        for shift_t in range(3)
        for shift_m in range(3)
    ]
    stacked = jnp.stack(tap_list, axis=3)
    return stacked.reshape(clip_count * frame_count * mel_count, 9 * chan_count)


def fold_rows(grad_rows, clip_count, frame_count, mel_count):
    chan_count = grad_rows.shape[1] // 9
    tap_terms = grad_rows.reshape(clip_count, frame_count, mel_count, 9, chan_count)
    summed = jnp.zeros((clip_count, frame_count + 2, mel_count + 2, chan_count), jnp.float32)
    for tap_index in range(9):
        shift_t = tap_index // 3
        shift_m = tap_index % 3
        summed = summed + jnp.pad(
            tap_terms[:, :, :, tap_index, :],
            ((0, 0), (shift_t, 2 - shift_t), (shift_m, 2 - shift_m), (0, 0)),
        )
    return summed[:, 1 : frame_count + 1, 1 : mel_count + 1, :]


def normalize(values_in, sum_first, sum_square, pixel_count, gain, shift):
    mean_value = sum_first / pixel_count
    inv_std = lax.rsqrt(sum_square / pixel_count - mean_value * mean_value + epsilon)
    normed = (values_in - mean_value) * inv_std
    return (normed, inv_std, normed * gain + shift)


def silu_slope(values_in):
    sigma = jax.nn.sigmoid(values_in)
    return sigma + values_in * sigma * (1.0 - sigma)


def transpose_dot(left, right):
    return lax.dot_general(
        left, right, (((0,), (0,)), ((), ())), preferred_element_type=jnp.float32
    )


def make_valid(clip_lengths, frame_count, mel_count):
    clip_count = clip_lengths.shape[0]
    frame_ids = lax.broadcasted_iota(jnp.int32, (clip_count, frame_count), 1)
    valid_two = (frame_ids < clip_lengths[:, None]).astype(jnp.float32)
    pixel_valid = jnp.broadcast_to(
        valid_two[:, :, None], (clip_count, frame_count, mel_count)
    ).reshape(-1, 1)
    return (valid_two[:, :, None, None], pixel_valid)


def pool_map(act_grid):
    clip_count, frame_count, mel_count, chans = act_grid.shape
    pooled = jnp.mean(
        act_grid.reshape(clip_count, frame_count // 2, 2, mel_count // 2, 2, chans), axis=(2, 4)
    )
    return jnp.mean(pooled, axis=2)


def pooled_slope(d_pooled, pre_two, pixel_valid, mel_count):
    clip_count, half_frames, chans = d_pooled.shape
    d_frames = jnp.repeat(d_pooled, 2, axis=1)[:, :, None, :] / (2.0 * mel_count)
    d_act_two = jnp.broadcast_to(d_frames, (clip_count, 2 * half_frames, mel_count, chans)).reshape(
        -1, chans
    )
    return d_act_two * pixel_valid * silu_slope(pre_two)


def tag_head(
    pooled, clip_lengths, labels, full_fc1, full_fc2, back_fc1, back_fc2, fc1_bias, fc2_bias
):
    clip_count, half_frames, chans = pooled.shape
    half_ids = lax.broadcasted_iota(jnp.int32, (clip_count, half_frames), 1)
    half_len = clip_lengths // 2
    pooled_valid = (half_ids < half_len[:, None]).astype(jnp.float32)[:, :, None]
    half_float = half_len.astype(jnp.float32)[:, None]
    largest = jnp.max(jnp.where(pooled_valid > 0, pooled, -1e30), axis=1, keepdims=True)
    exp_terms = jnp.exp(pooled - largest) * pooled_valid
    exp_sum = jnp.sum(exp_terms, axis=1)
    log_sum = largest[:, 0, :] + jnp.log(exp_sum)
    mean_time = jnp.sum(pooled * pooled_valid, axis=1) / half_float
    embedding = (log_sum + mean_time).astype(jnp.bfloat16)
    hidden = jnp.dot(embedding, full_fc1, preferred_element_type=jnp.float32) + fc1_bias
    gated_low = jax.nn.silu(hidden).astype(jnp.bfloat16)
    class_logits = jnp.dot(gated_low, full_fc2, preferred_element_type=jnp.float32) + fc2_bias
    d_logits = (jax.nn.sigmoid(class_logits) - labels.astype(jnp.float32)).astype(jnp.bfloat16)
    fc2_term = transpose_dot(gated_low, d_logits)
    fc2_bias_term = jnp.sum(d_logits.astype(jnp.float32), axis=0)
    d_gated = jnp.dot(d_logits, back_fc2.T, preferred_element_type=jnp.float32)
    d_hidden = (d_gated * silu_slope(hidden)).astype(jnp.bfloat16)
    fc1_term = transpose_dot(embedding, d_hidden)
    fc1_bias_term = jnp.sum(d_hidden.astype(jnp.float32), axis=0)
    d_embed = jnp.dot(d_hidden, back_fc1.T, preferred_element_type=jnp.float32)
    soft_weights = exp_terms / exp_sum[:, None, :]
    d_pooled = d_embed[:, None, :] * (soft_weights + pooled_valid / half_float[:, :, None])
    return (class_logits, d_pooled, fc1_term, fc2_term, fc1_bias_term, fc2_bias_term)


def on_device(
    clip_maps,
    lengths,
    labels,
    conv1_weight,
    norm1_gain,
    norm1_shift,
    conv2_weight,
    norm2_gain,
    norm2_shift,
    fc1_weight,
    fc1_bias,
    fc2_weight,
    fc2_bias,
):
    clip_count, frame_count, mel_count, chan_in = clip_maps.shape
    chan_mid = norm1_gain.shape[0]
    valid_four, pixel_valid = make_valid(lengths, frame_count, mel_count)
    masked = clip_maps * valid_four.astype(jnp.bfloat16)
    sent = (conv1_weight, conv2_weight, fc1_weight, fc2_weight)
    gathered = (
        lax.all_gather(sent[0], "shard", axis=0, tiled=True),
        lax.all_gather(sent[1], "shard", axis=0, tiled=True),
        lax.all_gather(sent[2], "shard", axis=0, tiled=True),
        lax.all_gather(sent[3], "shard", axis=0, tiled=True),
    )
    full_one, full_two, full_fc1, full_fc2 = gathered
    patch_one = patch_rows(masked)
    first_out = jnp.dot(patch_one, full_one, preferred_element_type=jnp.float32)
    sum_one, square_one, pixel_count = lax.psum(
        (
            jnp.sum(first_out * pixel_valid, axis=0),
            jnp.sum(first_out * first_out * pixel_valid, axis=0),
            jnp.sum(pixel_valid),
        ),
        ("dp", "shard"),
    )
    normed_one, inv_one, pre_one = normalize(
        first_out, sum_one, square_one, pixel_count, norm1_gain, norm1_shift
    )
    act_one = (jax.nn.silu(pre_one) * pixel_valid).astype(jnp.bfloat16)
    patch_two = patch_rows(act_one.reshape(clip_count, frame_count, mel_count, chan_mid))
    second_out = jnp.dot(patch_two, full_two, preferred_element_type=jnp.float32)
    sum_two, square_two = lax.psum(
        (
            jnp.sum(second_out * pixel_valid, axis=0),
            jnp.sum(second_out * second_out * pixel_valid, axis=0),
        ),
        ("dp", "shard"),
    )
    normed_two, inv_two, pre_two = normalize(
        second_out, sum_two, square_two, pixel_count, norm2_gain, norm2_shift
    )
    act_two = (jax.nn.silu(pre_two) * pixel_valid).reshape(
        clip_count, frame_count, mel_count, chan_mid
    )
    pooled_own = pool_map(act_two)
    back_weights = (
        lax.all_gather(sent[0], "shard", axis=0, tiled=True),
        lax.all_gather(sent[1], "shard", axis=0, tiled=True),
        lax.all_gather(sent[2], "shard", axis=0, tiled=True),
        lax.all_gather(sent[3], "shard", axis=0, tiled=True),
    )
    back_one, back_two, back_fc1, back_fc2 = back_weights
    class_logits, d_pooled, fc1_term, fc2_term, fc1_bias_term, fc2_bias_term = tag_head(
        pooled_own, lengths, labels, full_fc1, full_fc2, back_fc1, back_fc2, fc1_bias, fc2_bias
    )
    dz_two = pooled_slope(d_pooled, pre_two, pixel_valid, mel_count)
    shift_two_grad, gain_two_grad, fc1_bias_grad, fc2_bias_grad = lax.psum(
        (
            jnp.sum(dz_two, axis=0),
            jnp.sum(dz_two * normed_two, axis=0),
            fc1_bias_term,
            fc2_bias_term,
        ),
        ("dp", "shard"),
    )
    d_second = (
        norm2_gain
        * inv_two
        * (dz_two - (shift_two_grad + normed_two * gain_two_grad) / pixel_count)
        * pixel_valid
    ).astype(jnp.bfloat16)
    conv2_part = lax.psum_scatter(
        transpose_dot(patch_two, d_second), "shard", scatter_dimension=0, tiled=True
    )
    d_patch_two = jnp.dot(d_second, back_two.T, preferred_element_type=jnp.float32)
    d_act_one = fold_rows(d_patch_two, clip_count, frame_count, mel_count).reshape(-1, chan_mid)
    dz_one = d_act_one * pixel_valid * silu_slope(pre_one)
    shift_one_grad, gain_one_grad = lax.psum(
        (jnp.sum(dz_one, axis=0), jnp.sum(dz_one * normed_one, axis=0)), ("dp", "shard")
    )
    d_first = (
        norm1_gain
        * inv_one
        * (dz_one - (shift_one_grad + normed_one * gain_one_grad) / pixel_count)
        * pixel_valid
    ).astype(jnp.bfloat16)
    conv1_term = transpose_dot(patch_one, d_first)
    d_patch_one = jnp.dot(d_first, back_one.T, preferred_element_type=jnp.float32)
    input_grad = fold_rows(d_patch_one, clip_count, frame_count, mel_count) * valid_four
    conv1_part, fc1_part, fc2_part = (
        lax.psum_scatter(conv1_term, "shard", scatter_dimension=0, tiled=True),
        lax.psum_scatter(fc1_term, "shard", scatter_dimension=0, tiled=True),
        lax.psum_scatter(fc2_term, "shard", scatter_dimension=0, tiled=True),
    )
    conv1_grad, conv2_grad, fc1_grad, fc2_grad = (
        lax.psum(conv1_part.astype(jnp.bfloat16), "dp").astype(jnp.float32),
        lax.psum(conv2_part.astype(jnp.bfloat16), "dp").astype(jnp.float32),
        lax.psum(fc1_part.astype(jnp.bfloat16), "dp").astype(jnp.float32),
        lax.psum(fc2_part.astype(jnp.bfloat16), "dp").astype(jnp.float32),
    )
    return (
        class_logits,
        input_grad,
        conv1_grad,
        gain_one_grad,
        shift_one_grad,
        conv2_grad,
        gain_two_grad,
        shift_two_grad,
        fc1_grad,
        fc1_bias_grad,
        fc2_grad,
        fc2_bias_grad,
    )


def solution(mesh):
    in_specs = (
        P(("dp", "shard"), None, None, None),
        P(("dp", "shard")),
        P(("dp", "shard"), None),
        P("shard", None),
        P(),
        P(),
        P("shard", None),
        P(),
        P(),
        P("shard", None),
        P(),
        P("shard", None),
        P(),
    )
    out_specs = (
        P(("dp", "shard"), None),
        P(("dp", "shard"), None, None, None),
        P("shard", None),
        P(),
        P(),
        P("shard", None),
        P(),
        P(),
        P("shard", None),
        P(),
        P("shard", None),
        P(),
    )
    dp, shard = mesh.shape["dp"], mesh.shape["shard"]
    step = make_device(dp, shard) if (dp, shard) == (4, 8) else on_device
    return jax.shard_map(
        step, mesh=mesh, in_specs=in_specs, out_specs=out_specs, check_vma=False
    )
```

```python
import functools
import math
import jax
import jax.numpy as jnp
from jax import lax
from jax.experimental import pallas as pl
from jax.experimental.pallas import tpu as pltpu
from jax.sharding import PartitionSpec as P
bf16 = jnp.bfloat16
f32 = jnp.float32
epsilon = 1e-05
big_vmem = 56 * 1024 * 1024
VM = pl.BlockSpec(memory_space=pltpu.VMEM)
SM = pl.BlockSpec(memory_space=pltpu.SMEM)
HB = pl.BlockSpec(memory_space=pl.ANY)

def params():
    return pltpu.CompilerParams(vmem_limit_bytes=big_vmem)

def cost(flops, moved):
    return pl.CostEstimate(flops=int(flops), bytes_accessed=int(moved), transcendentals=0)


def split_kernel(depth, place, weight, *refs):
    outs, (own, sem) = refs[:depth], refs[depth:]
    copy = pltpu.make_async_copy(weight.at[:, place[0]], own, sem)
    copy.start()
    copy.wait()
    line, core = lax.div(place[1], 2), lax.rem(place[1], 2)
    for step in range(depth):
        for other in range(2):
            column = 2 * lax.rem(line - step + depth, depth) + lax.bitwise_xor(core, other)
            width = outs[step].shape[3]
            outs[step][other] = own[:, :, pl.ds(pl.multiple_of(column * width, width), width)]


def split_weight(weight, place, dp, shard):
    rows, columns = weight.shape
    part, depth = rows // (9 * dp), shard // 2
    chunk = jax.ShapeDtypeStruct((2, 9, part, columns // shard), bf16)
    return pl.pallas_call(
        functools.partial(split_kernel, depth),
        out_shape=[chunk] * depth,
        in_specs=[SM, HB],
        out_specs=[VM] * depth,
        scratch_shapes=[pltpu.VMEM((9, part, columns), bf16), pltpu.SemaphoreType.DMA(())],
        compiler_params=params(),
        cost_estimate=cost(0, 4 * rows * columns // dp),
        name="split_weight",
    )(place, weight.reshape(9, dp, part, columns))


def expand_kernel(shard, by_mel, table, *refs):
    depth = shard // 2
    pieces, across, (spread, out, held) = refs[:depth], refs[depth], refs[depth + 1 :]
    for step in range(depth):
        held[pl.ds(9 * step, 9)] = pieces[step][0]
        held[pl.ds(9 * (depth + step), 9)] = across[step]
    part = held.shape[1]
    for a in range(3):
        taps = [
            jnp.concatenate([held[table[(3 * a + b) * shard + position]] for position in range(shard)], axis=0)
            for b in range(3)
        ]
        for m in range(2):
            pair = jnp.concatenate([taps[m + 1], taps[m]], axis=1)
            wide = jnp.dot(pair, spread[...], preferred_element_type=f32).astype(bf16)
            for position in range(shard):
                rows = wide[position * part : (position + 1) * part]
                if by_mel:
                    out[a, m, position] = rows
                else:
                    out[a, position, pl.ds(m * part, part)] = rows


def expand_weight(pieces, across, table, spread, by_mel):
    shard = 2 * len(pieces)
    _, _, part, columns = pieces[0].shape
    shape = (3, 2, shard, part, 2 * columns) if by_mel else (3, shard, 2 * part, 2 * columns)
    wide = pl.pallas_call(
        functools.partial(expand_kernel, shard, by_mel),
        out_shape=jax.ShapeDtypeStruct(shape, bf16),
        in_specs=[SM] + [VM] * (len(pieces) + 2),
        out_specs=VM,
        scratch_shapes=[pltpu.VMEM((9 * shard, part, columns), bf16)],
        compiler_params=params(),
        cost_estimate=cost(2 * 6 * shard * part * 4 * columns * columns, 30 * shard * part * columns),
        name="expand_weight",
    )(table, *pieces, across, spread)
    return wide.reshape(3, 2 * shard * part, 2 * columns)


def conv_kernel(count, back, tile, *refs):
    rows_in, taps, outs, (first, last) = refs[:count], refs[count], refs[count + 1 : -2], refs[-2:]
    height = first.shape[0] - 8
    width = first.shape[1]
    first[0:8] = jnp.zeros((8, width), f32)
    last[height:] = jnp.zeros((8, width), f32)
    late, early = (2, 0) if back else (0, 2)
    contract = (((1,), (1,)), ((), ())) if back else (((1,), (0,)), ((), ()))

    def block(ref, at):
        value = ref[at] if len(ref.shape) == 2 else jnp.concatenate(
            [ref[i, at] for i in range(ref.shape[0])], axis=1)
        return value

    def one(i, carry):
        at = pl.ds(pl.multiple_of(i * tile, tile), tile)
        rows = jnp.concatenate([block(ref, at) for ref in rows_in], axis=1)
        first[pl.ds(pl.multiple_of(i * tile + 8, 8), tile)] = lax.dot_general(
            rows, taps[late], contract, preferred_element_type=f32)
        last[at] = lax.dot_general(rows, taps[early], contract, preferred_element_type=f32)
        return carry

    lax.fori_loop(0, height // tile, one, 0)

    def two(i, carry):
        start = pl.multiple_of(i * tile, tile)
        at = pl.ds(start, tile)
        rows = jnp.concatenate([block(ref, at) for ref in rows_in], axis=1)
        total = lax.dot_general(rows, taps[1], contract, preferred_element_type=f32)
        before = first[pl.ds(start, tile + 8)]
        after = last[pl.ds(start, tile + 8)]
        total = total + before[7 : tile + 7] + after[1 : tile + 1]
        total = total.astype(bf16)
        column = 0
        for out in outs:
            if len(out.shape) == 2:
                step = out.shape[1]
                out[at] = total[:, column : column + step]
                column += step
            else:
                step = out.shape[2]
                for k in range(out.shape[0]):
                    out[k, at] = total[:, column : column + step]
                    column += step
        return carry

    lax.fori_loop(0, height // tile, two, 0)


def whole(shape):
    return pl.BlockSpec(shape, lambda i: (0,) * len(shape))


def convolve(rows_in, taps, out_shapes, back=False, chunk=None, name="convolve"):
    height = out_shapes[0][-2]
    width = taps.shape[1] if back else taps.shape[2]
    specs = [whole(v.shape) for v in rows_in]
    if chunk is not None:
        count, _, lanes = rows_in[0].shape
        specs = [pl.BlockSpec((count, height, lanes), lambda i: (0, chunk, 0))]
    moved = 2 * (taps.size + sum(math.prod(s) for s in out_shapes)) + 2 * height * taps.shape[2 if back else 1]
    return pl.pallas_call(
        functools.partial(conv_kernel, len(rows_in), back, height // 2),
        grid=(1,),
        out_shape=[jax.ShapeDtypeStruct(s, bf16) for s in out_shapes],
        in_specs=specs + [whole(taps.shape)],
        out_specs=[whole(s) for s in out_shapes],
        scratch_shapes=[pltpu.VMEM((height + 8, width), f32)] * 2,
        compiler_params=params(),
        cost_estimate=cost(2 * height * taps.size, moved),
        name=name,
    )(*rows_in, taps)


def grad_kernel(chunks, x_count, g_count, first, count, by_mel, shard, tile, table, *refs):
    n, m = chunks * x_count, chunks * g_count
    x_refs, g_refs = refs[:n], refs[n : n + m]
    spread = refs[n + m]
    out, total, moved, done, sem = refs[-5:]
    height = g_refs[0].shape[0]
    half = spread.shape[0] // 2
    width = 2 * half
    part = out.shape[1]
    total[...] = jnp.zeros_like(total)
    moved[0:8] = jnp.zeros((8, width), f32)
    moved[height + 8 :] = jnp.zeros((8, width), f32)
    for chunk in range(chunks):
        xs = x_refs[chunk * x_count : (chunk + 1) * x_count]
        gs = g_refs[chunk * g_count : (chunk + 1) * g_count]
        column = 0
        for g in gs:
            moved[8 : height + 8, column : column + g.shape[1]] = g[...].astype(f32)
            column += g.shape[1]

        def one(i, carry, xs=xs):
            start = pl.multiple_of(i * tile, tile)
            at = pl.ds(start, tile)
            if by_mel:
                rows = jnp.concatenate(
                    [xs[0][at, (mel * shard + first) * part : (mel * shard + first + count) * part]
                     for mel in range(2)], axis=1)
            else:
                rows = jnp.concatenate([xs[0][i, at] for i in range(count)], axis=1)
            around = moved[pl.ds(start, tile + 16)]
            three = jnp.concatenate(
                [around[9 - a : 9 - a + tile].astype(bf16) for a in range(3)], axis=1)
            total[...] += lax.dot_general(
                rows, three, (((0,), (0,)), ((), ())), preferred_element_type=f32)
            return carry

        lax.fori_loop(0, height // tile, one, 0)

    def fold(position, carry):
        for a in range(3):
            if by_mel:
                at = [pl.multiple_of((mel * count + position) * part, part) for mel in range(2)]
            else:
                at = [pl.multiple_of((2 * position + mel) * part, part) for mel in range(2)]
            top, bottom = [
                lax.dot_general(
                    total[pl.ds(start, part), a * width : (a + 1) * width].astype(bf16),
                    spread[...], (((1,), (1,)), ((), ())), preferred_element_type=f32)
                for start in at
            ]
            taps = [top[:, half:], top[:, :half] + bottom[:, half:], bottom[:, :half]]
            for b in range(3):
                done[(3 * a + b) * count + position] = taps[b].astype(bf16)
        return carry

    lax.fori_loop(0, count, fold, 0)
    copies = [
        pltpu.make_async_copy(
            done.at[tap * count + position], out.at[table[tap * shard + first + position]],
            sem.at[tap * count + position])
        for tap in range(9) for position in range(count)
    ]
    for copy in copies:
        copy.start()
    for copy in copies:
        copy.wait()


def weight_grad(x_chunks, g_chunks, table, spread, part, by_mel, shard, first, count, before=None, name="weight_grad"):
    xs = [v for v, _ in x_chunks]
    gs = [g for chunk in g_chunks for g in chunk]
    height = gs[0].shape[0]
    wide = spread.shape[0]
    deep = 2 * count * part
    flops = 2 * len(x_chunks) * height * deep * wide * 3
    inputs = [table] + xs + gs + [spread]
    specs = [pl.BlockSpec(memory_space=pltpu.SMEM)]
    for v, row in x_chunks:
        if by_mel:
            specs.append(pl.BlockSpec((height, v.shape[1]), lambda i, row=row: (row, 0)))
        else:
            specs.append(pl.BlockSpec((count, height, v.shape[2]), lambda i, row=row: (first // count, row, 0)))
    specs += [whole(v.shape) for v in gs + [spread]]
    if before is not None:
        inputs, specs = inputs + [before], specs + [HB]
    return pl.pallas_call(
        functools.partial(grad_kernel, len(x_chunks), 1, len(g_chunks[0]), first, count, by_mel, shard, height),
        grid=(1,),
        out_shape=jax.ShapeDtypeStruct((9 * shard, part, wide // 2), bf16),
        in_specs=specs,
        out_specs=HB,
        input_output_aliases={} if before is None else {len(inputs) - 1: 0},
        scratch_shapes=[
            pltpu.VMEM((deep, 3 * wide), f32),
            pltpu.VMEM((height + 16, wide), f32),
            pltpu.VMEM((9 * count, part, wide // 2), bf16),
            pltpu.SemaphoreType.DMA((9 * count,)),
        ],
        compiler_params=params(),
        cost_estimate=cost(flops, 2 * len(xs) * height * deep + sum(2 * v.size for v in gs) + 9 * count * part * wide),
        name=name,
    )(*inputs)


def join_kernel(dp, depth, place, *refs):
    parts, out = refs[:-1], refs[-1]
    half = depth // 2
    width = parts[0].shape[4]
    line, core = lax.div(place[1], 2), lax.rem(place[1], 2)
    for source in range(dp):
        group = lax.bitwise_xor(place[0], source)
        for step in range(depth):
            for other in range(2):
                column = 2 * lax.rem(line - step + depth, depth) + lax.bitwise_xor(core, other)
                value = parts[2 * source + step // half][step % half, other, 0]
                out[0, group, :, pl.ds(pl.multiple_of(column * width, width), width)] = value.astype(f32)


def join_grad(parts, place, dp, shard):
    half, _, _, part, width = parts[0].shape
    block = pl.BlockSpec((half, 2, 1, part, width), lambda i: (0, 0, i, 0, 0))
    out = pl.pallas_call(
        functools.partial(join_kernel, dp, shard // 2),
        grid=(9,),
        out_shape=jax.ShapeDtypeStruct((9, dp, part, shard * width), f32),
        in_specs=[SM] + [block] * len(parts),
        out_specs=pl.BlockSpec((1, dp, part, shard * width), lambda i: (i, 0, 0, 0)),
        compiler_params=params(),
        cost_estimate=cost(0, 6 * 9 * dp * part * shard * width),
        name="join_grad",
    )(place, *parts)
    return out.reshape(9 * dp * part, shard * width)


def valid_rows(frames, lanes, length):
    return (lax.broadcasted_iota(jnp.int32, (frames, lanes), 0) < length).astype(f32)


def pack_maps_kernel(frames, order, offset, length, maps, *refs):
    outs, (mask, held, packed, flags) = refs[:-4], refs[-4:]
    step = outs[0].shape[0]
    held[...] = maps[...].astype(f32)
    packed[...] = jnp.zeros_like(packed)
    flags[...] = jnp.zeros_like(flags)

    def one(k, carry):
        source = pl.ds(pl.multiple_of(order[k] * frames, frames), frames)
        at = pl.ds(pl.multiple_of(offset[k], 8), frames)
        packed[at] = held[source]
        flags[at] = valid_rows(frames, flags.shape[1], length[k])
        return carry

    lax.fori_loop(0, order.shape[0], one, 0)
    for p, out in enumerate(outs):
        out[...] = packed[p * step : (p + 1) * step].astype(bf16)
    mask[...] = flags[: mask.shape[0]]


def pack_maps(maps, packing, frames, height, chunks):
    rows, lanes = maps.shape
    *parts, mask = pl.pallas_call(
        functools.partial(pack_maps_kernel, frames),
        out_shape=[jax.ShapeDtypeStruct((height // chunks, lanes), bf16)] * chunks
        + [jax.ShapeDtypeStruct((height, 128), f32)],
        in_specs=[SM] * 3 + [VM],
        out_specs=[VM] * (chunks + 1),
        scratch_shapes=[
            pltpu.VMEM((rows, lanes), f32),
            pltpu.VMEM((height + frames, lanes), f32),
            pltpu.VMEM((height + frames, 128), f32),
        ],
        compiler_params=params(),
        cost_estimate=cost(0, 8 * rows * lanes),
        name="pack_maps",
    )(*packing, maps)
    return parts, mask


def unpack_maps_kernel(frames, order, offset, *refs):
    parts, (out, held, spaced) = refs[:-3], refs[-3:]
    step = parts[0].shape[0]
    for p, part in enumerate(parts):
        held[p * step : (p + 1) * step] = part[...].astype(f32)
    held[len(parts) * step :] = jnp.zeros((frames, held.shape[1]), f32)

    def one(k, carry):
        target = pl.ds(pl.multiple_of(order[k] * frames, frames), frames)
        spaced[target] = held[pl.ds(pl.multiple_of(offset[k], 8), frames)]
        return carry

    lax.fori_loop(0, order.shape[0], one, 0)
    out[...] = spaced[...].astype(bf16)


def unpack_maps(parts, packing, frames, rows):
    step, lanes = parts[0].shape
    return pl.pallas_call(
        functools.partial(unpack_maps_kernel, frames),
        out_shape=jax.ShapeDtypeStruct((rows, lanes), bf16),
        in_specs=[SM] * 2 + [VM] * len(parts),
        out_specs=VM,
        scratch_shapes=[
            pltpu.VMEM((len(parts) * step + frames, lanes), f32),
            pltpu.VMEM((rows, lanes), f32),
        ],
        compiler_params=params(),
        cost_estimate=cost(0, 8 * rows * lanes),
        name="unpack_maps",
    )(*packing[:2], *parts)


def unpack_rows_kernel(frames, order, offset, length, value, out, held):
    height = value.shape[0]
    held[:height] = value[...]
    held[height:] = jnp.zeros((frames, held.shape[1]), f32)

    def one(k, carry):
        target = pl.ds(pl.multiple_of(order[k] * frames, frames), frames)
        rows = held[pl.ds(pl.multiple_of(offset[k], 8), frames)]
        out[target] = rows * valid_rows(frames, rows.shape[1], length[k])
        return carry

    lax.fori_loop(0, order.shape[0], one, 0)


def pack_rows_kernel(frames, order, offset, length, value, out, held):
    held[...] = jnp.zeros_like(held)

    def one(k, carry):
        rows = value[pl.ds(pl.multiple_of(order[k] * frames, frames), frames)]
        target = pl.ds(pl.multiple_of(offset[k], 8), frames)
        held[target] = rows * valid_rows(frames, rows.shape[1], length[k])
        return carry

    lax.fori_loop(0, order.shape[0], one, 0)
    out[...] = held[: out.shape[0]]


def move_rows(value, packing, frames, height, packed):
    lanes = value.shape[1]
    held = height if packed else value.shape[0]
    return pl.pallas_call(
        functools.partial(pack_rows_kernel if packed else unpack_rows_kernel, frames),
        out_shape=jax.ShapeDtypeStruct((height, lanes), f32),
        in_specs=[SM] * 3 + [VM],
        out_specs=VM,
        scratch_shapes=[pltpu.VMEM((held + frames, lanes), f32)],
        compiler_params=params(),
        cost_estimate=cost(0, 8 * height * lanes),
        name="pack_rows" if packed else "unpack_rows",
    )(*packing, value)


under_way_xy, chunks = 3, 4


def roll_to(stacked, start, axis):
    size = stacked.shape[axis]
    doubled = jnp.concatenate([stacked, stacked], axis=axis)
    return lax.dynamic_slice_in_dim(doubled, start, size, axis=axis)


def pick(stacked, index):
    return lax.dynamic_index_in_dim(stacked, index, 0, keepdims=False)


def dot(left, right):
    return jnp.dot(left, right, preferred_element_type=f32)


def dot_transpose(left, right):
    return lax.dot_general(left, right, (((1,), (1,)), ((), ())), preferred_element_type=f32)


def both_mels(sums):
    half = sums.shape[0] // 2
    total = sums[:half] + sums[half:]
    return total, jnp.concatenate([total, total])


def norm_of(values_in, valid, pixel_count):
    _, sum_first = both_mels(jnp.sum(values_in * valid, axis=0))
    _, sum_square = both_mels(jnp.sum(values_in * values_in * valid, axis=0))
    mean_value = sum_first / pixel_count
    inv_std = lax.rsqrt(sum_square / pixel_count - mean_value * mean_value + epsilon)
    return (values_in - mean_value) * inv_std, inv_std


def make_device(dp, shard):
    depth = shard // 2
    lanes = {}

    def after(value, *earlier):
        return lax.optimization_barrier((value,) + earlier)[0]

    def queued(lane, value, send, most=2):
        sent = lanes.setdefault(lane, [])
        if len(sent) >= most:
            value = after(value, sent[-most])
        sent.append(send(value))
        return sent[-1]

    def permute(value, axis, size, move):
        return lax.ppermute(value, axis, [(i, move(i) % size) for i in range(size)])

    def from_z(value, k):
        return queued("z", value, lambda v: permute(v, "shard", shard, lambda i: i - 2 * k), under_way_z)

    def to_z(value, k):
        return queued("z", value, lambda v: permute(v, "shard", shard, lambda i: i + 2 * k), under_way_z)

    def to_z(value, k, most, *earlier):
        value = after(value, *earlier)
        return queued("z", value, lambda v: permute(v, "shard", shard, lambda i: i + 2 * k), most)

    def other_core(value):
        return permute(value, "shard", shard, lambda i: i ^ 1)

    def other_dp(value, r):
        return queued("xy", value, lambda v: permute(v, "dp", dp, lambda i: i ^ r), under_way_xy)

    def gather_dp(value, order):
        one, two = other_dp(value, 1), other_dp(value, 2)
        three = other_dp(one, 2) if order == 0 else other_dp(two, 1)
        return [value, one, two, three]

    def gather_chunks(values):
        near = [[values[0], other_dp(values[0], 1), other_dp(values[0], 2), other_dp(values[0], 3)]]
        for p, value in enumerate(values[1:], 1):
            near.append([value, other_dp(value, 1), other_dp(value, 2)])
            if p > 1:
                near[p - 1].append(other_dp(near[p - 1][1 + (p - 1) % 2], 2 - (p - 1) % 2))
        near[-1].append(other_dp(near[-1][1 + p % 2], 2 - p % 2))
        return near

    def tied(values, *earlier):
        return [after(values[0], *earlier)] + list(values[1:])

    def unswap(parts, d):
        low = [jnp.where(d % 2 == 1, parts[r ^ 1], parts[r]) for r in range(dp)]
        return [jnp.where(d // 2 == 1, low[r ^ 2], low[r]) for r in range(dp)]

    far = [k for k in range(1, depth) if 2 * k != depth] + [depth // 2]

    def core_order(mine, theirs, c):
        return [jnp.where(c == 0, mine, theirs), jnp.where(c == 0, theirs, mine)]

    def gather_small(value, d, z, c):
        near = [permute(value, "dp", dp, lambda i, r=r: i ^ r) for r in range(1, dp)]
        square = jnp.stack(unswap([value] + near, d))
        far = [permute(square, "shard", shard, lambda i, k=k: i - 2 * k) for k in range(1, depth)]
        line = roll_to(jnp.stack([square] + far), (depth - z) % depth, 0)
        return jnp.stack(core_order(line, other_core(line), c), axis=1)

    def weight_in(pieces, most):
        pieces = [pieces[0]] + [to_z(pieces[k], -k, most) for k in range(1, depth)]
        return pieces, other_core(jnp.stack([v[1] for v in pieces]))

    def send_grad(grad, done=()):
        done = dict(done)
        pieces = grad.reshape((2, depth, 9) + grad.shape[1:])
        pieces = jnp.stack([pieces[0], other_core(pieces[1])], axis=1)
        return [pieces[0]] + [to_z(pieces[k], k, 3, *done.get(k, ())) for k in range(1, depth)]

    def near_grad(parts, *earlier):
        def along(value, r, *earlier):
            return permute(after(value, *earlier), "dp", dp, lambda i: i ^ r)

        half = depth // 2
        low, high = jnp.stack(parts[:half]), jnp.stack(parts[half:])
        low_one, high_two = along(low, 1), along(high, 2)
        low_three, high_one = along(low_one, 2, high_two), along(high, 1, low_one)
        low_two, high_three = along(low, 2, low_three, *earlier), along(high_two, 1, high_one, *earlier)
        return [[low, low_one, low_two, low_three], [high, high_one, high_two, high_three]]

    def on_device(
        clip_maps,
        lengths,
        labels,
        conv1_weight,
        norm1_gain,
        norm1_shift,
        conv2_weight,
        norm2_gain,
        norm2_shift,
        fc1_weight,
        fc1_bias,
        fc2_weight,
        fc2_bias,
    ):
        lanes.clear()
        d, s = lax.axis_index("dp"), lax.axis_index("shard")
        z, c = s // 2, s % 2
        place = jnp.stack([d, s]).astype(jnp.int32)
        clip_count, frames, mels, chan_in = clip_maps.shape
        chan_mid = norm1_gain.shape[0]
        classes = labels.shape[1]
        clips = clip_count * dp * shard
        rows = clips * frames
        own_rows = clip_count * frames
        lane = chan_mid // (dp * shard)
        lane_in = chan_in // (dp * shard)
        wide = mels * lane
        quarter = shard * lane_in
        wide_in = mels * quarter

        position = lax.broadcasted_iota(jnp.int32, (9, shard), 1)
        tap = lax.broadcasted_iota(jnp.int32, (9, shard), 0)

        def table_of(block):
            group = tap * shard + block
            owner = group // 9
            place = (owner % 2 ^ c) * depth + (owner // 2 - z + depth) % depth
            return (place * 9 + group % 9).reshape(9 * shard).astype(jnp.int32)

        table = table_of(position)

        from_row = lax.broadcasted_iota(jnp.int32, (dp * wide, dp * wide), 0)
        to_lane = lax.broadcasted_iota(jnp.int32, (dp * wide, dp * wide), 1)
        spread = (
            (from_row // (dp * lane) == to_lane // lane % mels)
            & (from_row // lane % dp == (d ^ (to_lane // wide)))
            & (from_row % lane == to_lane % lane)
        ).astype(bf16)
        from_row = lax.broadcasted_iota(jnp.int32, (chan_in, chan_in), 0)
        to_lane = lax.broadcasted_iota(jnp.int32, (chan_in, chan_in), 1)
        sort_in = (
            (from_row // (dp * lane_in) == to_lane // lane_in % shard)
            & (from_row // lane_in % dp == (d ^ (to_lane // quarter)))
            & (from_row % lane_in == to_lane % lane_in)
        ).astype(bf16)

        pieces_one, across_one = weight_in(split_weight(conv1_weight, place, dp, shard), 3)
        own_frames = lax.broadcasted_iota(jnp.int32, (clip_count, frames), 1)
        own_valid = (own_frames < lengths[:, None])[:, :, None, None]
        clip_maps = after(clip_maps, pieces_one[0])
        masked = clip_maps * own_valid.astype(bf16)
        sorted_in = [dot(masked[:, :, m].reshape(own_rows, chan_in), sort_in).astype(bf16) for m in range(mels)]
        from_dp = []
        for r in range(dp):
            at = slice(r * quarter, (r + 1) * quarter)
            part = jnp.concatenate([v[:, at] for v in sorted_in], axis=1)
            from_dp.append(other_dp(part, r) if r else part)
        group = jnp.concatenate(unswap(from_dp, d), axis=0)
        all_maps = lax.all_gather(after(group, pieces_one[1]), "shard", tiled=True)
        wide_one = expand_weight(pieces_one, across_one, table, spread, True)
        split_two = split_weight(after(conv2_weight, from_dp[1]), place, dp, shard)

        notes = jnp.concatenate([labels, lengths[:, None]], axis=1).astype(bf16)
        notes = gather_small(jnp.pad(notes, ((0, 0), (0, -(classes + 1) % 128))), d, z, c)
        notes = notes.reshape(clips, notes.shape[-1])
        all_labels = notes[:, :classes].astype(f32)
        all_lengths = notes[:, classes].astype(jnp.int32)
        kinds = jnp.stack([all_lengths > frames // 2, (all_lengths > frames // 4) & (all_lengths <= frames // 2), all_lengths <= frames // 4])
        kinds = kinds.astype(jnp.int32)
        taken = jnp.array([frames, frames // 2, frames // 4], jnp.int32)[:, None]
        before = lax.broadcasted_iota(jnp.int32, (clips, clips), 0) < lax.broadcasted_iota(jnp.int32, (clips, clips), 1)
        among = jnp.sum(kinds[:, :, None] * before.astype(jnp.int32)[None], axis=1)
        number = jnp.sum(kinds, axis=1, keepdims=True)
        first_rank = jnp.concatenate([jnp.zeros((1, 1), jnp.int32), number[:1], number[:1] + number[1:2]])
        used = number * taken
        first_row = jnp.concatenate([jnp.zeros((1, 1), jnp.int32), used[:1], used[:1] + used[1:2]])
        rank = jnp.sum(kinds * (first_rank + among), axis=0)
        start = jnp.sum(kinds * (first_row + among * taken), axis=0)
        ranked = (rank[None, :] == lax.broadcasted_iota(jnp.int32, (clips, clips), 0)).astype(jnp.int32)
        clip_ids = lax.broadcasted_iota(jnp.int32, (clips,), 0)
        packing = [jnp.sum(ranked * v[None, :], axis=1) for v in (clip_ids, start, all_lengths)]
        pixel_count = (jnp.sum(all_lengths) * mels).astype(f32)

        def after_maps(height):
            lanes.clear()
            step, half = height // chunks, height // 2
            def scatter_dp(outs):
                total = outs[0].astype(f32)
                for r in range(1, dp):
                    total = total + other_dp(outs[r], r).astype(f32)
                return total

            maps_in, valid = pack_maps(all_maps, packing, frames, height, chunks)
            pieces_two, across_two = weight_in(split_two, 3)
            parts = []
            for p in range(chunks):
                value = after(maps_in[p], *())
                outs = convolve([value], wide_one, [(step, wide)] * dp, name="conv1")
                parts.append(scatter_dp(outs))
            parts = tied(parts, *pieces_two[1:2])
            first_out = jnp.concatenate(parts, axis=0)

            wide_two = expand_weight(pieces_two, across_two, table, spread, False)

            own_start = (s * dp + d) * lane

            def own_channels(vector):
                own = lax.dynamic_slice_in_dim(vector, own_start, lane)
                return jnp.concatenate([own] * mels)

            gain_one, shift_one = own_channels(norm1_gain), own_channels(norm1_shift)
            gain_two, shift_two = own_channels(norm2_gain), own_channels(norm2_shift)

            normed_one, inv_one = norm_of(first_out, valid, pixel_count)
            pre_one = normed_one * gain_one + shift_one
            act_one = (jax.nn.silu(pre_one) * valid).astype(bf16)
            acts = [
                lax.all_gather(after(act_one[:half], *pieces_two[2:3]), "shard"),
                lax.all_gather(after(act_one[half:], wide_two), "shard"),
            ]
            fc_rows = fc1_weight.shape[0]
            own_fc1 = lax.dynamic_slice_in_dim(fc1_weight, d * lane, lane, axis=0)
            some_fc1 = lax.all_gather(after(own_fc1, wide_two), "shard", tiled=True)
            own_fc2 = jnp.pad(fc2_weight, ((0, 0), (0, -classes % 128)))
            own_fc2 = after(lax.dynamic_slice_in_dim(own_fc2, d * lane, lane, axis=0), act_one)
            line = [own_fc2] + [permute(own_fc2, "shard", shard, lambda i, k=k: i - 2 * k) for k in range(1, depth)]
            line = roll_to(jnp.stack(line), (depth - z) % depth, 0)
            parts, outs = [], []
            for p in range(chunks):
                value = after(acts[p // 2], *outs[:1])
                if p >= 2:
                    value = after(value, parts[p - 2])
                outs = convolve([value], wide_two, [(step, wide)] * dp, chunk=p % 2, name="conv2")
                parts.append(scatter_dp(outs))
                if p == 1:
                    line = after(line, outs[0])
                    near = [permute(line, "dp", dp, lambda i, r=r: i ^ r) for r in range(1, dp)]
                    square = jnp.stack(unswap([line] + near, d), axis=1)
                    full_fc2 = jnp.stack(core_order(square, other_core(square), c), axis=1)
                    full_fc2 = full_fc2.reshape(chan_mid, own_fc2.shape[1])[:, :classes]
            parts = tied(parts, full_fc2)
            second_out = jnp.concatenate(parts, axis=0)
            normed_two, inv_two = norm_of(second_out, valid, pixel_count)
            pre_two = normed_two * gain_two + shift_two
            sigma_two = jax.nn.sigmoid(pre_two)
            act_two = pre_two * sigma_two * valid
            slope_two = (sigma_two + act_two * (1.0 - sigma_two)) * valid

            halves = frames // 2
            act_two = move_rows(act_two, packing, frames, rows, False)
            pooled = jnp.sum(act_two.reshape(clips, halves, 2, wide), axis=2)
            pooled = (pooled[:, :, :lane] + pooled[:, :, lane:]) / (2.0 * mels)
            half_len = all_lengths // 2
            half_ids = lax.broadcasted_iota(jnp.int32, (clips, halves), 1)
            pooled_valid = (half_ids < half_len[:, None]).astype(f32)[:, :, None]
            half_float = half_len.astype(f32)[:, None]
            largest = jnp.max(jnp.where(pooled_valid > 0, pooled, -1e30), axis=1, keepdims=True)
            exp_terms = jnp.exp(pooled - largest) * pooled_valid
            exp_sum = jnp.sum(exp_terms, axis=1)
            log_sum = largest[:, 0, :] + jnp.log(exp_sum)
            mean_time = jnp.sum(pooled * pooled_valid, axis=1) / half_float
            own_embedding = (log_sum + mean_time).astype(bf16)
            own_embedding = own_embedding.T
            line = [own_embedding] + [permute(own_embedding, "shard", shard, lambda i, k=k: i - 2 * k) for k in range(1, depth)]
            line = roll_to(jnp.stack(line), (depth - z) % depth, 0)
            line = jnp.stack(core_order(line, other_core(line), c), axis=1).reshape(shard * lane, clips)
            part = lax.dynamic_slice_in_dim(line, c * (clips // 2), clips // 2, axis=1)
            part = transpose_dot(part, some_fc1).astype(bf16)
            near = [permute(part, "dp", dp, lambda i, r=r: i ^ r) for r in range(1, dp)]
            part = sum(v.astype(f32) for v in unswap([part] + near, d))
            hidden = jnp.concatenate(core_order(part, other_core(part), c), axis=0) + fc1_bias
            near = [permute(after(own_embedding, part), "dp", dp, lambda i, r=r: i ^ r) for r in range(1, dp)]
            own_columns = jnp.concatenate(unswap([own_embedding] + near, d), axis=0)
            sigma = jax.nn.sigmoid(hidden)
            gated = (hidden * sigma).astype(bf16)
            logits = dot(gated, full_fc2) + fc2_bias
            d_logits = (jax.nn.sigmoid(logits) - all_labels).astype(bf16)
            d_gated = dot_transpose(d_logits, full_fc2)
            d_hidden = (d_gated * (sigma + hidden * sigma * (1.0 - sigma))).astype(bf16)
            d_embed = dot_transpose(d_hidden, own_fc1)
            soft = exp_terms / exp_sum[:, None, :]
            d_pooled = d_embed[:, None, :] * (soft + pooled_valid / half_float[:, :, None])

            fc1_grad = dot(own_columns, d_hidden)
            own_columns = lax.dynamic_slice_in_dim(gated, s * fc_rows, fc_rows, axis=1)
            fc2_grad = dot(own_columns.T, d_logits)
            fc1_bias_grad = jnp.sum(d_hidden.astype(f32), axis=0)
            fc2_bias_grad = jnp.sum(d_logits.astype(f32), axis=0)
            own_clips = (s * dp + d) * clip_count
            own_logits = lax.dynamic_slice_in_dim(logits, own_clips, clip_count, axis=0)

            d_frames = jnp.concatenate([d_pooled, d_pooled], axis=2) / (2.0 * mels)
            d_frames = jnp.broadcast_to(d_frames[:, :, None, :], (clips, halves, 2, wide))
            dz_two = move_rows(d_frames.reshape(rows, wide), packing, frames, height, True) * slope_two
            shift_two_grad, shift_two_lanes = both_mels(jnp.sum(dz_two, axis=0))
            gain_two_grad, gain_two_lanes = both_mels(jnp.sum(dz_two * normed_two, axis=0))
            d_second = (
                gain_two
                * inv_two
                * (dz_two - (shift_two_lanes + normed_two * gain_two_lanes) / pixel_count)
                * valid
            ).astype(bf16)

            grads_two = gather_chunks(list(d_second.reshape(chunks, step, wide)))
            parts, outs = [], []
            for p in range(chunks):
                ready = tied(grads_two[p], *outs[-1:], *(grads_two[p + 1][1:3] if p + 1 < chunks else ()))
                outs += convolve(ready, wide_two, [(shard, step, wide)], back=True, name="back2")
                if p % 2:
                    out = jnp.concatenate(outs[-2:], axis=1)
                    parts.append(lax.psum_scatter(out, "shard", scatter_dimension=0))

            grad_two = None
            count = shard // 4
            act_chunks = [(acts[p // 2], p % 2) for p in range(chunks)]
            for first in range(0, shard, count):
                ready = [tied(grads_two[0], outs[-1])] + grads_two[1:]
                grad_two = weight_grad(
                    act_chunks, ready, table, spread, lane, False, shard, first, count, grad_two, name="grad2",
                )
            parts = tied(parts, grad_two)

            d_act_one = jnp.concatenate(parts, axis=0).astype(f32)
            sigma_one = jax.nn.sigmoid(pre_one)
            dz_one = d_act_one * valid * (sigma_one + pre_one * sigma_one * (1.0 - sigma_one))
            shift_one_grad, shift_one_lanes = both_mels(jnp.sum(dz_one, axis=0))
            gain_one_grad, gain_one_lanes = both_mels(jnp.sum(dz_one * normed_one, axis=0))
            d_first = (
                gain_one
                * inv_one
                * (dz_one - (shift_one_lanes + normed_one * gain_one_lanes) / pixel_count)
                * valid
            ).astype(bf16)
            values = list(d_first.reshape(chunks, step, wide))
            norm_grads = jnp.stack([gain_one_grad, shift_one_grad, gain_two_grad, shift_two_grad])
            grads_one = gather_chunks(values)
            sent_two = send_grad(grad_two, {2: grads_one[1][1:3], 3: grads_one[3][1:3]})
            outs = []
            for p in range(chunks):
                ready = tied(grads_one[p], *outs[-1:], *(grads_one[p + 1][1:3] if p + 1 < chunks else ()))
                outs += convolve(ready, wide_one, [(step, wide_in)], back=True, name="back1")
            near = [permute(norm_grads, "dp", dp, lambda i, r=r: i ^ r) for r in range(1, dp)]
            norm_grads = jnp.stack(unswap([norm_grads] + near, d))
            near_two = near_grad([after(v, grads_one[-1][3], norm_grads) for v in sent_two])

            grad_one, d_in = None, None
            count = shard // 2
            for first in range(0, shard, count):
                ready = [tied(grads_one[0], outs[-1], *((near_two[0][0], near_two[1][0]) if first else sent_two[1:2]))] + grads_one[1:]
                grad_one = weight_grad(
                    [(v, 0) for v in maps_in], ready, table, spread, lane_in, True, shard, first, count, grad_one, name="grad1",
                )
            d_in = unpack_maps(tied(outs, grad_one), packing, frames, rows)
            d_in = d_in.reshape(shard, rows // shard, wide_in)
            total = lax.psum_scatter(d_in, "shard", scatter_dimension=0)
            sent_one = send_grad(grad_one)
            conv2_grad = join_grad([h for pair in zip(*near_two) for h in pair], place, dp, shard)
            total = total.reshape(dp, own_rows, wide_in)
            from_dp = [other_dp(pick(total, d ^ r), r) if r else pick(total, d) for r in range(dp)]
            near_one = near_grad([after(v, near_two[0][2], near_two[1][3]) for v in sent_one], *from_dp[1:])
            conv1_grad = join_grad([h for pair in zip(*near_one) for h in pair], place, dp, shard)

            norm_grads = after(norm_grads, sent_one[-1])
            line = [norm_grads] + [permute(norm_grads, "shard", shard, lambda i, k=k: i - 2 * k) for k in range(1, depth)]
            line = roll_to(jnp.stack(line), (depth - z) % depth, 0)
            norm_grads = jnp.stack(core_order(line, other_core(line), c), axis=1)
            norm_grads = norm_grads.reshape(dp * shard, 4, lane)
            norm_grads = jnp.moveaxis(norm_grads, 0, 1).reshape(4, chan_mid)

            input_grad = []
            for m in range(mels):
                at = slice(m * quarter, (m + 1) * quarter)
                mixed = jnp.concatenate([v[:, at] for v in from_dp], axis=1)
                input_grad.append(dot_transpose(mixed, sort_in).reshape(clip_count, frames, chan_in))
            input_grad = jnp.stack(input_grad, axis=2) * own_valid.astype(f32)

            return (
                own_logits,
                input_grad,
                conv1_grad,
                norm_grads[0],
                norm_grads[1],
                conv2_grad,
                norm_grads[2],
                norm_grads[3],
                fc1_grad,
                fc1_bias_grad,
                fc2_grad,
                fc2_bias_grad,
            )

        def rest(height):
            def run():
                return after_maps(height)

            return run

        few = rows * 21 // 32
        assert few % (32 * chunks) == 0
        return lax.cond(jnp.sum(used) <= few, rest(few), rest(rows))

    return on_device


def patch_rows(grid_in):
    clip_count, frame_count, mel_count, chan_count = grid_in.shape
    padded = jnp.pad(grid_in, ((0, 0), (1, 1), (1, 1), (0, 0)))
    tap_list = [
        padded[:, shift_t : shift_t + frame_count, shift_m : shift_m + mel_count, :]
        for shift_t in range(3)
        for shift_m in range(3)
    ]
    stacked = jnp.stack(tap_list, axis=3)
    return stacked.reshape(clip_count * frame_count * mel_count, 9 * chan_count)


def fold_rows(grad_rows, clip_count, frame_count, mel_count):
    chan_count = grad_rows.shape[1] // 9
    tap_terms = grad_rows.reshape(clip_count, frame_count, mel_count, 9, chan_count)
    summed = jnp.zeros((clip_count, frame_count + 2, mel_count + 2, chan_count), jnp.float32)
    for tap_index in range(9):
        shift_t = tap_index // 3
        shift_m = tap_index % 3
        summed = summed + jnp.pad(
            tap_terms[:, :, :, tap_index, :],
            ((0, 0), (shift_t, 2 - shift_t), (shift_m, 2 - shift_m), (0, 0)),
        )
    return summed[:, 1 : frame_count + 1, 1 : mel_count + 1, :]


def normalize(values_in, sum_first, sum_square, pixel_count, gain, shift):
    mean_value = sum_first / pixel_count
    inv_std = lax.rsqrt(sum_square / pixel_count - mean_value * mean_value + epsilon)
    normed = (values_in - mean_value) * inv_std
    return (normed, inv_std, normed * gain + shift)


def silu_slope(values_in):
    sigma = jax.nn.sigmoid(values_in)
    return sigma + values_in * sigma * (1.0 - sigma)


def transpose_dot(left, right):
    return lax.dot_general(
        left, right, (((0,), (0,)), ((), ())), preferred_element_type=jnp.float32
    )


def make_valid(clip_lengths, frame_count, mel_count):
    clip_count = clip_lengths.shape[0]
    frame_ids = lax.broadcasted_iota(jnp.int32, (clip_count, frame_count), 1)
    valid_two = (frame_ids < clip_lengths[:, None]).astype(jnp.float32)
    pixel_valid = jnp.broadcast_to(
        valid_two[:, :, None], (clip_count, frame_count, mel_count)
    ).reshape(-1, 1)
    return (valid_two[:, :, None, None], pixel_valid)


def pool_map(act_grid):
    clip_count, frame_count, mel_count, chans = act_grid.shape
    pooled = jnp.mean(
        act_grid.reshape(clip_count, frame_count // 2, 2, mel_count // 2, 2, chans), axis=(2, 4)
    )
    return jnp.mean(pooled, axis=2)


def pooled_slope(d_pooled, pre_two, pixel_valid, mel_count):
    clip_count, half_frames, chans = d_pooled.shape
    d_frames = jnp.repeat(d_pooled, 2, axis=1)[:, :, None, :] / (2.0 * mel_count)
    d_act_two = jnp.broadcast_to(d_frames, (clip_count, 2 * half_frames, mel_count, chans)).reshape(
        -1, chans
    )
    return d_act_two * pixel_valid * silu_slope(pre_two)


def tag_head(
    pooled, clip_lengths, labels, full_fc1, full_fc2, back_fc1, back_fc2, fc1_bias, fc2_bias
):
    clip_count, half_frames, chans = pooled.shape
    half_ids = lax.broadcasted_iota(jnp.int32, (clip_count, half_frames), 1)
    half_len = clip_lengths // 2
    pooled_valid = (half_ids < half_len[:, None]).astype(jnp.float32)[:, :, None]
    half_float = half_len.astype(jnp.float32)[:, None]
    largest = jnp.max(jnp.where(pooled_valid > 0, pooled, -1e30), axis=1, keepdims=True)
    exp_terms = jnp.exp(pooled - largest) * pooled_valid
    exp_sum = jnp.sum(exp_terms, axis=1)
    log_sum = largest[:, 0, :] + jnp.log(exp_sum)
    mean_time = jnp.sum(pooled * pooled_valid, axis=1) / half_float
    embedding = (log_sum + mean_time).astype(jnp.bfloat16)
    hidden = jnp.dot(embedding, full_fc1, preferred_element_type=jnp.float32) + fc1_bias
    gated_low = jax.nn.silu(hidden).astype(jnp.bfloat16)
    class_logits = jnp.dot(gated_low, full_fc2, preferred_element_type=jnp.float32) + fc2_bias
    d_logits = (jax.nn.sigmoid(class_logits) - labels.astype(jnp.float32)).astype(jnp.bfloat16)
    fc2_term = transpose_dot(gated_low, d_logits)
    fc2_bias_term = jnp.sum(d_logits.astype(jnp.float32), axis=0)
    d_gated = jnp.dot(d_logits, back_fc2.T, preferred_element_type=jnp.float32)
    d_hidden = (d_gated * silu_slope(hidden)).astype(jnp.bfloat16)
    fc1_term = transpose_dot(embedding, d_hidden)
    fc1_bias_term = jnp.sum(d_hidden.astype(jnp.float32), axis=0)
    d_embed = jnp.dot(d_hidden, back_fc1.T, preferred_element_type=jnp.float32)
    soft_weights = exp_terms / exp_sum[:, None, :]
    d_pooled = d_embed[:, None, :] * (soft_weights + pooled_valid / half_float[:, :, None])
    return (class_logits, d_pooled, fc1_term, fc2_term, fc1_bias_term, fc2_bias_term)


def on_device(
    clip_maps,
    lengths,
    labels,
    conv1_weight,
    norm1_gain,
    norm1_shift,
    conv2_weight,
    norm2_gain,
    norm2_shift,
    fc1_weight,
    fc1_bias,
    fc2_weight,
    fc2_bias,
):
    clip_count, frame_count, mel_count, chan_in = clip_maps.shape
    chan_mid = norm1_gain.shape[0]
    valid_four, pixel_valid = make_valid(lengths, frame_count, mel_count)
    masked = clip_maps * valid_four.astype(jnp.bfloat16)
    sent = (conv1_weight, conv2_weight, fc1_weight, fc2_weight)
    gathered = (
        lax.all_gather(sent[0], "shard", axis=0, tiled=True),
        lax.all_gather(sent[1], "shard", axis=0, tiled=True),
        lax.all_gather(sent[2], "shard", axis=0, tiled=True),
        lax.all_gather(sent[3], "shard", axis=0, tiled=True),
    )
    full_one, full_two, full_fc1, full_fc2 = gathered
    patch_one = patch_rows(masked)
    first_out = jnp.dot(patch_one, full_one, preferred_element_type=jnp.float32)
    sum_one, square_one, pixel_count = lax.psum(
        (
            jnp.sum(first_out * pixel_valid, axis=0),
            jnp.sum(first_out * first_out * pixel_valid, axis=0),
            jnp.sum(pixel_valid),
        ),
        ("dp", "shard"),
    )
    normed_one, inv_one, pre_one = normalize(
        first_out, sum_one, square_one, pixel_count, norm1_gain, norm1_shift
    )
    act_one = (jax.nn.silu(pre_one) * pixel_valid).astype(jnp.bfloat16)
    patch_two = patch_rows(act_one.reshape(clip_count, frame_count, mel_count, chan_mid))
    second_out = jnp.dot(patch_two, full_two, preferred_element_type=jnp.float32)
    sum_two, square_two = lax.psum(
        (
            jnp.sum(second_out * pixel_valid, axis=0),
            jnp.sum(second_out * second_out * pixel_valid, axis=0),
        ),
        ("dp", "shard"),
    )
    normed_two, inv_two, pre_two = normalize(
        second_out, sum_two, square_two, pixel_count, norm2_gain, norm2_shift
    )
    act_two = (jax.nn.silu(pre_two) * pixel_valid).reshape(
        clip_count, frame_count, mel_count, chan_mid
    )
    pooled_own = pool_map(act_two)
    back_weights = (
        lax.all_gather(sent[0], "shard", axis=0, tiled=True),
        lax.all_gather(sent[1], "shard", axis=0, tiled=True),
        lax.all_gather(sent[2], "shard", axis=0, tiled=True),
        lax.all_gather(sent[3], "shard", axis=0, tiled=True),
    )
    back_one, back_two, back_fc1, back_fc2 = back_weights
    class_logits, d_pooled, fc1_term, fc2_term, fc1_bias_term, fc2_bias_term = tag_head(
        pooled_own, lengths, labels, full_fc1, full_fc2, back_fc1, back_fc2, fc1_bias, fc2_bias
    )
    dz_two = pooled_slope(d_pooled, pre_two, pixel_valid, mel_count)
    shift_two_grad, gain_two_grad, fc1_bias_grad, fc2_bias_grad = lax.psum(
        (
            jnp.sum(dz_two, axis=0),
            jnp.sum(dz_two * normed_two, axis=0),
            fc1_bias_term,
            fc2_bias_term,
        ),
        ("dp", "shard"),
    )
    d_second = (
        norm2_gain
        * inv_two
        * (dz_two - (shift_two_grad + normed_two * gain_two_grad) / pixel_count)
        * pixel_valid
    ).astype(jnp.bfloat16)
    conv2_part = lax.psum_scatter(
        transpose_dot(patch_two, d_second), "shard", scatter_dimension=0, tiled=True
    )
    d_patch_two = jnp.dot(d_second, back_two.T, preferred_element_type=jnp.float32)
    d_act_one = fold_rows(d_patch_two, clip_count, frame_count, mel_count).reshape(-1, chan_mid)
    dz_one = d_act_one * pixel_valid * silu_slope(pre_one)
    shift_one_grad, gain_one_grad = lax.psum(
        (jnp.sum(dz_one, axis=0), jnp.sum(dz_one * normed_one, axis=0)), ("dp", "shard")
    )
    d_first = (
        norm1_gain
        * inv_one
        * (dz_one - (shift_one_grad + normed_one * gain_one_grad) / pixel_count)
        * pixel_valid
    ).astype(jnp.bfloat16)
    conv1_term = transpose_dot(patch_one, d_first)
    d_patch_one = jnp.dot(d_first, back_one.T, preferred_element_type=jnp.float32)
    input_grad = fold_rows(d_patch_one, clip_count, frame_count, mel_count) * valid_four
    conv1_part, fc1_part, fc2_part = (
        lax.psum_scatter(conv1_term, "shard", scatter_dimension=0, tiled=True),
        lax.psum_scatter(fc1_term, "shard", scatter_dimension=0, tiled=True),
        lax.psum_scatter(fc2_term, "shard", scatter_dimension=0, tiled=True),
    )
    conv1_grad, conv2_grad, fc1_grad, fc2_grad = (
        lax.psum(conv1_part.astype(jnp.bfloat16), "dp").astype(jnp.float32),
        lax.psum(conv2_part.astype(jnp.bfloat16), "dp").astype(jnp.float32),
        lax.psum(fc1_part.astype(jnp.bfloat16), "dp").astype(jnp.float32),
        lax.psum(fc2_part.astype(jnp.bfloat16), "dp").astype(jnp.float32),
    )
    return (
        class_logits,
        input_grad,
        conv1_grad,
        gain_one_grad,
        shift_one_grad,
        conv2_grad,
        gain_two_grad,
        shift_two_grad,
        fc1_grad,
        fc1_bias_grad,
        fc2_grad,
        fc2_bias_grad,
    )


def solution(mesh):
    in_specs = (
        P(("dp", "shard"), None, None, None),
        P(("dp", "shard")),
        P(("dp", "shard"), None),
        P("shard", None),
        P(),
        P(),
        P("shard", None),
        P(),
        P(),
        P("shard", None),
        P(),
        P("shard", None),
        P(),
    )
    out_specs = (
        P(("dp", "shard"), None),
        P(("dp", "shard"), None, None, None),
        P("shard", None),
        P(),
        P(),
        P("shard", None),
        P(),
        P(),
        P("shard", None),
        P(),
        P("shard", None),
        P(),
    )
    dp, shard = mesh.shape["dp"], mesh.shape["shard"]
    step = make_device(dp, shard) if (dp, shard) == (4, 8) else on_device
    return jax.shard_map(
        step, mesh=mesh, in_specs=in_specs, out_specs=out_specs, check_vma=False
    )
```

```python
import functools
import math
import jax
import jax.numpy as jnp
from jax import lax
from jax.experimental import pallas as pl
from jax.experimental.pallas import tpu as pltpu
from jax.sharding import PartitionSpec as P
bf16 = jnp.bfloat16
f32 = jnp.float32
epsilon = 1e-05
big_vmem = 56 * 1024 * 1024
VM = pl.BlockSpec(memory_space=pltpu.VMEM)
SM = pl.BlockSpec(memory_space=pltpu.SMEM)
HB = pl.BlockSpec(memory_space=pl.ANY)

def params():
    return pltpu.CompilerParams(vmem_limit_bytes=big_vmem)

def cost(flops, moved):
    return pl.CostEstimate(flops=int(flops), bytes_accessed=int(moved), transcendentals=0)


def split_kernel(depth, place, weight, *refs):
    outs, (own, sem) = refs[:depth], refs[depth:]
    copy = pltpu.make_async_copy(weight.at[:, place[0]], own, sem)
    copy.start()
    copy.wait()
    line, core = lax.div(place[1], 2), lax.rem(place[1], 2)
    for step in range(depth):
        for other in range(2):
            column = 2 * lax.rem(line - step + depth, depth) + lax.bitwise_xor(core, other)
            width = outs[step].shape[3]
            outs[step][other] = own[:, :, pl.ds(pl.multiple_of(column * width, width), width)]


def split_weight(weight, place, dp, shard):
    rows, columns = weight.shape
    part, depth = rows // (9 * dp), shard // 2
    chunk = jax.ShapeDtypeStruct((2, 9, part, columns // shard), bf16)
    return pl.pallas_call(
        functools.partial(split_kernel, depth),
        out_shape=[chunk] * depth,
        in_specs=[SM, HB],
        out_specs=[VM] * depth,
        scratch_shapes=[pltpu.VMEM((9, part, columns), bf16), pltpu.SemaphoreType.DMA(())],
        compiler_params=params(),
        cost_estimate=cost(0, 4 * rows * columns // dp),
        name="split_weight",
    )(place, weight.reshape(9, dp, part, columns))


def expand_kernel(shard, by_mel, table, *refs):
    depth = shard // 2
    pieces, across, (spread, out, held) = refs[:depth], refs[depth], refs[depth + 1 :]
    for step in range(depth):
        held[pl.ds(9 * step, 9)] = pieces[step][0]
        held[pl.ds(9 * (depth + step), 9)] = across[step]
    part = held.shape[1]
    for a in range(3):
        taps = [
            jnp.concatenate([held[table[(3 * a + b) * shard + position]] for position in range(shard)], axis=0)
            for b in range(3)
        ]
        for m in range(2):
            pair = jnp.concatenate([taps[m + 1], taps[m]], axis=1)
            wide = jnp.dot(pair, spread[...], preferred_element_type=f32).astype(bf16)
            for position in range(shard):
                rows = wide[position * part : (position + 1) * part]
                if by_mel:
                    out[a, m, position] = rows
                else:
                    out[a, position, pl.ds(m * part, part)] = rows


def expand_weight(pieces, across, table, spread, by_mel):
    shard = 2 * len(pieces)
    _, _, part, columns = pieces[0].shape
    shape = (3, 2, shard, part, 2 * columns) if by_mel else (3, shard, 2 * part, 2 * columns)
    wide = pl.pallas_call(
        functools.partial(expand_kernel, shard, by_mel),
        out_shape=jax.ShapeDtypeStruct(shape, bf16),
        in_specs=[SM] + [VM] * (len(pieces) + 2),
        out_specs=VM,
        scratch_shapes=[pltpu.VMEM((9 * shard, part, columns), bf16)],
        compiler_params=params(),
        cost_estimate=cost(2 * 6 * shard * part * 4 * columns * columns, 30 * shard * part * columns),
        name="expand_weight",
    )(table, *pieces, across, spread)
    return wide.reshape(3, 2 * shard * part, 2 * columns)


def conv_kernel(count, back, tile, *refs):
    rows_in, taps, outs, (first, last) = refs[:count], refs[count], refs[count + 1 : -2], refs[-2:]
    height = first.shape[0] - 8
    width = first.shape[1]
    first[0:8] = jnp.zeros((8, width), f32)
    last[height:] = jnp.zeros((8, width), f32)
    late, early = (2, 0) if back else (0, 2)
    contract = (((1,), (1,)), ((), ())) if back else (((1,), (0,)), ((), ()))

    def block(ref, at):
        value = ref[at] if len(ref.shape) == 2 else jnp.concatenate(
            [ref[i, at] for i in range(ref.shape[0])], axis=1)
        return value

    def one(i, carry):
        at = pl.ds(pl.multiple_of(i * tile, tile), tile)
        rows = jnp.concatenate([block(ref, at) for ref in rows_in], axis=1)
        first[pl.ds(pl.multiple_of(i * tile + 8, 8), tile)] = lax.dot_general(
            rows, taps[late], contract, preferred_element_type=f32)
        last[at] = lax.dot_general(rows, taps[early], contract, preferred_element_type=f32)
        return carry

    lax.fori_loop(0, height // tile, one, 0)

    def two(i, carry):
        start = pl.multiple_of(i * tile, tile)
        at = pl.ds(start, tile)
        rows = jnp.concatenate([block(ref, at) for ref in rows_in], axis=1)
        total = lax.dot_general(rows, taps[1], contract, preferred_element_type=f32)
        before = first[pl.ds(start, tile + 8)]
        after = last[pl.ds(start, tile + 8)]
        total = total + before[7 : tile + 7] + after[1 : tile + 1]
        total = total.astype(bf16)
        column = 0
        for out in outs:
            if len(out.shape) == 2:
                step = out.shape[1]
                out[at] = total[:, column : column + step]
                column += step
            else:
                step = out.shape[2]
                for k in range(out.shape[0]):
                    out[k, at] = total[:, column : column + step]
                    column += step
        return carry

    lax.fori_loop(0, height // tile, two, 0)


def whole(shape):
    return pl.BlockSpec(shape, lambda i: (0,) * len(shape))


def convolve(rows_in, taps, out_shapes, back=False, chunk=None, name="convolve"):
    height = out_shapes[0][-2]
    width = taps.shape[1] if back else taps.shape[2]
    specs = [whole(v.shape) for v in rows_in]
    if chunk is not None:
        lanes = rows_in[0].shape[-1]
        if len(rows_in[0].shape) == 2:
            specs = [pl.BlockSpec((height, lanes), lambda i: (chunk, 0))]
        else:
            specs = [pl.BlockSpec((rows_in[0].shape[0], height, lanes), lambda i: (0, chunk, 0))]
    moved = 2 * (taps.size + sum(math.prod(s) for s in out_shapes)) + 2 * height * taps.shape[2 if back else 1]
    return pl.pallas_call(
        functools.partial(conv_kernel, len(rows_in), back, height // 2),
        grid=(1,),
        out_shape=[jax.ShapeDtypeStruct(s, bf16) for s in out_shapes],
        in_specs=specs + [whole(taps.shape)],
        out_specs=[whole(s) for s in out_shapes],
        scratch_shapes=[pltpu.VMEM((height + 8, width), f32)] * 2,
        compiler_params=params(),
        cost_estimate=cost(2 * height * taps.size, moved),
        name=name,
    )(*rows_in, taps)


def grad_kernel(chunks, x_count, g_count, first, count, by_mel, shard, tile, table, *refs):
    n, m = chunks * x_count, chunks * g_count
    x_refs, g_refs = refs[:n], refs[n : n + m]
    spread = refs[n + m]
    out, total, moved, done, sem = refs[-5:]
    height = g_refs[0].shape[0]
    half = spread.shape[0] // 2
    width = 2 * half
    part = out.shape[1]
    total[...] = jnp.zeros_like(total)
    moved[0:8] = jnp.zeros((8, width), f32)
    moved[height + 8 :] = jnp.zeros((8, width), f32)
    for chunk in range(chunks):
        xs = x_refs[chunk * x_count : (chunk + 1) * x_count]
        gs = g_refs[chunk * g_count : (chunk + 1) * g_count]
        column = 0
        for g in gs:
            moved[8 : height + 8, column : column + g.shape[1]] = g[...].astype(f32)
            column += g.shape[1]

        def one(i, carry, xs=xs):
            start = pl.multiple_of(i * tile, tile)
            at = pl.ds(start, tile)
            if by_mel:
                rows = jnp.concatenate(
                    [xs[0][at, (mel * shard + first) * part : (mel * shard + first + count) * part]
                     for mel in range(2)], axis=1)
            else:
                rows = jnp.concatenate([xs[0][i, at] for i in range(count)], axis=1)
            around = moved[pl.ds(start, tile + 16)]
            three = jnp.concatenate(
                [around[9 - a : 9 - a + tile].astype(bf16) for a in range(3)], axis=1)
            total[...] += lax.dot_general(
                rows, three, (((0,), (0,)), ((), ())), preferred_element_type=f32)
            return carry

        lax.fori_loop(0, height // tile, one, 0)

    def fold(position, carry):
        for a in range(3):
            if by_mel:
                at = [pl.multiple_of((mel * count + position) * part, part) for mel in range(2)]
            else:
                at = [pl.multiple_of((2 * position + mel) * part, part) for mel in range(2)]
            top, bottom = [
                lax.dot_general(
                    total[pl.ds(start, part), a * width : (a + 1) * width].astype(bf16),
                    spread[...], (((1,), (1,)), ((), ())), preferred_element_type=f32)
                for start in at
            ]
            taps = [top[:, half:], top[:, :half] + bottom[:, half:], bottom[:, :half]]
            for b in range(3):
                done[(3 * a + b) * count + position] = taps[b].astype(bf16)
        return carry

    lax.fori_loop(0, count, fold, 0)
    copies = [
        pltpu.make_async_copy(
            done.at[tap * count + position], out.at[table[tap * shard + first + position]],
            sem.at[tap * count + position])
        for tap in range(9) for position in range(count)
    ]
    for copy in copies:
        copy.start()
    for copy in copies:
        copy.wait()


def weight_grad(x_chunks, g_chunks, table, spread, part, by_mel, shard, first, count, before=None, name="weight_grad"):
    xs = [v for v, _ in x_chunks]
    gs = [g for chunk in g_chunks for g in chunk]
    height = gs[0].shape[0]
    wide = spread.shape[0]
    deep = 2 * count * part
    flops = 2 * len(x_chunks) * height * deep * wide * 3
    inputs = [table] + xs + gs + [spread]
    specs = [pl.BlockSpec(memory_space=pltpu.SMEM)]
    for v, row in x_chunks:
        if by_mel:
            specs.append(pl.BlockSpec((height, v.shape[1]), lambda i, row=row: (row, 0)))
        else:
            specs.append(pl.BlockSpec((count, height, v.shape[2]), lambda i, row=row: (first // count, row, 0)))
    specs += [whole(v.shape) for v in gs + [spread]]
    if before is not None:
        inputs, specs = inputs + [before], specs + [HB]
    return pl.pallas_call(
        functools.partial(grad_kernel, len(x_chunks), 1, len(g_chunks[0]), first, count, by_mel, shard, height // 2),
        grid=(1,),
        out_shape=jax.ShapeDtypeStruct((9 * shard, part, wide // 2), bf16),
        in_specs=specs,
        out_specs=HB,
        input_output_aliases={} if before is None else {len(inputs) - 1: 0},
        scratch_shapes=[
            pltpu.VMEM((deep, 3 * wide), f32),
            pltpu.VMEM((height + 16, wide), f32),
            pltpu.VMEM((9 * count, part, wide // 2), bf16),
            pltpu.SemaphoreType.DMA((9 * count,)),
        ],
        compiler_params=params(),
        cost_estimate=cost(flops, 2 * len(xs) * height * deep + sum(2 * v.size for v in gs) + 9 * count * part * wide),
        name=name,
    )(*inputs)


def join_kernel(dp, depth, place, *refs):
    parts, out = refs[:-1], refs[-1]
    half = depth // 2
    width = parts[0].shape[4]
    line, core = lax.div(place[1], 2), lax.rem(place[1], 2)
    for source in range(dp):
        group = lax.bitwise_xor(place[0], source)
        for step in range(depth):
            for other in range(2):
                column = 2 * lax.rem(line - step + depth, depth) + lax.bitwise_xor(core, other)
                value = parts[2 * source + step // half][step % half, other, 0]
                out[0, group, :, pl.ds(pl.multiple_of(column * width, width), width)] = value.astype(f32)


def join_grad(parts, place, dp, shard):
    half, _, _, part, width = parts[0].shape
    block = pl.BlockSpec((half, 2, 1, part, width), lambda i: (0, 0, i, 0, 0))
    out = pl.pallas_call(
        functools.partial(join_kernel, dp, shard // 2),
        grid=(9,),
        out_shape=jax.ShapeDtypeStruct((9, dp, part, shard * width), f32),
        in_specs=[SM] + [block] * len(parts),
        out_specs=pl.BlockSpec((1, dp, part, shard * width), lambda i: (i, 0, 0, 0)),
        compiler_params=params(),
        cost_estimate=cost(0, 6 * 9 * dp * part * shard * width),
        name="join_grad",
    )(place, *parts)
    return out.reshape(9 * dp * part, shard * width)


def valid_rows(frames, lanes, length):
    return (lax.broadcasted_iota(jnp.int32, (frames, lanes), 0) < length).astype(f32)


def pack_maps_kernel(frames, order, offset, length, maps, *refs):
    outs, (mask, held, packed, flags) = refs[:-4], refs[-4:]
    step = outs[0].shape[0]
    held[...] = maps[...].astype(f32)
    packed[...] = jnp.zeros_like(packed)
    flags[...] = jnp.zeros_like(flags)

    def one(k, carry):
        source = pl.ds(pl.multiple_of(order[k] * frames, frames), frames)
        at = pl.ds(pl.multiple_of(offset[k], 8), frames)
        packed[at] = held[source]
        flags[at] = valid_rows(frames, flags.shape[1], length[k])
        return carry

    lax.fori_loop(0, order.shape[0], one, 0)
    for p, out in enumerate(outs):
        out[...] = packed[p * step : (p + 1) * step].astype(bf16)
    mask[...] = flags[: mask.shape[0]]


def pack_maps(maps, packing, frames, height, chunks):
    rows, lanes = maps.shape
    *parts, mask = pl.pallas_call(
        functools.partial(pack_maps_kernel, frames),
        out_shape=[jax.ShapeDtypeStruct((height // chunks, lanes), bf16)] * chunks
        + [jax.ShapeDtypeStruct((height, 128), f32)],
        in_specs=[SM] * 3 + [VM],
        out_specs=[VM] * (chunks + 1),
        scratch_shapes=[
            pltpu.VMEM((rows, lanes), f32),
            pltpu.VMEM((height + frames, lanes), f32),
            pltpu.VMEM((height + frames, 128), f32),
        ],
        compiler_params=params(),
        cost_estimate=cost(0, 8 * rows * lanes),
        name="pack_maps",
    )(*packing, maps)
    return parts, mask


def unpack_maps_kernel(frames, order, offset, *refs):
    parts, (out, held, spaced) = refs[:-3], refs[-3:]
    step = parts[0].shape[0]
    for p, part in enumerate(parts):
        held[p * step : (p + 1) * step] = part[...].astype(f32)
    held[len(parts) * step :] = jnp.zeros((frames, held.shape[1]), f32)

    def one(k, carry):
        target = pl.ds(pl.multiple_of(order[k] * frames, frames), frames)
        spaced[target] = held[pl.ds(pl.multiple_of(offset[k], 8), frames)]
        return carry

    lax.fori_loop(0, order.shape[0], one, 0)
    out[...] = spaced[...].astype(bf16)


def unpack_maps(parts, packing, frames, rows):
    step, lanes = parts[0].shape
    return pl.pallas_call(
        functools.partial(unpack_maps_kernel, frames),
        out_shape=jax.ShapeDtypeStruct((rows, lanes), bf16),
        in_specs=[SM] * 2 + [VM] * len(parts),
        out_specs=VM,
        scratch_shapes=[
            pltpu.VMEM((len(parts) * step + frames, lanes), f32),
            pltpu.VMEM((rows, lanes), f32),
        ],
        compiler_params=params(),
        cost_estimate=cost(0, 8 * rows * lanes),
        name="unpack_maps",
    )(*packing[:2], *parts)


def pool_rows_kernel(frames, order, offset, length, value, out, held):
    height = value.shape[0]
    held[:height] = value[...]
    held[height:] = jnp.zeros((frames, held.shape[1]), f32)
    halves = frames // 2

    def one(k, carry):
        target = pl.ds(pl.multiple_of(order[k] * halves, halves), halves)
        rows = held[pl.ds(pl.multiple_of(offset[k], 8), frames)].reshape(halves, 2, held.shape[1])
        out[target] = jnp.sum(rows, axis=1) * valid_rows(halves, held.shape[1], lax.div(length[k], 2))
        return carry

    lax.fori_loop(0, order.shape[0], one, 0)


def spread_rows_kernel(frames, order, offset, value, out, held):
    held[...] = jnp.zeros_like(held)
    halves = frames // 2

    def one(k, carry):
        rows = value[pl.ds(pl.multiple_of(order[k] * halves, halves), halves)]
        rows = jnp.broadcast_to(rows[:, None, :], (halves, 2, rows.shape[1])).reshape(frames, rows.shape[1])
        held[pl.ds(pl.multiple_of(offset[k], 8), frames)] = rows
        return carry

    lax.fori_loop(0, order.shape[0], one, 0)
    out[...] = held[: out.shape[0]]


def pool_rows(value, packing, frames, clips):
    height, lanes = value.shape
    return pl.pallas_call(
        functools.partial(pool_rows_kernel, frames),
        out_shape=jax.ShapeDtypeStruct((clips * frames // 2, lanes), f32),
        in_specs=[SM] * 3 + [VM],
        out_specs=VM,
        scratch_shapes=[pltpu.VMEM((height + frames, lanes), f32)],
        compiler_params=params(),
        cost_estimate=cost(0, 8 * height * lanes),
        name="pool_rows",
    )(*packing, value)


def spread_rows(value, packing, frames, height):
    lanes = value.shape[1]
    return pl.pallas_call(
        functools.partial(spread_rows_kernel, frames),
        out_shape=jax.ShapeDtypeStruct((height, lanes), f32),
        in_specs=[SM] * 2 + [VM],
        out_specs=VM,
        scratch_shapes=[pltpu.VMEM((height + frames, lanes), f32)],
        compiler_params=params(),
        cost_estimate=cost(0, 8 * height * lanes),
        name="spread_rows",
    )(*packing[:2], value)


under_way_xy, chunks = 3, 4


def roll_to(stacked, start, axis):
    size = stacked.shape[axis]
    doubled = jnp.concatenate([stacked, stacked], axis=axis)
    return lax.dynamic_slice_in_dim(doubled, start, size, axis=axis)


def pick(stacked, index):
    return lax.dynamic_index_in_dim(stacked, index, 0, keepdims=False)


def dot(left, right):
    return jnp.dot(left, right, preferred_element_type=f32)


def dot_transpose(left, right):
    return lax.dot_general(left, right, (((1,), (1,)), ((), ())), preferred_element_type=f32)


def both_mels(sums):
    half = sums.shape[0] // 2
    total = sums[:half] + sums[half:]
    return total, jnp.concatenate([total, total])


def norm_of(values_in, valid, pixel_count):
    _, sum_first = both_mels(jnp.sum(values_in * valid, axis=0))
    _, sum_square = both_mels(jnp.sum(values_in * values_in * valid, axis=0))
    mean_value = sum_first / pixel_count
    inv_std = lax.rsqrt(sum_square / pixel_count - mean_value * mean_value + epsilon)
    return (values_in - mean_value) * inv_std, inv_std


def make_device(dp, shard):
    depth = shard // 2
    lanes = {}

    def after(value, *earlier):
        return lax.optimization_barrier((value,) + earlier)[0]

    def queued(lane, value, send, most=2):
        sent = lanes.setdefault(lane, [])
        if len(sent) >= most:
            value = after(value, sent[-most])
        sent.append(send(value))
        return sent[-1]

    def permute(value, axis, size, move):
        return lax.ppermute(value, axis, [(i, move(i) % size) for i in range(size)])

    def from_z(value, k):
        return queued("z", value, lambda v: permute(v, "shard", shard, lambda i: i - 2 * k), under_way_z)

    def to_z(value, k):
        return queued("z", value, lambda v: permute(v, "shard", shard, lambda i: i + 2 * k), under_way_z)

    def to_z(value, k, most, *earlier):
        value = after(value, *earlier)
        return queued("z", value, lambda v: permute(v, "shard", shard, lambda i: i + 2 * k), most)

    def other_core(value):
        return permute(value, "shard", shard, lambda i: i ^ 1)

    def other_dp(value, r):
        return queued("xy", value, lambda v: permute(v, "dp", dp, lambda i: i ^ r), under_way_xy)

    def gather_dp(value):
        three = other_dp(value, 3)
        return [value, other_dp(value, 1), other_dp(value, 2), three]

    def tied(values, *earlier):
        return [after(values[0], *earlier)] + list(values[1:])

    def unswap(parts, d):
        low = [jnp.where(d % 2 == 1, parts[r ^ 1], parts[r]) for r in range(dp)]
        return [jnp.where(d // 2 == 1, low[r ^ 2], low[r]) for r in range(dp)]

    far = [k for k in range(1, depth) if 2 * k != depth] + [depth // 2]

    def core_order(mine, theirs, c):
        return [jnp.where(c == 0, mine, theirs), jnp.where(c == 0, theirs, mine)]

    def gather_small(value, d, z, c):
        near = [permute(value, "dp", dp, lambda i, r=r: i ^ r) for r in range(1, dp)]
        square = jnp.stack(unswap([value] + near, d))
        far = [permute(square, "shard", shard, lambda i, k=k: i - 2 * k) for k in range(1, depth)]
        line = roll_to(jnp.stack([square] + far), (depth - z) % depth, 0)
        return jnp.stack(core_order(line, other_core(line), c), axis=1)

    def weight_in(pieces, most):
        pieces = [pieces[0]] + [to_z(pieces[k], -k, most) for k in range(1, depth)]
        return pieces, other_core(jnp.stack([v[1] for v in pieces]))

    def send_grad(grad, done=()):
        done = dict(done)
        pieces = grad.reshape((2, depth, 9) + grad.shape[1:])
        pieces = jnp.stack([pieces[0], other_core(pieces[1])], axis=1)
        return [pieces[0]] + [to_z(pieces[k], k, 3, *done.get(k, ())) for k in range(1, depth)]

    def along(value, r, *earlier):
        return permute(after(value, *earlier), "dp", dp, lambda i: i ^ r)

    def near_start(parts):
        half = depth // 2
        low, high = jnp.stack(parts[:half]), jnp.stack(parts[half:])
        return low, high, along(low, 1), along(high, 2)

    def near_finish(start, second=(), third=()):
        low, high, low_one, high_two = start
        low_three, high_one = along(low_one, 2, high_two, *second), along(high, 1, low_one, *second)
        low_two, high_three = along(low, 2, low_three, *third), along(high_two, 1, high_one, *third)
        return [[low, low_one, low_two, low_three], [high, high_one, high_two, high_three]]

    def on_device(
        clip_maps,
        lengths,
        labels,
        conv1_weight,
        norm1_gain,
        norm1_shift,
        conv2_weight,
        norm2_gain,
        norm2_shift,
        fc1_weight,
        fc1_bias,
        fc2_weight,
        fc2_bias,
    ):
        lanes.clear()
        d, s = lax.axis_index("dp"), lax.axis_index("shard")
        z, c = s // 2, s % 2
        place = jnp.stack([d, s]).astype(jnp.int32)
        clip_count, frames, mels, chan_in = clip_maps.shape
        chan_mid = norm1_gain.shape[0]
        classes = labels.shape[1]
        clips = clip_count * dp * shard
        rows = clips * frames
        own_rows = clip_count * frames
        lane = chan_mid // (dp * shard)
        lane_in = chan_in // (dp * shard)
        wide = mels * lane
        quarter = shard * lane_in
        wide_in = mels * quarter

        position = lax.broadcasted_iota(jnp.int32, (9, shard), 1)
        tap = lax.broadcasted_iota(jnp.int32, (9, shard), 0)

        def table_of(block):
            group = tap * shard + block
            owner = group // 9
            place = (owner % 2 ^ c) * depth + (owner // 2 - z + depth) % depth
            return (place * 9 + group % 9).reshape(9 * shard).astype(jnp.int32)

        table = table_of(position)

        from_row = lax.broadcasted_iota(jnp.int32, (dp * wide, dp * wide), 0)
        to_lane = lax.broadcasted_iota(jnp.int32, (dp * wide, dp * wide), 1)
        spread = (
            (from_row // (dp * lane) == to_lane // lane % mels)
            & (from_row // lane % dp == (d ^ (to_lane // wide)))
            & (from_row % lane == to_lane % lane)
        ).astype(bf16)
        from_row = lax.broadcasted_iota(jnp.int32, (chan_in, chan_in), 0)
        to_lane = lax.broadcasted_iota(jnp.int32, (chan_in, chan_in), 1)
        sort_in = (
            (from_row // (dp * lane_in) == to_lane // lane_in % shard)
            & (from_row // lane_in % dp == (d ^ (to_lane // quarter)))
            & (from_row % lane_in == to_lane % lane_in)
        ).astype(bf16)

        pieces_one, across_one = weight_in(split_weight(conv1_weight, place, dp, shard), 3)
        own_frames = lax.broadcasted_iota(jnp.int32, (clip_count, frames), 1)
        own_valid = (own_frames < lengths[:, None])[:, :, None, None]
        clip_maps = after(clip_maps, pieces_one[0])
        masked = clip_maps * own_valid.astype(bf16)
        sorted_in = [dot(masked[:, :, m].reshape(own_rows, chan_in), sort_in).astype(bf16) for m in range(mels)]
        from_dp = []
        for r in range(dp):
            at = slice(r * quarter, (r + 1) * quarter)
            part = jnp.concatenate([v[:, at] for v in sorted_in], axis=1)
            from_dp.append(other_dp(part, r) if r else part)
        group = jnp.concatenate(unswap(from_dp, d), axis=0)
        all_maps = lax.all_gather(after(group, pieces_one[1]), "shard", tiled=True)
        wide_one = expand_weight(pieces_one, across_one, table, spread, True)
        split_two = split_weight(after(conv2_weight, from_dp[1]), place, dp, shard)

        notes = jnp.concatenate([labels, lengths[:, None]], axis=1).astype(bf16)
        notes = gather_small(jnp.pad(notes, ((0, 0), (0, -(classes + 1) % 128))), d, z, c)
        notes = notes.reshape(clips, notes.shape[-1])
        all_labels = notes[:, :classes].astype(f32)
        all_lengths = notes[:, classes].astype(jnp.int32)
        kinds = jnp.stack([all_lengths > frames // 2, (all_lengths > frames // 4) & (all_lengths <= frames // 2), all_lengths <= frames // 4])
        kinds = kinds.astype(jnp.int32)
        taken = jnp.array([frames, frames // 2, frames // 4], jnp.int32)[:, None]
        before = lax.broadcasted_iota(jnp.int32, (clips, clips), 0) < lax.broadcasted_iota(jnp.int32, (clips, clips), 1)
        among = jnp.sum(kinds[:, :, None] * before.astype(jnp.int32)[None], axis=1)
        number = jnp.sum(kinds, axis=1, keepdims=True)
        first_rank = jnp.concatenate([jnp.zeros((1, 1), jnp.int32), number[:1], number[:1] + number[1:2]])
        used = number * taken
        first_row = jnp.concatenate([jnp.zeros((1, 1), jnp.int32), used[:1], used[:1] + used[1:2]])
        rank = jnp.sum(kinds * (first_rank + among), axis=0)
        start = jnp.sum(kinds * (first_row + among * taken), axis=0)
        ranked = (rank[None, :] == lax.broadcasted_iota(jnp.int32, (clips, clips), 0)).astype(jnp.int32)
        clip_ids = lax.broadcasted_iota(jnp.int32, (clips,), 0)
        packing = [jnp.sum(ranked * v[None, :], axis=1) for v in (clip_ids, start, all_lengths)]
        pixel_count = (jnp.sum(all_lengths) * mels).astype(f32)

        def after_maps(height):
            lanes.clear()
            step, half = height // chunks, height // 2
            def scatter_dp(outs):
                total = outs[0].astype(f32)
                for r in range(1, dp):
                    total = total + other_dp(outs[r], r).astype(f32)
                return total

            maps_in, valid = pack_maps(all_maps, packing, frames, height, 2)
            pieces_two, across_two = weight_in(split_two, 3)
            parts = []
            for p in range(chunks):
                outs = convolve([maps_in[p // 2]], wide_one, [(step, wide)] * dp, chunk=p % 2, name="conv1")
                parts.append(scatter_dp(outs))
            parts = tied(parts, *pieces_two[1:])
            first_out = jnp.concatenate(parts, axis=0)

            wide_two = expand_weight(pieces_two, across_two, table, spread, False)

            own_start = (s * dp + d) * lane

            def own_channels(vector):
                own = lax.dynamic_slice_in_dim(vector, own_start, lane)
                return jnp.concatenate([own] * mels)

            gain_one, shift_one = own_channels(norm1_gain), own_channels(norm1_shift)
            gain_two, shift_two = own_channels(norm2_gain), own_channels(norm2_shift)

            normed_one, inv_one = norm_of(first_out, valid, pixel_count)
            pre_one = normed_one * gain_one + shift_one
            act_one = (jax.nn.silu(pre_one) * valid).astype(bf16)
            acts = [
                lax.all_gather(act_one[:half], "shard"),
                lax.all_gather(after(act_one[half:], wide_two), "shard"),
            ]
            fc_rows = fc1_weight.shape[0]
            own_fc1 = lax.dynamic_slice_in_dim(fc1_weight, d * lane, lane, axis=0)
            some_fc1 = lax.all_gather(after(own_fc1, wide_two), "shard", tiled=True)
            own_fc2 = jnp.pad(fc2_weight, ((0, 0), (0, -classes % 128)))
            own_fc2 = after(lax.dynamic_slice_in_dim(own_fc2, d * lane, lane, axis=0), act_one)
            line = [own_fc2] + [permute(own_fc2, "shard", shard, lambda i, k=k: i - 2 * k) for k in range(1, depth)]
            line = roll_to(jnp.stack(line), (depth - z) % depth, 0)
            parts, outs = [], []
            for p in range(chunks):
                value = after(acts[p // 2], *outs[:1])
                if p >= 2:
                    value = after(value, parts[p - 2])
                outs = convolve([value], wide_two, [(step, wide)] * dp, chunk=p % 2, name="conv2")
                parts.append(scatter_dp(outs))
                if p == 1:
                    line = after(line, outs[0])
                    near = [permute(line, "dp", dp, lambda i, r=r: i ^ r) for r in range(1, dp)]
                    square = jnp.stack(unswap([line] + near, d), axis=1)
                    full_fc2 = jnp.stack(core_order(square, other_core(square), c), axis=1)
                    full_fc2 = full_fc2.reshape(chan_mid, own_fc2.shape[1])[:, :classes]
            parts = tied(parts, full_fc2)
            second_out = jnp.concatenate(parts, axis=0)
            normed_two, inv_two = norm_of(second_out, valid, pixel_count)
            pre_two = normed_two * gain_two + shift_two
            sigma_two = jax.nn.sigmoid(pre_two)
            act_two = pre_two * sigma_two * valid
            slope_two = (sigma_two + act_two * (1.0 - sigma_two)) * valid

            halves = frames // 2
            pooled = pool_rows(act_two, packing, frames, clips).reshape(clips, halves, wide)
            pooled = (pooled[:, :, :lane] + pooled[:, :, lane:]) / (2.0 * mels)
            half_len = all_lengths // 2
            half_ids = lax.broadcasted_iota(jnp.int32, (clips, halves), 1)
            pooled_valid = (half_ids < half_len[:, None]).astype(f32)[:, :, None]
            half_float = half_len.astype(f32)[:, None]
            largest = jnp.max(jnp.where(pooled_valid > 0, pooled, -1e30), axis=1, keepdims=True)
            exp_terms = jnp.exp(pooled - largest) * pooled_valid
            exp_sum = jnp.sum(exp_terms, axis=1)
            log_sum = largest[:, 0, :] + jnp.log(exp_sum)
            mean_time = jnp.sum(pooled * pooled_valid, axis=1) / half_float
            own_embedding = (log_sum + mean_time).astype(bf16)
            own_embedding = own_embedding.T
            line = [own_embedding] + [permute(own_embedding, "shard", shard, lambda i, k=k: i - 2 * k) for k in range(1, depth)]
            line = roll_to(jnp.stack(line), (depth - z) % depth, 0)
            line = jnp.stack(core_order(line, other_core(line), c), axis=1).reshape(shard * lane, clips)
            part = lax.dynamic_slice_in_dim(line, c * (clips // 2), clips // 2, axis=1)
            part = transpose_dot(part, some_fc1).astype(bf16)
            near = [permute(part, "dp", dp, lambda i, r=r: i ^ r) for r in range(1, dp)]
            part = sum(v.astype(f32) for v in unswap([part] + near, d))
            hidden = jnp.concatenate(core_order(part, other_core(part), c), axis=0) + fc1_bias
            near = [permute(after(own_embedding, part), "dp", dp, lambda i, r=r: i ^ r) for r in range(1, dp)]
            own_columns = jnp.concatenate(unswap([own_embedding] + near, d), axis=0)
            sigma = jax.nn.sigmoid(hidden)
            gated = (hidden * sigma).astype(bf16)
            logits = dot(gated, full_fc2) + fc2_bias
            d_logits = (jax.nn.sigmoid(logits) - all_labels).astype(bf16)
            d_gated = dot_transpose(d_logits, full_fc2)
            d_hidden = (d_gated * (sigma + hidden * sigma * (1.0 - sigma))).astype(bf16)
            d_embed = dot_transpose(d_hidden, own_fc1)
            soft = exp_terms / exp_sum[:, None, :]
            d_pooled = d_embed[:, None, :] * (soft + pooled_valid / half_float[:, :, None])

            fc1_grad = dot(own_columns, d_hidden)
            own_gated = lax.dynamic_slice_in_dim(gated, s * fc_rows, fc_rows, axis=1)
            fc2_grad = dot(own_gated.T, d_logits)
            fc1_bias_grad = jnp.sum(d_hidden.astype(f32), axis=0)
            fc2_bias_grad = jnp.sum(d_logits.astype(f32), axis=0)
            own_clips = (s * dp + d) * clip_count
            own_logits = lax.dynamic_slice_in_dim(logits, own_clips, clip_count, axis=0)

            d_frames = jnp.concatenate([d_pooled, d_pooled], axis=2) / (2.0 * mels)
            dz_two = spread_rows(d_frames.reshape(clips * halves, wide), packing, frames, height) * slope_two
            shift_two_grad, shift_two_lanes = both_mels(jnp.sum(dz_two, axis=0))
            gain_two_grad, gain_two_lanes = both_mels(jnp.sum(dz_two * normed_two, axis=0))
            d_second = (
                gain_two
                * inv_two
                * (dz_two - (shift_two_lanes + normed_two * gain_two_lanes) / pixel_count)
                * valid
            ).astype(bf16)

            grads_two = [gather_dp(v) for v in d_second.reshape(2, half, wide)]
            parts, outs = [], []
            for p in range(2):
                ready = tied(grads_two[p], *outs[-1:], *((own_columns,) if p else ()))
                outs += convolve(ready, wide_two, [(shard, half, wide)], back=True, name="back2")
                parts.append(lax.psum_scatter(outs[p], "shard", scatter_dimension=0))

            grad_two = None
            count = shard // 4
            act_chunks = [(v, 0) for v in acts]
            for first in range(0, shard, count):
                ready = [tied(grads_two[0], outs[-1])] + grads_two[1:]
                grad_two = weight_grad(
                    act_chunks, ready, table, spread, lane, False, shard, first, count, grad_two, name="grad2",
                )
            parts = tied(parts, grad_two)

            d_act_one = jnp.concatenate(parts, axis=0).astype(f32)
            sigma_one = jax.nn.sigmoid(pre_one)
            dz_one = d_act_one * valid * (sigma_one + pre_one * sigma_one * (1.0 - sigma_one))
            shift_one_grad, shift_one_lanes = both_mels(jnp.sum(dz_one, axis=0))
            gain_one_grad, gain_one_lanes = both_mels(jnp.sum(dz_one * normed_one, axis=0))
            d_first = (
                gain_one
                * inv_one
                * (dz_one - (shift_one_lanes + normed_one * gain_one_lanes) / pixel_count)
                * valid
            ).astype(bf16)
            norm_grads = jnp.stack([gain_one_grad, shift_one_grad, gain_two_grad, shift_two_grad])
            grads_one = [gather_dp(v) for v in d_first.reshape(2, half, wide)]
            sent_two = send_grad(grad_two, {2: grads_one[0][1:3], 3: grads_one[1][1:3]})
            outs = []
            for p in range(2):
                ready = tied(grads_one[p], *outs[-1:])
                outs += convolve(ready, wide_one, [(half, wide_in)], back=True, name="back1")
            near = [permute(norm_grads, "dp", dp, lambda i, r=r: i ^ r) for r in range(1, dp)]
            norm_grads = jnp.stack(unswap([norm_grads] + near, d))
            start_two = near_start([after(v, outs[-1], norm_grads) for v in sent_two])

            grad_one, d_in = None, None
            count = shard // 2
            for first in range(0, shard, count):
                ready = [tied(grads_one[0], outs[-1], *start_two[:2])] + grads_one[1:]
                grad_one = weight_grad(
                    [(v, 0) for v in maps_in], ready, table, spread, lane_in, True, shard, first, count, grad_one, name="grad1",
                )
            d_in = unpack_maps(tied(outs, grad_one), packing, frames, rows)
            d_in = d_in.reshape(shard, rows // shard, wide_in)
            sent_one = send_grad(grad_one)
            near_two = near_finish(start_two, sent_one[:1], sent_one[1:])
            total = lax.psum_scatter(after(d_in, near_two[0][3], near_two[1][1], *sent_one[1:]), "shard", scatter_dimension=0)
            conv2_grad = join_grad([h for pair in zip(*near_two) for h in pair], place, dp, shard)
            total = total.reshape(dp, own_rows, wide_in)
            from_dp = [other_dp(pick(total, d ^ r), r) if r else pick(total, d) for r in range(dp)]
            near_one = near_finish(near_start([after(v, near_two[0][2], near_two[1][3]) for v in sent_one]), (), from_dp[1:])
            conv1_grad = join_grad([h for pair in zip(*near_one) for h in pair], place, dp, shard)

            norm_grads = after(norm_grads, total)
            line = [norm_grads] + [permute(norm_grads, "shard", shard, lambda i, k=k: i - 2 * k) for k in range(1, depth)]
            line = roll_to(jnp.stack(line), (depth - z) % depth, 0)
            norm_grads = jnp.stack(core_order(line, other_core(line), c), axis=1)
            norm_grads = norm_grads.reshape(dp * shard, 4, lane)
            norm_grads = jnp.moveaxis(norm_grads, 0, 1).reshape(4, chan_mid)

            input_grad = []
            for m in range(mels):
                at = slice(m * quarter, (m + 1) * quarter)
                mixed = jnp.concatenate([v[:, at] for v in from_dp], axis=1)
                input_grad.append(dot_transpose(mixed, sort_in).reshape(clip_count, frames, chan_in))
            input_grad = jnp.stack(input_grad, axis=2) * own_valid.astype(f32)

            return (
                own_logits,
                input_grad,
                conv1_grad,
                norm_grads[0],
                norm_grads[1],
                conv2_grad,
                norm_grads[2],
                norm_grads[3],
                fc1_grad,
                fc1_bias_grad,
                fc2_grad,
                fc2_bias_grad,
            )

        def rest(height):
            def run():
                return after_maps(height)

            return run

        few = rows * 21 // 32
        assert few % (32 * chunks) == 0
        return lax.cond(jnp.sum(used) <= few, rest(few), rest(rows))

    return on_device


def patch_rows(grid_in):
    clip_count, frame_count, mel_count, chan_count = grid_in.shape
    padded = jnp.pad(grid_in, ((0, 0), (1, 1), (1, 1), (0, 0)))
    tap_list = [
        padded[:, shift_t : shift_t + frame_count, shift_m : shift_m + mel_count, :]
        for shift_t in range(3)
        for shift_m in range(3)
    ]
    stacked = jnp.stack(tap_list, axis=3)
    return stacked.reshape(clip_count * frame_count * mel_count, 9 * chan_count)


def fold_rows(grad_rows, clip_count, frame_count, mel_count):
    chan_count = grad_rows.shape[1] // 9
    tap_terms = grad_rows.reshape(clip_count, frame_count, mel_count, 9, chan_count)
    summed = jnp.zeros((clip_count, frame_count + 2, mel_count + 2, chan_count), jnp.float32)
    for tap_index in range(9):
        shift_t = tap_index // 3
        shift_m = tap_index % 3
        summed = summed + jnp.pad(
            tap_terms[:, :, :, tap_index, :],
            ((0, 0), (shift_t, 2 - shift_t), (shift_m, 2 - shift_m), (0, 0)),
        )
    return summed[:, 1 : frame_count + 1, 1 : mel_count + 1, :]


def normalize(values_in, sum_first, sum_square, pixel_count, gain, shift):
    mean_value = sum_first / pixel_count
    inv_std = lax.rsqrt(sum_square / pixel_count - mean_value * mean_value + epsilon)
    normed = (values_in - mean_value) * inv_std
    return (normed, inv_std, normed * gain + shift)


def silu_slope(values_in):
    sigma = jax.nn.sigmoid(values_in)
    return sigma + values_in * sigma * (1.0 - sigma)


def transpose_dot(left, right):
    return lax.dot_general(
        left, right, (((0,), (0,)), ((), ())), preferred_element_type=jnp.float32
    )


def make_valid(clip_lengths, frame_count, mel_count):
    clip_count = clip_lengths.shape[0]
    frame_ids = lax.broadcasted_iota(jnp.int32, (clip_count, frame_count), 1)
    valid_two = (frame_ids < clip_lengths[:, None]).astype(jnp.float32)
    pixel_valid = jnp.broadcast_to(
        valid_two[:, :, None], (clip_count, frame_count, mel_count)
    ).reshape(-1, 1)
    return (valid_two[:, :, None, None], pixel_valid)


def pool_map(act_grid):
    clip_count, frame_count, mel_count, chans = act_grid.shape
    pooled = jnp.mean(
        act_grid.reshape(clip_count, frame_count // 2, 2, mel_count // 2, 2, chans), axis=(2, 4)
    )
    return jnp.mean(pooled, axis=2)


def pooled_slope(d_pooled, pre_two, pixel_valid, mel_count):
    clip_count, half_frames, chans = d_pooled.shape
    d_frames = jnp.repeat(d_pooled, 2, axis=1)[:, :, None, :] / (2.0 * mel_count)
    d_act_two = jnp.broadcast_to(d_frames, (clip_count, 2 * half_frames, mel_count, chans)).reshape(
        -1, chans
    )
    return d_act_two * pixel_valid * silu_slope(pre_two)


def tag_head(
    pooled, clip_lengths, labels, full_fc1, full_fc2, back_fc1, back_fc2, fc1_bias, fc2_bias
):
    clip_count, half_frames, chans = pooled.shape
    half_ids = lax.broadcasted_iota(jnp.int32, (clip_count, half_frames), 1)
    half_len = clip_lengths // 2
    pooled_valid = (half_ids < half_len[:, None]).astype(jnp.float32)[:, :, None]
    half_float = half_len.astype(jnp.float32)[:, None]
    largest = jnp.max(jnp.where(pooled_valid > 0, pooled, -1e30), axis=1, keepdims=True)
    exp_terms = jnp.exp(pooled - largest) * pooled_valid
    exp_sum = jnp.sum(exp_terms, axis=1)
    log_sum = largest[:, 0, :] + jnp.log(exp_sum)
    mean_time = jnp.sum(pooled * pooled_valid, axis=1) / half_float
    embedding = (log_sum + mean_time).astype(jnp.bfloat16)
    hidden = jnp.dot(embedding, full_fc1, preferred_element_type=jnp.float32) + fc1_bias
    gated_low = jax.nn.silu(hidden).astype(jnp.bfloat16)
    class_logits = jnp.dot(gated_low, full_fc2, preferred_element_type=jnp.float32) + fc2_bias
    d_logits = (jax.nn.sigmoid(class_logits) - labels.astype(jnp.float32)).astype(jnp.bfloat16)
    fc2_term = transpose_dot(gated_low, d_logits)
    fc2_bias_term = jnp.sum(d_logits.astype(jnp.float32), axis=0)
    d_gated = jnp.dot(d_logits, back_fc2.T, preferred_element_type=jnp.float32)
    d_hidden = (d_gated * silu_slope(hidden)).astype(jnp.bfloat16)
    fc1_term = transpose_dot(embedding, d_hidden)
    fc1_bias_term = jnp.sum(d_hidden.astype(jnp.float32), axis=0)
    d_embed = jnp.dot(d_hidden, back_fc1.T, preferred_element_type=jnp.float32)
    soft_weights = exp_terms / exp_sum[:, None, :]
    d_pooled = d_embed[:, None, :] * (soft_weights + pooled_valid / half_float[:, :, None])
    return (class_logits, d_pooled, fc1_term, fc2_term, fc1_bias_term, fc2_bias_term)


def on_device(
    clip_maps,
    lengths,
    labels,
    conv1_weight,
    norm1_gain,
    norm1_shift,
    conv2_weight,
    norm2_gain,
    norm2_shift,
    fc1_weight,
    fc1_bias,
    fc2_weight,
    fc2_bias,
):
    clip_count, frame_count, mel_count, chan_in = clip_maps.shape
    chan_mid = norm1_gain.shape[0]
    valid_four, pixel_valid = make_valid(lengths, frame_count, mel_count)
    masked = clip_maps * valid_four.astype(jnp.bfloat16)
    sent = (conv1_weight, conv2_weight, fc1_weight, fc2_weight)
    gathered = (
        lax.all_gather(sent[0], "shard", axis=0, tiled=True),
        lax.all_gather(sent[1], "shard", axis=0, tiled=True),
        lax.all_gather(sent[2], "shard", axis=0, tiled=True),
        lax.all_gather(sent[3], "shard", axis=0, tiled=True),
    )
    full_one, full_two, full_fc1, full_fc2 = gathered
    patch_one = patch_rows(masked)
    first_out = jnp.dot(patch_one, full_one, preferred_element_type=jnp.float32)
    sum_one, square_one, pixel_count = lax.psum(
        (
            jnp.sum(first_out * pixel_valid, axis=0),
            jnp.sum(first_out * first_out * pixel_valid, axis=0),
            jnp.sum(pixel_valid),
        ),
        ("dp", "shard"),
    )
    normed_one, inv_one, pre_one = normalize(
        first_out, sum_one, square_one, pixel_count, norm1_gain, norm1_shift
    )
    act_one = (jax.nn.silu(pre_one) * pixel_valid).astype(jnp.bfloat16)
    patch_two = patch_rows(act_one.reshape(clip_count, frame_count, mel_count, chan_mid))
    second_out = jnp.dot(patch_two, full_two, preferred_element_type=jnp.float32)
    sum_two, square_two = lax.psum(
        (
            jnp.sum(second_out * pixel_valid, axis=0),
            jnp.sum(second_out * second_out * pixel_valid, axis=0),
        ),
        ("dp", "shard"),
    )
    normed_two, inv_two, pre_two = normalize(
        second_out, sum_two, square_two, pixel_count, norm2_gain, norm2_shift
    )
    act_two = (jax.nn.silu(pre_two) * pixel_valid).reshape(
        clip_count, frame_count, mel_count, chan_mid
    )
    pooled_own = pool_map(act_two)
    back_weights = (
        lax.all_gather(sent[0], "shard", axis=0, tiled=True),
        lax.all_gather(sent[1], "shard", axis=0, tiled=True),
        lax.all_gather(sent[2], "shard", axis=0, tiled=True),
        lax.all_gather(sent[3], "shard", axis=0, tiled=True),
    )
    back_one, back_two, back_fc1, back_fc2 = back_weights
    class_logits, d_pooled, fc1_term, fc2_term, fc1_bias_term, fc2_bias_term = tag_head(
        pooled_own, lengths, labels, full_fc1, full_fc2, back_fc1, back_fc2, fc1_bias, fc2_bias
    )
    dz_two = pooled_slope(d_pooled, pre_two, pixel_valid, mel_count)
    shift_two_grad, gain_two_grad, fc1_bias_grad, fc2_bias_grad = lax.psum(
        (
            jnp.sum(dz_two, axis=0),
            jnp.sum(dz_two * normed_two, axis=0),
            fc1_bias_term,
            fc2_bias_term,
        ),
        ("dp", "shard"),
    )
    d_second = (
        norm2_gain
        * inv_two
        * (dz_two - (shift_two_grad + normed_two * gain_two_grad) / pixel_count)
        * pixel_valid
    ).astype(jnp.bfloat16)
    conv2_part = lax.psum_scatter(
        transpose_dot(patch_two, d_second), "shard", scatter_dimension=0, tiled=True
    )
    d_patch_two = jnp.dot(d_second, back_two.T, preferred_element_type=jnp.float32)
    d_act_one = fold_rows(d_patch_two, clip_count, frame_count, mel_count).reshape(-1, chan_mid)
    dz_one = d_act_one * pixel_valid * silu_slope(pre_one)
    shift_one_grad, gain_one_grad = lax.psum(
        (jnp.sum(dz_one, axis=0), jnp.sum(dz_one * normed_one, axis=0)), ("dp", "shard")
    )
    d_first = (
        norm1_gain
        * inv_one
        * (dz_one - (shift_one_grad + normed_one * gain_one_grad) / pixel_count)
        * pixel_valid
    ).astype(jnp.bfloat16)
    conv1_term = transpose_dot(patch_one, d_first)
    d_patch_one = jnp.dot(d_first, back_one.T, preferred_element_type=jnp.float32)
    input_grad = fold_rows(d_patch_one, clip_count, frame_count, mel_count) * valid_four
    conv1_part, fc1_part, fc2_part = (
        lax.psum_scatter(conv1_term, "shard", scatter_dimension=0, tiled=True),
        lax.psum_scatter(fc1_term, "shard", scatter_dimension=0, tiled=True),
        lax.psum_scatter(fc2_term, "shard", scatter_dimension=0, tiled=True),
    )
    conv1_grad, conv2_grad, fc1_grad, fc2_grad = (
        lax.psum(conv1_part.astype(jnp.bfloat16), "dp").astype(jnp.float32),
        lax.psum(conv2_part.astype(jnp.bfloat16), "dp").astype(jnp.float32),
        lax.psum(fc1_part.astype(jnp.bfloat16), "dp").astype(jnp.float32),
        lax.psum(fc2_part.astype(jnp.bfloat16), "dp").astype(jnp.float32),
    )
    return (
        class_logits,
        input_grad,
        conv1_grad,
        gain_one_grad,
        shift_one_grad,
        conv2_grad,
        gain_two_grad,
        shift_two_grad,
        fc1_grad,
        fc1_bias_grad,
        fc2_grad,
        fc2_bias_grad,
    )


def solution(mesh):
    in_specs = (
        P(("dp", "shard"), None, None, None),
        P(("dp", "shard")),
        P(("dp", "shard"), None),
        P("shard", None),
        P(),
        P(),
        P("shard", None),
        P(),
        P(),
        P("shard", None),
        P(),
        P("shard", None),
        P(),
    )
    out_specs = (
        P(("dp", "shard"), None),
        P(("dp", "shard"), None, None, None),
        P("shard", None),
        P(),
        P(),
        P("shard", None),
        P(),
        P(),
        P("shard", None),
        P(),
        P("shard", None),
        P(),
    )
    dp, shard = mesh.shape["dp"], mesh.shape["shard"]
    step = make_device(dp, shard) if (dp, shard) == (4, 8) else on_device
    return jax.shard_map(
        step, mesh=mesh, in_specs=in_specs, out_specs=out_specs, check_vma=False
    )
```
